32 devices in a mesh: section: 2 (over y), dp: 16 (over z, x, core).
Axes of the slice: x: 2, y: 2, z: 4, core: 2. Of those that a mesh axis runs over, the one named last changes fastest.
Arguments:
- features: bfloat16 [2, 16, 512, 1024], P(None, 'dp'), may hold values from -18 to 18
- cotangent: bfloat16 [2, 16, 512, 1024], P(None, 'dp'), may hold values from -6 to 6
- lengths: int32 [2, 16], P(None, 'dp'), may hold values from 32 to 512, as said below
- codebook_index: int32 [2, 16], P(None, 'dp'), may hold values from 0 to 6
- attention_in: bfloat16 [2, 1024, 3072], P('section'), may hold values from -0.1875 to 0.1875
- attention_out: bfloat16 [2, 1024, 1024], P('section'), may hold values from -0.75 to 0.75
- feed_up: bfloat16 [2, 1024, 4096], P('section'), may hold values from -1 to 1
- feed_down: bfloat16 [2, 4096, 1024], P('section'), may hold values from -0.09375 to 0.09375
- vectors: float32 [2, 12288], P('section'), may hold values from -1.5 to 1.5
- adaptive_weight: bfloat16 [1024, 4096], replicated, may hold values from -0.046875 to 0.046875
- codebook_table: bfloat16 [7, 1024], replicated, may hold values from -6 to 6
Outputs:
- layer_outputs: bfloat16 [2, 2, 16, 512, 1024], P('section', None, 'dp')
- input_grads: bfloat16 [2, 2, 16, 512, 1024], P('section', None, 'dp')
- grad_attention_in: float32 [2, 1024, 3072], P('section', 'dp')
- grad_attention_out: float32 [2, 1024, 1024], P('section', 'dp')
- grad_feed_up: float32 [2, 1024, 4096], P('section', 'dp')
- grad_feed_down: float32 [2, 4096, 1024], P('section', 'dp')
- grad_vectors: float32 [2, 12288], P('section', 'dp')
- grad_adaptive: float32 [1024, 4096], P(None, ('section', 'dp'))
- residual_rms: float32 [2, 4], P('section')
The draws below stay inside these ranges and needn't reach their ends.
Inputs may be any that keep to these rules, and one draw needn't show every extreme that they name: `lengths`: in every draw some utterance has all 512 frames valid.
All inputs are finite; a program needn't handle non-finite values.
Results may differ from the reference program's by a relative error of at most 0.017.
Values may be sent and summed in bfloat16 or wider, within the bound.
No kernel may reach another device: no remote copies, remote signals or barrier semaphores. Data moves between devices by JAX's collectives and lax.ppermute only.
A program may use at most 384 MiB of HBM per device.

```python
import math
import jax
import jax.numpy as jnp
from jax import lax

D = 1024
HEAD = 64
FF = 4096
NCB = 7
SEQ = 512
MB = 2
UTTS = 16


def draw_features(key, part):
    key = jax.random.fold_in(key, 3)
    rising = 1.0 + 2.0 * jnp.arange(UTTS, dtype=jnp.float32) / max(UTTS - 1, 1)
    sample = jnp.clip(jax.random.normal(key, (MB, UTTS, SEQ, D), jnp.float32), -6.0, 6.0)
    return (sample * rising[None, :, None, None]).astype(jnp.bfloat16)


def draw_lengths(key, part):
    key = jax.random.fold_in(key, 5)
    first_key, second_key = jax.random.split(key)
    shortest = max(1, SEQ // 16)
    drawn = jax.random.randint(first_key, (MB * UTTS,), shortest, SEQ + 1, dtype=jnp.int32)
    chosen = jax.random.randint(second_key, (), 0, MB * UTTS, dtype=jnp.int32)
    drawn = jnp.where(jnp.arange(MB * UTTS, dtype=jnp.int32) == chosen, SEQ, drawn)
    return drawn.reshape(MB, UTTS)


def draw_vectors(key, part):
    key = jax.random.fold_in(key, 7)
    gain_key, shift_key, bias_key = jax.random.split(key, 3)
    gain_rows = jax.random.uniform(gain_key, (2, 2, 1, D), jnp.float32, 0.5, 1.5)
    shifts = jnp.clip(jax.random.normal(shift_key, (2, 2, 1, D), jnp.float32) * 0.3, -1.5, 1.5)
    norm_part = jnp.concatenate([gain_rows, shifts], axis=2).reshape(2, 4 * D)
    biases = jnp.clip(jax.random.normal(bias_key, (2, 4 * D + FF), jnp.float32) * 0.3, -1.5, 1.5)
    return jnp.concatenate([norm_part, biases], axis=1)


def draw_feed_up(key, part):
    key = jax.random.fold_in(key, 11)
    entry_key = jax.random.fold_in(key, 0)
    spread = 1.0 / math.sqrt(D)
    sample = jnp.clip(jax.random.normal(entry_key, (2, D, FF), jnp.float32), -6.0, 6.0) * spread
    return sample.astype(jnp.bfloat16)


def set_ends(array, stream_key, least, top_value):
    dims = array.shape
    place = [jax.random.randint(jax.random.fold_in(stream_key, axis), (), 0, dims[axis]) for axis in range(len(dims))]
    array = array.at[tuple(place)].set(least)
    longest = dims.index(max(dims))
    place[longest] = (place[longest] + 1) % dims[longest]
    return array.at[tuple(place)].set(top_value)


def steps_of(rng, dims, shards, least, high):
    def one(axis_at, blocks):
        heights = jax.random.uniform(jax.random.fold_in(jax.random.fold_in(rng, 6), axis_at), (blocks,), jnp.float32, least / len(shards), high / len(shards))
        return jnp.repeat(jnp.exp(heights), dims[axis_at] // blocks).reshape((-1,) + (1,) * (len(dims) - axis_at - 1))

    factor_of = one(*shards[0])
    for cut in shards[1:]:
        factor_of = factor_of * one(*cut)
    return factor_of


def bell_draw(own_key, dims, scale, most, shards=(), kind=jnp.bfloat16):
    loudness = steps_of(own_key, dims, shards, -0.22, 0.18) if shards else 1.0
    values = jax.random.normal(own_key, dims, jnp.float32) * scale * loudness
    return jnp.minimum(jnp.maximum(values, -most), most).astype(kind)


def setup_inputs(seed: int = 0) -> dict:
    arg_keys = jax.random.split(jax.random.key(seed), 12)
    features = draw_features(jax.random.fold_in(arg_keys[11], 71), 0)
    cotangent = bell_draw(arg_keys[1], (MB, UTTS, SEQ, D), 1.0, 6.0, ((1, 16),))
    lengths = draw_lengths(jax.random.fold_in(arg_keys[11], 71), 0)
    codebook_index = set_ends(jax.random.randint(arg_keys[3], (MB, UTTS), 0, NCB), jax.random.fold_in(arg_keys[3], 1), 0, NCB - 1).astype(jnp.int32)
    attention_in = bell_draw(arg_keys[4], (2, D, 3 * D), D ** -0.5, 0.1875, ((0, 2),))
    attention_out = bell_draw(arg_keys[5], (2, D, D), (D // 16) ** -0.5, 0.75, ((0, 2),))
    feed_up = draw_feed_up(jax.random.fold_in(arg_keys[11], 71), 0)
    feed_down = bell_draw(arg_keys[7], (2, FF, D), FF ** -0.5, 0.09375, ((0, 2),))
    vectors = draw_vectors(jax.random.fold_in(arg_keys[11], 71), 0)
    adaptive_weight = bell_draw(arg_keys[9], (D, 4 * D), (16 * D) ** -0.5, 0.046875)
    codebook_table = bell_draw(arg_keys[10], (NCB, D), 1.0, 6.0)
    return {"features": features, "cotangent": cotangent, "lengths": lengths, "codebook_index": codebook_index, "attention_in": attention_in, "attention_out": attention_out, "feed_up": feed_up, "feed_down": feed_down, "vectors": vectors, "adaptive_weight": adaptive_weight, "codebook_table": codebook_table}


@jax.custom_vjp
def low(v):
    return lax.optimization_barrier(v.astype(jnp.bfloat16)).astype(jnp.float32)

@jax.custom_vjp
def low_back(v):
    return v

def low_keep(v):
    return (low(v), None)

def low_pass(kept, grad):
    return (grad,)

def back_keep(v):
    return (v, None)

def back_low(kept, grad):
    return (low(grad),)
low.defvjp(low_keep, low_pass)
low_back.defvjp(back_keep, back_low)
norm_eps = 1e-05
root_half = 0.7071067811865476
score_scale = 0.125
big_negative = -1e+30
highest = lax.Precision.HIGHEST

def product(former, latter):
    return jnp.dot(former, latter, precision=highest, preferred_element_type=jnp.float32)

def normalize(residual, scaling, offset):
    average = lax.optimization_barrier(jnp.mean(residual, axis=-1, keepdims=True))
    centered = residual - average
    spread = lax.optimization_barrier(jnp.mean(centered * centered, axis=-1, keepdims=True))
    return centered * lax.rsqrt(spread + norm_eps) * scaling + offset

def smooth_gate(values):
    return 0.5 * values * (1.0 + lax.erf(values * root_half))

def decoder_layer(residual, length, causal, vector, condition, attention_in, attention_out, feed_up, feed_down):
    frames, model_width = residual.shape
    head_count = model_width // HEAD
    gain_rows = vector[:4 * model_width] + condition
    gain_one = gain_rows[:model_width]
    bias_one = gain_rows[model_width:2 * model_width]
    gain_two = gain_rows[2 * model_width:3 * model_width]
    bias_two = gain_rows[3 * model_width:]
    query_bias = vector[4 * model_width:5 * model_width]
    value_bias = vector[5 * model_width:6 * model_width]
    mixer_bias = vector[6 * model_width:7 * model_width]
    down_bias = vector[7 * model_width:8 * model_width]
    up_bias = vector[8 * model_width:]
    mixer_input = low(normalize(residual, gain_one, bias_one))
    projected = product(mixer_input, attention_in) + jnp.concatenate([query_bias, jnp.zeros_like(query_bias), value_bias])
    projected = low(low_back(projected))
    queries = projected[:, :model_width].reshape(frames, head_count, HEAD)
    key_rows = projected[:, model_width:2 * model_width].reshape(frames, head_count, HEAD)
    value_rows = projected[:, 2 * model_width:].reshape(frames, head_count, HEAD)
    scores = jnp.einsum('qhd,khd->hqk', queries, key_rows, precision=highest) * score_scale
    scores = low_back(scores)
    places = jnp.arange(frames, dtype=jnp.int32)
    allowed = places[None, :] < length
    if causal:
        allowed = allowed & (places[None, :] <= places[:, None])
    scores = jnp.where(allowed[None], scores, big_negative)
    row_max = lax.optimization_barrier(jnp.max(scores, axis=-1, keepdims=True))
    exponent = jnp.exp(scores - row_max)
    attn_weights = low(exponent / lax.optimization_barrier(jnp.sum(exponent, axis=-1, keepdims=True)))
    context = jnp.einsum('hqk,khd->qhd', attn_weights, value_rows, precision=highest).reshape(frames, model_width)
    context = low(low_back(context))
    attn_branch = low_back(product(context, attention_out) + mixer_bias)
    middle = residual + attn_branch
    feed_input = low(normalize(middle, gain_two, bias_two))
    hidden_pre = low_back(product(feed_input, feed_up) + up_bias)
    hidden_act = low(smooth_gate(hidden_pre))
    feed_branch = low_back(product(hidden_act, feed_down) + down_bias)
    output = middle + feed_branch
    valid_rows = (places < length).astype(jnp.float32)[:, None]
    squares = jnp.stack([jnp.sum(valid_rows * middle * middle), jnp.sum(valid_rows * output * output), jnp.sum(valid_rows * attn_branch * attn_branch), jnp.sum(valid_rows * feed_branch * feed_branch)])
    return (output, squares)

def reference(features, cotangent, lengths, codebook_index, attention_in, attention_out, feed_up, feed_down, vectors, adaptive_weight, codebook_table):
    micro_count, utterances, frames, model_width = features.shape
    total_rows = micro_count * utterances
    residual = features.reshape(total_rows, frames, model_width).astype(jnp.float32)
    valid_lengths = lengths.reshape(total_rows)
    one_hot = (codebook_index.reshape(total_rows)[:, None] == jnp.arange(NCB, dtype=jnp.int32)[None, :]).astype(jnp.float32)
    places = jnp.arange(frames, dtype=jnp.int32)
    row_mask = (places[None, :] < valid_lengths[:, None]).astype(jnp.float32)
    upstream = cotangent.reshape(total_rows, frames, model_width).astype(jnp.float32) * row_mask[:, :, None]
    table = codebook_table.astype(jnp.float32)
    params = (attention_in.astype(jnp.float32), attention_out.astype(jnp.float32), feed_up.astype(jnp.float32), feed_down.astype(jnp.float32), vectors, adaptive_weight.astype(jnp.float32))
    boundary_shift = jnp.zeros_like(residual)

    def forward(params, residual, boundary_shift):
        mats_in, mats_out, mats_up, mats_down, vector_pair, adaptive = params
        condition_table = product(table, adaptive)

        def utterance(operands):
            rows_in, length, selector, shift_rows = operands
            condition = product(selector[None, :], condition_table)[0]
            causal_out, causal_squares = decoder_layer(rows_in, length, True, vector_pair[0], jnp.zeros_like(condition), mats_in[0], mats_out[0], mats_up[0], mats_down[0])
            boundary = low(low_back(causal_out)) + shift_rows
            adaptive_out, adaptive_squares = decoder_layer(boundary, length, False, vector_pair[1], condition, mats_in[1], mats_out[1], mats_up[1], mats_down[1])
            return (adaptive_out, (causal_out, jnp.stack([causal_squares, adaptive_squares])))
        adaptive_out, (causal_out, squares) = lax.map(jax.checkpoint(utterance), (residual, valid_lengths, one_hot, boundary_shift))
        return (adaptive_out, (causal_out, squares))
    adaptive_out, pullback, (causal_out, squares) = jax.vjp(forward, params, residual, boundary_shift, has_aux=True)
    param_grads, residual_grad, boundary_grad = pullback(upstream)
    full_shape = (micro_count, utterances, frames, model_width)
    layer_outputs = jnp.stack([causal_out.reshape(full_shape), adaptive_out.reshape(full_shape)]).astype(jnp.bfloat16)
    input_grads = jnp.stack([residual_grad.reshape(full_shape), boundary_grad.reshape(full_shape)]).astype(jnp.bfloat16)
    token_count = jnp.sum(valid_lengths).astype(jnp.float32)
    residual_rms = jnp.sqrt(lax.optimization_barrier(jnp.sum(squares, axis=0)) / (token_count * model_width))
    return (layer_outputs, input_grads, param_grads[0], param_grads[1], param_grads[2], param_grads[3], param_grads[4], param_grads[5], residual_rms)
```

```python
import functools

import jax
import jax.numpy as jnp
from jax import lax
from jax.experimental import pallas as pl
from jax.experimental.pallas import tpu as pltpu
from jax.sharding import PartitionSpec as P

HEAD = 64
norm_eps = 1e-05
root_half = 0.7071067811865476
slope_scale = 0.3989422804014327
score_scale = 0.125
big_negative = -1e30
f32 = jnp.float32
bf16 = jnp.bfloat16
GROUP = 4 * HEAD
TILE = 512
WIDE = 1024
STASH = 10


def nn(a, b):
    return lax.dot_general(a, b, (((1,), (0,)), ((), ())), preferred_element_type=f32)


def nt(a, b):
    return lax.dot_general(a, b, (((1,), (1,)), ((), ())), preferred_element_type=f32)


def row_stats(rows):
    average = jnp.mean(rows, axis=-1, keepdims=True)
    centered = rows - average
    inverse = lax.rsqrt(jnp.mean(centered * centered, axis=-1, keepdims=True) + norm_eps)
    return centered * inverse, inverse


def gate(values):
    bell = jnp.exp(-0.5 * values * values)
    upper = 0.5 * (1.0 + lax.erf(values * root_half))
    return values * upper, upper + values * bell * slope_scale


def loop(count, body, unroll=1):
    def run(i, carry):
        body(i)
        return carry

    lax.fori_loop(0, count, run, 0, unroll=unroll)


def part(i, size):
    return pl.ds(pl.multiple_of(i * size, size), size)


def copies(pairs, sem):
    return [pltpu.make_async_copy(a, b, sem.at[i]) for i, (a, b) in enumerate(pairs)]


def forward_kernel(slot, *refs):
    flags, norms, biases, feat, recv, w_in, w_out, w_up, w_down = refs[:9]
    z_out, squares_out = refs[19:21]
    s_x, s_a, s_qkv, s_c, s_l, s_h, s_b, s_g, s_d, s_p = refs[21:31]
    (v_in, v_out, v_up, v_down, v_x, v_a, v_qkv, v_c, v_l, v_h, v_b, v_g, v_d, v_p, v_bias, v_acc, v_z,
     sem_w, sem_x, sem_o, sem_p, sem_g, sem_d) = refs[31:]
    rows, width = v_x.shape
    hidden = v_up.shape[1]
    here = pl.ds(slot * rows, rows)

    @pl.when(flags[0] == 1)
    def _():
        length = flags[1]
        causal = flags[2] == 1
        from_feat = flags[3] == 1
        picked = flags[4]

        @pl.when(from_feat)
        def _():
            pltpu.make_async_copy(feat.at[picked], v_x, sem_x.at[0]).start()

        @pl.when(jnp.logical_not(from_feat))
        def _():
            pltpu.make_async_copy(recv, v_x, sem_x.at[0]).start()

        def column(source, target, index):
            def at(i):
                return pltpu.make_async_copy(
                    source.at[:, part(i, WIDE)], target.at[:, part(i, WIDE)], sem_w.at[index + i]
                )

            return at

        def down_copy(i):
            return pltpu.make_async_copy(
                w_down.at[part(i, WIDE)], v_down.at[part(i, WIDE)], sem_w.at[3 + 1 + hidden // WIDE + i]
            )

        in_copy, out_copy, up_copy = column(w_in, v_in, 0), column(w_out, v_out, 3), column(w_up, v_up, 4)
        for i in range(3):
            in_copy(i).start()
        out_copy(0).start()
        for i in range(hidden // WIDE):
            up_copy(i).start()
            down_copy(i).start()

        def bias_rows(i):
            at = part(i, 128)
            query = lax.broadcasted_iota(jnp.int32, (128, rows), 0) + i * 128
            key = lax.broadcasted_iota(jnp.int32, (128, rows), 1)
            open_ = (key < length) & ((key <= query) | jnp.logical_not(causal))
            v_bias[at, :] = jnp.where(open_, 0.0, big_negative)

        loop(rows // 128, bias_rows)
        pltpu.make_async_copy(recv, v_x, sem_x.at[0]).wait()

        def first_norm(i):
            at = part(i, 64)
            normed, _ = row_stats(v_x[at, :].astype(f32))
            v_a[at, :] = (normed * norms[0:1, :] + norms[1:2, :]).astype(bf16)

        loop(rows // 64, first_norm)
        outs = []

        def send(source, target, index):
            copy = pltpu.make_async_copy(source, target, sem_o.at[index])
            copy.start()
            outs.append(copy)

        send(v_x, s_x.at[here], 0)
        send(v_a, s_a.at[here], 1)
        def project(i):
            in_copy(i).wait()
            at = part(i, WIDE)
            tile = nn(v_a[...], v_in[:, at]) + biases[0:1, at]
            v_qkv[:, at] = tile.astype(bf16)

        loop(3 * width // WIDE, project)
        send(v_qkv, s_qkv.at[here], 2)
        lane = lax.broadcasted_iota(jnp.int32, (1, GROUP), 1) // HEAD
        groups = width // GROUP

        def p_copy(i):
            return pltpu.make_async_copy(
                v_p.at[i % 2], s_p.at[slot, pl.ds(i * 4, 4)], sem_p.at[i % 2]
            )

        def attend(i):
            at = part(i, GROUP)
            query = v_qkv[:, at]
            key = v_qkv[:, pl.ds(pl.multiple_of(width + i * GROUP, GROUP), GROUP)]
            value = v_qkv[:, pl.ds(pl.multiple_of(2 * width + i * GROUP, GROUP), GROUP)]

            @pl.when(i >= 2)
            def _():
                p_copy(i - 2).wait()

            half = rows // 2
            for r in range(2):
                picked_rows = slice(r * half, (r + 1) * half)
                scaled = query[picked_rows] * score_scale
                total = jnp.zeros((half, GROUP), f32)
                sums = jnp.ones((half, GROUP), f32)
                for h in range(4):
                    masked = jnp.where(lane == h, scaled, 0).astype(bf16)
                    scores = nt(masked, key) + v_bias[picked_rows, :]
                    top = jnp.max(scores, axis=-1, keepdims=True)
                    raised = jnp.exp(scores - top).astype(bf16)
                    v_p[i % 2, h, picked_rows, :] = raised
                    product = nn(raised, jnp.where(lane == h, value, 1).astype(bf16))
                    total = jnp.where(lane == h, product, total)
                    sums = jnp.where(lane == (h ^ 1), product, sums)
                inverse = 1.0 / jnp.concatenate(
                    [pltpu.roll(sums[:, k : k + 128], HEAD, 1) for k in (0, 128)], axis=1
                )
                v_l[picked_rows, at] = inverse
                v_c[picked_rows, at] = (total * inverse).astype(bf16)
            p_copy(i).start()

        loop(groups, attend)
        send(v_c, s_c.at[here], 8)
        send(v_l, s_l.at[here], 9)
        out_copy(0).wait()
        def mix(i):
            at = part(i, WIDE)
            v_acc[:, at] = nn(v_c[...], v_out[:, at]) + biases[3:4, at]

        loop(width // WIDE, mix)

        valid = lambda i, n: (lax.broadcasted_iota(jnp.int32, (n, 1), 0) + i * n < length).astype(f32)

        def square(values, mask):
            return jnp.sum((values * values * mask).reshape(-1, 8, width), axis=0)

        def second_norm(i, carry):
            at = part(i, 64)
            branch = v_acc[at, :]
            middle = v_x[at, :].astype(f32) + branch
            v_h[at, :] = middle
            normed, _ = row_stats(middle)
            v_b[at, :] = (normed * norms[2:3, :] + norms[3:4, :]).astype(bf16)
            v_acc[at, :] = jnp.broadcast_to(biases[4:5, :width], (64, width))
            mask = valid(i, 64)
            return (carry[0] + square(middle, mask), carry[1] + square(branch, mask))

        nothing = jnp.zeros((8, width), f32)
        sums_one = (nothing, nothing)
        sums_one = lax.fori_loop(0, rows // 64, second_norm, sums_one)
        send(v_h, s_h.at[here], 3)
        send(v_b, s_b.at[here], 4)

        def feed(i):
            up_copy(i).wait()
            down_copy(i).wait()
            at = part(i, WIDE)
            half = rows // 2
            for r in range(2):
                rr = slice(r * half, (r + 1) * half)
                pre = nn(v_b[rr, :], v_up[:, at]) + biases[5:6, at]
                act, slope = gate(pre)
                act = act.astype(bf16)
                v_g[rr, at] = act
                v_d[rr, at] = slope.astype(bf16)
                v_acc[rr, :] += nn(act, v_down[at, :])
            g_copy(i).start()
            d_copy(i).start()

        def g_copy(i):
            at = part(i, WIDE)
            return pltpu.make_async_copy(v_g.at[:, at], s_g.at[here, at], sem_g.at[i])

        def d_copy(i):
            at = part(i, WIDE)
            return pltpu.make_async_copy(v_d.at[:, at], s_d.at[here, at], sem_d.at[i])

        loop(hidden // WIDE, feed)

        def finish(i, carry):
            at = part(i, 64)
            branch = v_acc[at, :]
            output = v_h[at, :] + branch
            v_z[at, :] = output.astype(bf16)
            mask = valid(i, 64)
            return (carry[0] + square(output, mask), carry[1] + square(branch, mask))

        sums_two = (nothing, nothing)
        sums_two = lax.fori_loop(0, rows // 64, finish, sums_two)
        send(v_z, z_out, 7)
        for k, value in enumerate((sums_one[0], sums_two[0], sums_one[1], sums_two[1])):
            squares_out[k] = value
        for copy in outs:
            copy.wait()
        for i in range(hidden // WIDE):
            g_copy(i).wait()
            d_copy(i).wait()
        p_copy(groups - 2).wait()
        p_copy(groups - 1).wait()

    @pl.when(flags[0] != 1)
    def _():
        squares_out[...] = jnp.zeros_like(squares_out)


def stash_shapes(rows, width, hidden):
    heads = width // HEAD
    return [
        jax.ShapeDtypeStruct((2 * rows, width), bf16),
        jax.ShapeDtypeStruct((2 * rows, width), bf16),
        jax.ShapeDtypeStruct((2 * rows, 3 * width), bf16),
        jax.ShapeDtypeStruct((2 * rows, width), bf16),
        jax.ShapeDtypeStruct((2 * rows, width), f32),
        jax.ShapeDtypeStruct((2 * rows, width), f32),
        jax.ShapeDtypeStruct((2 * rows, width), bf16),
        jax.ShapeDtypeStruct((2 * rows, hidden), bf16),
        jax.ShapeDtypeStruct((2 * rows, hidden), bf16),
        jax.ShapeDtypeStruct((2, heads, rows, rows), bf16),
    ]


def forward_call(slot, flags, norms, biases, feat, recv, weights, stash):
    rows, width = recv.shape
    hidden = weights[2].shape[1]
    any_ = pl.BlockSpec(memory_space=pl.ANY)
    vm = pl.BlockSpec(memory_space=pltpu.VMEM)
    first = stash is None
    shapes = stash_shapes(rows, width, hidden)
    if first:
        stash = [jnp.zeros((8, 128), f32)] * STASH
    results = pl.pallas_call(
        functools.partial(forward_kernel, slot),
        in_specs=[pl.BlockSpec(memory_space=pltpu.SMEM), vm, vm] + [any_] * 6 + [any_] * STASH,
        out_specs=[any_, vm] + [any_] * STASH,
        out_shape=[jax.ShapeDtypeStruct((rows, width), bf16), jax.ShapeDtypeStruct((4, 8, width), f32)] + shapes,
        input_output_aliases={} if first else {9 + k: 2 + k for k in range(STASH)},
        scratch_shapes=[
            pltpu.VMEM(w.shape, bf16) for w in weights
        ] + [
            pltpu.VMEM((rows, width), bf16),
            pltpu.VMEM((rows, width), bf16),
            pltpu.VMEM((rows, 3 * width), bf16),
            pltpu.VMEM((rows, width), bf16),
            pltpu.VMEM((rows, width), f32),
            pltpu.VMEM((rows, width), f32),
            pltpu.VMEM((rows, width), bf16),
            pltpu.VMEM((rows, hidden), bf16),
            pltpu.VMEM((rows, hidden), bf16),
            pltpu.VMEM((2, 4, rows, rows), bf16),
            pltpu.VMEM((rows, rows), f32),
            pltpu.VMEM((rows, width), f32),
            pltpu.VMEM((rows, width), bf16),
            pltpu.SemaphoreType.DMA((4 + 2 * hidden // WIDE,)),
            pltpu.SemaphoreType.DMA((1,)),
            pltpu.SemaphoreType.DMA((10,)),
            pltpu.SemaphoreType.DMA((2,)),
            pltpu.SemaphoreType.DMA((hidden // WIDE,)),
            pltpu.SemaphoreType.DMA((hidden // WIDE,)),
        ],
        compiler_params=pltpu.CompilerParams(vmem_limit_bytes=62 * 2**20),
        cost_estimate=pl.CostEstimate(flops=14 * 10**9, bytes_accessed=50 * 10**6, transcendentals=6 * 10**6),
        name="layer_forward",
    )(flags, norms, biases, feat, recv, *weights, *stash)
    return results[0], results[1], results[2:]


def backward_kernel(slot, *refs):
    flags, norms, cot, recv, w_in, w_out, w_up, w_down = refs[:8]
    s_x, s_qkv, s_c, s_l, s_h, s_d, s_p = refs[8:15]
    dx_out, smalls = refs[18:20]
    g_up, g_mid, g_qkv = refs[20:23]
    (v_in, v_out, v_up, v_down, v_x, v_dy, v_qkv, v_c, v_l, v_h, v_d, v_p, v_du, v_do, v_dc, v_dqkv, v_acc,
     v_s, v_k, v_dx, sem_w, sem_x, sem_d, sem_p, sem_o) = refs[23:]
    rows, width = v_x.shape
    hidden = v_up.shape[1]
    here = pl.ds(slot * rows, rows)
    tiles = hidden // WIDE

    @pl.when(flags[0] == 1)
    def _():
        length = flags[1]
        from_cot = flags[3] == 0
        picked = flags[4]

        @pl.when(from_cot)
        def _():
            pltpu.make_async_copy(cot.at[picked], v_dy, sem_x.at[0]).start()

        @pl.when(jnp.logical_not(from_cot))
        def _():
            pltpu.make_async_copy(recv, v_dy, sem_x.at[0]).start()

        def down_copy(i):
            return pltpu.make_async_copy(
                w_down.at[part(i, WIDE)], v_down.at[part(i, WIDE)], sem_w.at[i]
            )

        def up_copy(i):
            at = part(i, WIDE)
            return pltpu.make_async_copy(w_up.at[:, at], v_up.at[:, at], sem_w.at[tiles + i])

        def d_copy(i):
            return pltpu.make_async_copy(
                s_d.at[here, part(i, WIDE)], v_d.at[i % 2], sem_d.at[i % 2]
            )

        def p_copy(i):
            return pltpu.make_async_copy(
                s_p.at[slot, pl.ds(i * 4, 4)], v_p.at[i % 2], sem_p.at[i % 2]
            )

        loads = copies(
            [
                (s_x.at[here], v_x),
                (s_qkv.at[here], v_qkv),
                (s_c.at[here], v_c),
                (s_l.at[here], v_l),
                (s_h.at[here], v_h),
                (w_out, v_out),
                (w_in, v_in),
            ],
            sem_x.at[pl.ds(1, 7)],
        )
        d_copy(0).start()
        for i in range(tiles):
            down_copy(i).start()
            up_copy(i).start()
            if i == 0:
                d_copy(1).start()
        for k in (4, 5, 1, 2, 3):
            loads[k].start()
        p_copy(0).start()
        p_copy(1).start()
        loads[6].start()
        loads[0].start()
        pltpu.make_async_copy(recv, v_dy, sem_x.at[0]).wait()
        nothing = jnp.zeros((8, width), f32)

        def fold(values):
            return jnp.sum(values.reshape(-1, 8, width), axis=0)

        def enter(i, total):
            at = part(i, 64)
            place = lax.broadcasted_iota(jnp.int32, (64, 1), 0) + i * 64
            masked = jnp.where(place < length, v_dy[at, :].astype(f32), 0.0)
            v_dy[at, :] = masked.astype(bf16)
            v_acc[at, :] = jnp.zeros((64, width), f32)
            return total + fold(masked)

        total = lax.fori_loop(0, rows // 64, enter, nothing)
        smalls[7:8, :] = jnp.sum(total, axis=0, keepdims=True)

        def feed(i):
            down_copy(i).wait()
            up_copy(i).wait()
            d_copy(i).wait()
            at = part(i, WIDE)
            half = rows // 2
            for r in range(2):
                rr = slice(r * half, (r + 1) * half)
                pre = nt(v_dy[rr, :], v_down[at, :]) * v_d[i % 2, rr, :].astype(f32)
                pre = pre.astype(bf16)
                v_du[rr, at] = pre
                v_acc[rr, :] += nt(pre, v_up[:, at])
            smalls[pl.ds(8 + i, 1), :] = jnp.sum(v_du[:, at].astype(f32), axis=0, keepdims=True)
            pltpu.make_async_copy(v_du.at[:, at], g_up.at[here, at], sem_o.at[3]).start()

            @pl.when(i + 2 < tiles)
            def _():
                d_copy(i + 2).start()

        loop(tiles, feed)
        loads[4].wait()
        loads[5].wait()

        def norm_back(source, grad, gain):
            normed, inverse = row_stats(source)
            scaled = grad * gain
            mean_one = jnp.mean(scaled, axis=-1, keepdims=True)
            mean_two = jnp.mean(scaled * normed, axis=-1, keepdims=True)
            return inverse * (scaled - mean_one - normed * mean_two), fold(grad * normed), fold(grad)

        def second_norm(i, carry):
            at = part(i, 64)
            rows_back, one, two = norm_back(v_h[at, :], v_acc[at, :], norms[2:3, :])
            middle = rows_back + v_dy[at, :].astype(f32)
            v_acc[at, :] = middle
            low = middle.astype(bf16)
            v_do[at, :] = low
            return carry[0] + one, carry[1] + two, carry[2] + fold(low.astype(f32))

        sums = lax.fori_loop(0, rows // 64, second_norm, (nothing,) * 3)
        for k, value in zip((2, 3, 6), sums):
            smalls[k : k + 1, :] = jnp.sum(value, axis=0, keepdims=True)
        do_copy = pltpu.make_async_copy(v_do, g_mid.at[here], sem_o.at[0])
        do_copy.start()
        v_dc[...] = nt(v_do[...], v_out[...]).astype(bf16)
        for k in (1, 2, 3):
            loads[k].wait()
        lane = lax.broadcasted_iota(jnp.int32, (1, GROUP), 1) // HEAD

        def attend(i):
            p_copy(i).wait()
            at = part(i, GROUP)
            key_at = pl.ds(pl.multiple_of(width + i * GROUP, GROUP), GROUP)
            value_at = pl.ds(pl.multiple_of(2 * width + i * GROUP, GROUP), GROUP)
            key = v_qkv[:, key_at]
            value = v_qkv[:, value_at]
            query = v_qkv[:, at]
            wide = v_dc[:, at].astype(f32) * v_l[:, at]
            low = wide.astype(bf16)
            dots = wide * v_c[:, at].astype(f32)
            for h in range(4):
                hs = slice(h * rows, (h + 1) * rows)
                v_k[hs, :] = jnp.where(lane == h, key, 0).astype(bf16)
                masked = jnp.where(lane == h, low, 0).astype(bf16)
                delta = jnp.sum(jnp.where(lane == h, dots, 0.0), axis=-1, keepdims=True)
                inner = nt(masked, value) - delta
                v_s[:, hs] = (v_p[i % 2, h].astype(f32) * inner).astype(bf16)
            grad_query = (nn(v_s[...], v_k[...]) * score_scale).astype(bf16)
            query_t = query.T
            low_t = low.T
            keys, values = [], []
            for h in range(4):
                hs = slice(h * HEAD, (h + 1) * HEAD)
                keys.append(nn(query_t[hs], v_s[:, h * rows : (h + 1) * rows]))
                values.append(nn(low_t[hs], v_p[i % 2, h]))
            grad_key = (jnp.concatenate(keys, axis=0) * score_scale).astype(bf16).T
            grad_value = jnp.concatenate(values, axis=0).astype(bf16).T
            v_dqkv[:, at] = grad_query
            v_dqkv[:, key_at] = grad_key
            v_dqkv[:, value_at] = grad_value
            smalls[4:5, at] = jnp.sum(grad_query.astype(f32), axis=0, keepdims=True)
            smalls[5:6, at] = jnp.sum(grad_value.astype(f32), axis=0, keepdims=True)

            @pl.when(i + 2 < width // GROUP)
            def _():
                p_copy(i + 2).start()

        loop(width // GROUP, attend)
        qkv_copy = pltpu.make_async_copy(v_dqkv, g_qkv.at[here], sem_o.at[1])
        qkv_copy.start()
        loads[6].wait()
        loads[0].wait()
        def enter_grad(i):
            at = part(i, TILE)
            v_h[:, at] = nt(v_dqkv[...], v_in[at, :])

        loop(width // TILE, enter_grad)

        def first_norm(i, carry):
            at = part(i, 64)
            rows_back, one, two = norm_back(v_x[at, :].astype(f32), v_h[at, :], norms[0:1, :])
            v_dx[at, :] = (rows_back + v_acc[at, :]).astype(bf16)
            return carry[0] + one, carry[1] + two

        sums = lax.fori_loop(0, rows // 64, first_norm, (nothing,) * 2)
        for k, value in enumerate(sums):
            smalls[k : k + 1, :] = jnp.sum(value, axis=0, keepdims=True)
        dx_copy = pltpu.make_async_copy(v_dx, dx_out, sem_o.at[2])
        dx_copy.start()
        for copy in (do_copy, qkv_copy, dx_copy):
            copy.wait()
        pltpu.make_async_copy(v_du, g_up.at[here], sem_o.at[3]).wait()

    @pl.when(flags[0] != 1)
    def _():
        smalls[...] = jnp.zeros_like(smalls)


def backward_call(slot, flags, norms, cot, recv, weights, stash, grads):
    rows, width = recv.shape
    hidden = weights[2].shape[1]
    any_ = pl.BlockSpec(memory_space=pl.ANY)
    vm = pl.BlockSpec(memory_space=pltpu.VMEM)
    first = grads is None
    shapes = [jax.ShapeDtypeStruct((2 * rows, n), bf16) for n in (hidden, width, 3 * width)]
    if first:
        grads = [jnp.zeros((8, 128), f32)] * 3
    s_x, s_a, s_qkv, s_c, s_l, s_h, s_b, s_g, s_d, s_p = stash
    results = pl.pallas_call(
        functools.partial(backward_kernel, slot),
        in_specs=[pl.BlockSpec(memory_space=pltpu.SMEM), vm] + [any_] * 16,
        out_specs=[any_, vm] + [any_] * 3,
        out_shape=[
            jax.ShapeDtypeStruct((rows, width), bf16),
            jax.ShapeDtypeStruct((8 + hidden // WIDE, width), f32),
        ] + shapes,
        input_output_aliases={} if first else {15 + k: 2 + k for k in range(3)},
        scratch_shapes=[pltpu.VMEM(w.shape, bf16) for w in weights] + [
            pltpu.VMEM((rows, width), bf16),
            pltpu.VMEM((rows, width), bf16),
            pltpu.VMEM((rows, 3 * width), bf16),
            pltpu.VMEM((rows, width), bf16),
            pltpu.VMEM((rows, width), f32),
            pltpu.VMEM((rows, width), f32),
            pltpu.VMEM((2, rows, WIDE), bf16),
            pltpu.VMEM((2, 4, rows, rows), bf16),
            pltpu.VMEM((rows, hidden), bf16),
            pltpu.VMEM((rows, width), bf16),
            pltpu.VMEM((rows, width), bf16),
            pltpu.VMEM((rows, 3 * width), bf16),
            pltpu.VMEM((rows, width), f32),
            pltpu.VMEM((rows, 4 * rows), bf16),
            pltpu.VMEM((4 * rows, GROUP), bf16),
            pltpu.VMEM((rows, width), bf16),
            pltpu.SemaphoreType.DMA((2 * hidden // WIDE,)),
            pltpu.SemaphoreType.DMA((8,)),
            pltpu.SemaphoreType.DMA((2,)),
            pltpu.SemaphoreType.DMA((2,)),
            pltpu.SemaphoreType.DMA((4,)),
        ],
        compiler_params=pltpu.CompilerParams(vmem_limit_bytes=62 * 2**20),
        cost_estimate=pl.CostEstimate(flops=18 * 10**9, bytes_accessed=60 * 10**6, transcendentals=0),
        name="layer_backward",
    )(flags, norms, cot, recv, *weights, s_x, s_qkv, s_c, s_l, s_h, s_d, s_p, *grads)
    return results[0], results[1], results[2:]


highest = lax.Precision.HIGHEST


def transposed_product(former, latter):
    return lax.dot_general(
        former, latter, (((0,), (0,)), ((), ())), preferred_element_type=jnp.float32
    )


def added(terms):
    total = terms[0].astype(f32)
    for term in terms[1:]:
        total = total + term.astype(f32)
    return total


def pick(array, axis, index):
    return lax.dynamic_index_in_dim(array, index, axis, keepdims=False)


class Exchange:
    def __init__(self, terms, bits, order):
        self.terms = terms
        self.left = list(range(bits - 1, -1, -1))
        self.order = list(order)
        self.kind = terms[0].dtype

    def step(self, theirs=None):
        bit = self.order.pop(0)
        axis = self.left.index(bit)
        self.left.pop(axis)
        mine = (lax.axis_index("dp") >> bit) & 1
        if theirs is None:
            theirs = added([pick(term, axis, 1 - mine) for term in self.terms]).astype(self.kind)
            self.terms = [pick(term, axis, mine) for term in self.terms]
        size = lax.axis_size("dp")
        pairs = [(i, i ^ (1 << bit)) for i in range(size)]
        self.terms = self.terms + [lax.ppermute(theirs, "dp", pairs)]

    def finish(self):
        while self.order:
            self.step()
        return added(self.terms)


def weight_sum(former, latter, bits, orders):
    rows = former.shape[0]
    size = 1 << bits
    blocks = former.reshape((rows, size // 2, 2, former.shape[1] // size))
    core = lax.axis_index("dp") & 1
    halves = []
    for which in (1 - core, core):
        columns = pick(blocks, 2, which).reshape(rows, former.shape[1] // 2)
        halves.append(transposed_product(columns, latter).astype(bf16))
    theirs, mine = halves
    size_of = [2] * (bits - 1) + [former.shape[1] // size]
    pairs = [(i, i ^ 1) for i in range(size)]
    received = lax.ppermute(theirs, "dp", pairs)
    start = 0
    parts = []
    for columns, order in orders:
        cut = slice(start, start + columns)
        start += columns
        exchange = Shifted(
            [half[:, cut].reshape(size_of + [columns]) for half in (mine, received)], bits - 1, order
        )
        parts.append(exchange)
    return parts


class Shifted(Exchange):
    def __init__(self, terms, bits, order):
        super().__init__(terms, bits, order)
        self.left = list(range(bits, 0, -1))


def shards(
    features,
    cotangent,
    lengths,
    codebook_index,
    attention_in,
    attention_out,
    feed_up,
    feed_down,
    vectors,
    adaptive_weight,
    codebook_table,
):
    is_first = lax.axis_index("section") == 0
    first = is_first.astype(jnp.int32)
    last = 1 - first
    rows, width = features.shape[2:]
    hidden = feed_up.shape[2]
    size = lax.axis_size("dp")
    bits = size.bit_length() - 1
    feats = features[:, 0]
    cots = cotangent[:, 0]
    spans = lengths[:, 0]
    weights = (attention_in[0], attention_out[0], feed_up[0], feed_down[0])
    vector = vectors[0]
    raw_norms = vector[: 4 * width].reshape(4, width)
    pad = jnp.zeros((hidden - width,), f32)
    query_bias, value_bias, out_bias, down_bias = [
        vector[k * width : (k + 1) * width] for k in range(4, 8)
    ]
    zero = jnp.zeros((width,), f32)
    empty = jnp.zeros((hidden,), f32)
    biases = jnp.stack(
        [
            jnp.concatenate([query_bias, zero, value_bias, empty[: hidden - 3 * width]]),
            empty,
            empty,
            jnp.concatenate([out_bias, pad]),
            jnp.concatenate([down_bias, pad]),
            vector[8 * width :],
            empty,
            empty,
        ]
    )

    def flags(*values):
        return jnp.stack([jnp.asarray(value, jnp.int32) for value in values])

    def chosen(a, b):
        return jnp.where(is_first, a, b)

    def send(value, to):
        return lax.ppermute(value, "section", [(1 - to, to)])

    z_one, squares_one, stash = forward_call(
        0, flags(first, spans[0], 1, 1, 0), raw_norms, biases, feats, feats[0], weights, None
    )
    received_one = send(z_one, 1)
    table, z_one = lax.optimization_barrier((codebook_table, z_one))
    condition_table = jnp.dot(table, adaptive_weight, preferred_element_type=f32)
    one_hot = (
        codebook_index[:, 0][:, None]
        == jnp.arange(codebook_table.shape[0], dtype=jnp.int32)[None, :]
    ).astype(f32)
    condition = (jnp.dot(one_hot, condition_table, precision=highest) * last.astype(f32)).reshape(
        -1, 4, width
    )
    norms = [raw_norms + condition[k] for k in range(2)]
    z_two, squares_two, stash = forward_call(
        1,
        flags(1, chosen(spans[1], spans[0]), first, first, 1),
        norms[0],
        biases,
        feats,
        received_one,
        weights,
        stash,
    )
    received_two = send(z_two, 1)
    dx_one, smalls_one, grads = backward_call(
        1, flags(last, spans[0], 0, 0, 0), norms[0], cots, cots[0], weights, stash, None
    )
    back_one = send(dx_one, 0)
    z_three, squares_three, stash = forward_call(
        0,
        flags(last, spans[1], 0, 0, 0),
        norms[1],
        biases,
        feats,
        received_two,
        weights,
        stash,
    )
    dx_two, smalls_two, grads = backward_call(
        0,
        flags(1, chosen(spans[0], spans[1]), 0, first, 1),
        norms[1],
        cots,
        back_one,
        weights,
        stash,
        grads,
    )
    back_two = send(dx_two, 0)
    places = jnp.arange(rows, dtype=jnp.int32)[None, :, None]
    masked = jnp.where(places < spans[:, None, None], cots, 0)
    grad_feed = chosen(
        jnp.stack([back_one, back_two]), jnp.stack([masked[1], masked[0]])
    ).reshape(2 * rows, width)
    s_x, s_a, s_qkv, s_c, s_l, s_h, s_b, s_g, s_d, s_p = stash
    lower = list(range(1, bits))
    side_first = lower
    line_first = lower[1:] + lower[:1]
    half = width // 2
    down_parts = weight_sum(
        s_g, grad_feed, bits, [(half, line_first), (half, side_first)]
    )
    for part_ in down_parts:
        part_.step()
    dx_three, smalls_three, (g_up, g_mid, g_qkv) = backward_call(
        1, flags(first, spans[1], 0, 1, 0), raw_norms, cots, back_two, weights, stash, grads
    )
    up_parts = weight_sum(s_b, g_up, bits, [(hidden // 2, side_first)] * 2)
    out_parts = weight_sum(s_c, g_mid, bits, [(width, side_first)])
    in_parts = weight_sum(s_a, g_qkv, bits, [(width, side_first)] * 3)

    smalls = smalls_one + smalls_two + smalls_three
    picks = [one_hot[0], one_hot[1]]
    table_grad = (
        picks[0][:, None] * smalls_one[:4].reshape(1, -1)
        + picks[1][:, None] * (smalls_two[:4].reshape(1, -1) * last.astype(f32))
    )
    codes = table_grad.shape[0]
    share = table_grad.shape[1] // (2 * size)
    table_blocks = table_grad.reshape(codes, 2, size, share).transpose(2, 1, 0, 3)
    squares = jnp.sum(squares_one + squares_two + squares_three, axis=(1, 2))
    counted = jnp.sum(spans).astype(f32)
    totals = jnp.concatenate([squares, counted[None], jnp.zeros((123,), f32)])
    packed = jnp.concatenate(
        [
            smalls.reshape(size, -1),
            table_blocks.reshape(size, -1),
            jnp.broadcast_to(totals[None], (size, 128)),
        ],
        axis=1,
    )
    length = packed.shape[1]
    small_sum = Exchange(
        [packed.reshape([2] * bits + [length])], bits, list(range(bits))
    ).finish()
    vector_share = small_sum[: smalls.size // size]
    table_share = small_sum[smalls.size // size : -128].reshape(2, codes, share)
    totals = small_sum[-128:]
    table_own = chosen(send(table_share[0], 0), table_share[1])
    grad_adaptive = lax.dot_general(
        codebook_table.astype(f32),
        table_own,
        (((0,), (0,)), ((), ())),
        precision=highest,
        preferred_element_type=f32,
    )
    residual_rms = jnp.sqrt(totals[:4] / (totals[4] * width))[None]

    def joined(parts):
        return jnp.concatenate([part_.finish() for part_ in parts], axis=-1)[None]

    layer_outputs = jnp.stack([chosen(z_one, z_two), chosen(z_two, z_three)])[None, :, None]
    input_grads = jnp.stack([chosen(dx_two, dx_one), chosen(dx_three, dx_two)])[None, :, None]
    down_sum = joined(down_parts)
    up_sum = joined(up_parts)
    out_sum = joined(out_parts)
    in_sum = joined(in_parts)
    return (
        layer_outputs,
        input_grads,
        in_sum,
        out_sum,
        up_sum,
        down_sum,
        vector_share[None],
        grad_adaptive,
        residual_rms,
    )


def solution(mesh):
    placed = (
        P(None, "dp", None, None),
        P(None, "dp", None, None),
        P(None, "dp"),
        P(None, "dp"),
        P("section", None, None),
        P("section", None, None),
        P("section", None, None),
        P("section", None, None),
        P("section", None),
        P(),
        P(),
    )
    return jax.shard_map(
        shards,
        mesh=mesh,
        in_specs=placed,
        out_specs=(
            P("section", None, "dp", None, None),
            P("section", None, "dp", None, None),
            P("section", "dp", None),
            P("section", "dp", None),
            P("section", "dp", None),
            P("section", "dp", None),
            P("section", "dp"),
            P(None, ("section", "dp")),
            P("section", None),
        ),
        check_vma=False,
    )
```

```python
import functools

import jax
import jax.numpy as jnp
from jax import lax
from jax.experimental import pallas as pl
from jax.experimental.pallas import tpu as pltpu
from jax.sharding import PartitionSpec as P

HEAD = 64
norm_eps = 1e-05
root_half = 0.7071067811865476
slope_scale = 0.3989422804014327
score_scale = 0.125
big_negative = -1e30
f32 = jnp.float32
bf16 = jnp.bfloat16
GROUP = 4 * HEAD
TILE = 512
WIDE = 1024


def nn(a, b):
    return lax.dot_general(a, b, (((1,), (0,)), ((), ())), preferred_element_type=f32)


def nt(a, b):
    return lax.dot_general(a, b, (((1,), (1,)), ((), ())), preferred_element_type=f32)


def row_stats(rows):
    average = jnp.mean(rows, axis=-1, keepdims=True)
    centered = rows - average
    inverse = lax.rsqrt(jnp.mean(centered * centered, axis=-1, keepdims=True) + norm_eps)
    return centered * inverse, inverse


def gate(values):
    bell = jnp.exp(-0.5 * values * values)
    upper = 0.5 * (1.0 + lax.erf(values * root_half))
    return values * upper, upper + values * bell * slope_scale


def loop(count, body, unroll=1):
    def run(i, carry):
        body(i)
        return carry

    lax.fori_loop(0, count, run, 0, unroll=unroll)


def part(i, size):
    return pl.ds(pl.multiple_of(i * size, size), size)


def copies(pairs, sem):
    return [pltpu.make_async_copy(a, b, sem.at[i]) for i, (a, b) in enumerate(pairs)]


def chosen_tick(first, plan):
    picked = jnp.where(first, plan[0] or 0, plan[1] or 0)
    active = jnp.where(first, int(plan[0] is not None), int(plan[1] is not None)) == 1
    return active, picked


def forward_kernel(slot, plan, aliased, *refs):
    spans, norms, vectors, feat, recv, w_in, w_out, w_up, w_down = refs[:9]
    refs = refs[9 + aliased :]
    z_out, squares_out = refs[:2]
    s_x, s_a, s_qkv, s_c, s_l, s_h, s_b, s_g, s_d, s_p, layers = refs[2:13]
    (v_in, v_out, v_up, v_down, v_x, v_a, v_qkv, v_c, v_l, v_h, v_b, v_g, v_d, v_p, v_bias, v_acc, v_z,
     sem_w, sem_x, sem_o, sem_p, sem_g, sem_d) = refs[13:]
    rows, width = v_x.shape
    hidden = v_up.shape[1]
    here = pl.ds(slot * rows, rows)
    first = lax.axis_index("section") == 0
    active, picked = chosen_tick(first, plan)

    def norm(k):
        return norms[:, k * width : (k + 1) * width]

    def bias(k):
        return vectors[:, k * width : (k + 1) * width]

    @pl.when(active)
    def _():
        length = spans[picked, 0]
        causal = first

        @pl.when(first)
        def _():
            pltpu.make_async_copy(feat.at[picked, 0], v_x, sem_x.at[0]).start()

        @pl.when(jnp.logical_not(first))
        def _():
            pltpu.make_async_copy(recv, v_x, sem_x.at[0]).start()

        def column(source, target, index):
            def at(i):
                return pltpu.make_async_copy(
                    source.at[:, part(i, WIDE)], target.at[:, part(i, WIDE)], sem_w.at[index + i]
                )

            return at

        def down_copy(i):
            return pltpu.make_async_copy(
                w_down.at[part(i, WIDE)], v_down.at[part(i, WIDE)], sem_w.at[3 + 1 + hidden // WIDE + i]
            )

        in_copy, out_copy, up_copy = column(w_in, v_in, 0), column(w_out, v_out, 3), column(w_up, v_up, 4)
        for i in range(3):
            in_copy(i).start()
        out_copy(0).start()
        for i in range(hidden // WIDE):
            up_copy(i).start()
            down_copy(i).start()

        def bias_rows(i):
            at = part(i, 128)
            query = lax.broadcasted_iota(jnp.int32, (128, rows), 0) + i * 128
            key = lax.broadcasted_iota(jnp.int32, (128, rows), 1)
            open_ = (key < length) & ((key <= query) | jnp.logical_not(causal))
            v_bias[at, :] = jnp.where(open_, 0.0, big_negative)

        loop(rows // 128, bias_rows)
        pltpu.make_async_copy(recv, v_x, sem_x.at[0]).wait()

        def first_norm(i):
            at = part(i, 64)
            normed, _ = row_stats(v_x[at, :].astype(f32))
            v_a[at, :] = (normed * norm(0) + norm(1)).astype(bf16)

        loop(rows // 64, first_norm)
        outs = []

        def send(source, target, index):
            copy = pltpu.make_async_copy(source, target, sem_o.at[index])
            copy.start()
            outs.append(copy)

        send(v_x, s_x.at[here], 0)
        send(v_a, s_a.at[here], 1)
        def project(i):
            in_copy(i).wait()
            at = part(i, WIDE)
            shift = vectors[:, pl.ds(pl.multiple_of((4 + i // 2) * width, width), width)]
            tile = nn(v_a[...], v_in[:, at]) + jnp.where(i == 1, 0.0, shift)
            v_qkv[:, at] = tile.astype(bf16)

        loop(3 * width // WIDE, project)
        send(v_qkv, s_qkv.at[here], 2)
        lane = lax.broadcasted_iota(jnp.int32, (1, GROUP), 1) // HEAD
        groups = width // GROUP

        def p_copy(i):
            return pltpu.make_async_copy(
                v_p.at[i % 2], s_p.at[slot, pl.ds(i * 4, 4)], sem_p.at[i % 2]
            )

        def attend(i):
            at = part(i, GROUP)
            query = v_qkv[:, at]
            key = v_qkv[:, pl.ds(pl.multiple_of(width + i * GROUP, GROUP), GROUP)]
            value = v_qkv[:, pl.ds(pl.multiple_of(2 * width + i * GROUP, GROUP), GROUP)]

            @pl.when(i >= 2)
            def _():
                p_copy(i - 2).wait()

            half = rows // 2
            for r in range(2):
                picked_rows = slice(r * half, (r + 1) * half)
                scaled = query[picked_rows] * score_scale
                total = jnp.zeros((half, GROUP), f32)
                sums = jnp.ones((half, GROUP), f32)
                for h in range(4):
                    masked = jnp.where(lane == h, scaled, 0).astype(bf16)
                    scores = nt(masked, key) + v_bias[picked_rows, :]
                    top = jnp.max(scores, axis=-1, keepdims=True)
                    raised = jnp.exp(scores - top).astype(bf16)
                    v_p[i % 2, h, picked_rows, :] = raised
                    product = nn(raised, jnp.where(lane == h, value, 1).astype(bf16))
                    total = jnp.where(lane == h, product, total)
                    sums = jnp.where(lane == (h ^ 1), product, sums)
                inverse = 1.0 / jnp.concatenate(
                    [pltpu.roll(sums[:, k : k + 128], HEAD, 1) for k in (0, 128)], axis=1
                )
                v_l[picked_rows, at] = inverse
                v_c[picked_rows, at] = (total * inverse).astype(bf16)
            p_copy(i).start()

        loop(groups, attend)
        send(v_c, s_c.at[here], 8)
        send(v_l, s_l.at[here], 9)
        out_copy(0).wait()
        def mix(i):
            at = part(i, WIDE)
            v_acc[:, at] = nn(v_c[...], v_out[:, at]) + bias(6)

        loop(width // WIDE, mix)

        valid = lambda i, n: (lax.broadcasted_iota(jnp.int32, (n, 1), 0) + i * n < length).astype(f32)

        def square(values, mask):
            return jnp.sum((values * values * mask).reshape(-1, 8, width), axis=0)

        def second_norm(i, carry):
            at = part(i, 64)
            branch = v_acc[at, :]
            middle = v_x[at, :].astype(f32) + branch
            v_h[at, :] = middle
            normed, _ = row_stats(middle)
            v_b[at, :] = (normed * norm(2) + norm(3)).astype(bf16)
            v_acc[at, :] = jnp.broadcast_to(bias(7), (64, width))
            mask = valid(i, 64)
            return (carry[0] + square(middle, mask), carry[1] + square(branch, mask))

        nothing = jnp.zeros((8, width), f32)
        sums_one = (nothing, nothing)
        sums_one = lax.fori_loop(0, rows // 64, second_norm, sums_one)
        send(v_h, s_h.at[here], 3)
        send(v_b, s_b.at[here], 4)

        def feed(i):
            up_copy(i).wait()
            down_copy(i).wait()
            at = part(i, WIDE)
            half = rows // 2
            for r in range(2):
                rr = slice(r * half, (r + 1) * half)
                shift = vectors[:, pl.ds(pl.multiple_of(8 * width + i * WIDE, WIDE), WIDE)]
                pre = nn(v_b[rr, :], v_up[:, at]) + shift
                act, slope = gate(pre)
                act = act.astype(bf16)
                v_g[rr, at] = act
                v_d[rr, at] = slope.astype(bf16)
                v_acc[rr, :] += nn(act, v_down[at, :])
            g_copy(i).start()
            d_copy(i).start()

        def g_copy(i):
            at = part(i, WIDE)
            return pltpu.make_async_copy(v_g.at[:, at], s_g.at[here, at], sem_g.at[i])

        def d_copy(i):
            at = part(i, WIDE)
            return pltpu.make_async_copy(v_d.at[:, at], s_d.at[here, at], sem_d.at[i])

        loop(hidden // WIDE, feed)

        def finish(i, carry):
            at = part(i, 64)
            branch = v_acc[at, :]
            output = v_h[at, :] + branch
            v_z[at, :] = output.astype(bf16)
            mask = valid(i, 64)
            return (carry[0] + square(output, mask), carry[1] + square(branch, mask))

        sums_two = (nothing, nothing)
        sums_two = lax.fori_loop(0, rows // 64, finish, sums_two)
        send(v_z, z_out, 7)
        send(v_z, layers.at[0, picked, 0], 5)
        for k, value in enumerate((sums_one[0], sums_two[0], sums_one[1], sums_two[1])):
            squares_out[k] = value
        for copy in outs:
            copy.wait()
        for i in range(hidden // WIDE):
            g_copy(i).wait()
            d_copy(i).wait()
        p_copy(groups - 2).wait()
        p_copy(groups - 1).wait()

    @pl.when(jnp.logical_not(active))
    def _():
        squares_out[...] = jnp.zeros_like(squares_out)


def stash_shapes(rows, width, hidden):
    heads = width // HEAD
    return [
        jax.ShapeDtypeStruct((2 * rows, width), bf16),
        jax.ShapeDtypeStruct((2 * rows, width), bf16),
        jax.ShapeDtypeStruct((2 * rows, 3 * width), bf16),
        jax.ShapeDtypeStruct((2 * rows, width), bf16),
        jax.ShapeDtypeStruct((2 * rows, width), f32),
        jax.ShapeDtypeStruct((2 * rows, width), f32),
        jax.ShapeDtypeStruct((2 * rows, width), bf16),
        jax.ShapeDtypeStruct((2 * rows, hidden), bf16),
        jax.ShapeDtypeStruct((2 * rows, hidden), bf16),
        jax.ShapeDtypeStruct((2, heads, rows, rows), bf16),
        jax.ShapeDtypeStruct((1, 2, 1, rows, width), bf16),
    ]


def forward_call(slot, plan, spans, norms, vectors, feat, recv, weights, stash=()):
    rows, width = recv.shape
    hidden = weights[2].shape[1]
    any_ = pl.BlockSpec(memory_space=pl.ANY)
    vm = pl.BlockSpec(memory_space=pltpu.VMEM)
    shapes = stash_shapes(rows, width, hidden)
    results = pl.pallas_call(
        functools.partial(forward_kernel, slot, plan, len(stash)),
        in_specs=[pl.BlockSpec(memory_space=pltpu.SMEM), vm, vm] + [any_] * (6 + len(stash)),
        out_specs=[any_, vm] + [any_] * len(shapes),
        out_shape=[jax.ShapeDtypeStruct((rows, width), bf16), jax.ShapeDtypeStruct((4, 8, width), f32)] + shapes,
        input_output_aliases={9 + k: 2 + k for k in range(len(stash))},
        scratch_shapes=[
            pltpu.VMEM(w.shape, bf16) for w in weights
        ] + [
            pltpu.VMEM((rows, width), bf16),
            pltpu.VMEM((rows, width), bf16),
            pltpu.VMEM((rows, 3 * width), bf16),
            pltpu.VMEM((rows, width), bf16),
            pltpu.VMEM((rows, width), f32),
            pltpu.VMEM((rows, width), f32),
            pltpu.VMEM((rows, width), bf16),
            pltpu.VMEM((rows, hidden), bf16),
            pltpu.VMEM((rows, hidden), bf16),
            pltpu.VMEM((2, 4, rows, rows), bf16),
            pltpu.VMEM((rows, rows), f32),
            pltpu.VMEM((rows, width), f32),
            pltpu.VMEM((rows, width), bf16),
            pltpu.SemaphoreType.DMA((4 + 2 * hidden // WIDE,)),
            pltpu.SemaphoreType.DMA((1,)),
            pltpu.SemaphoreType.DMA((10,)),
            pltpu.SemaphoreType.DMA((2,)),
            pltpu.SemaphoreType.DMA((hidden // WIDE,)),
            pltpu.SemaphoreType.DMA((hidden // WIDE,)),
        ],
        compiler_params=pltpu.CompilerParams(vmem_limit_bytes=62 * 2**20),
        cost_estimate=pl.CostEstimate(flops=14 * 10**9, bytes_accessed=50 * 10**6, transcendentals=6 * 10**6),
        name="layer_forward",
    )(spans, norms, vectors, feat, recv, *weights, *stash)
    return results[0], results[1], results[2:]


def backward_kernel(slot, plan, aliased, fed, *refs):
    spans, norms, cot, recv, w_in, w_out, w_up, w_down = refs[:8]
    s_x, s_qkv, s_c, s_l, s_h, s_d, s_p = refs[8:15]
    refs = refs[15 + aliased :]
    dx_out, smalls = refs[:2]
    g_up, g_mid, g_qkv, inputs = refs[2:6]
    if fed:
        g_feed = refs[6]
    refs = refs[6 + fed :]
    (v_in, v_out, v_up, v_down, v_x, v_dy, v_qkv, v_c, v_l, v_h, v_d, v_p, v_du, v_do, v_dc, v_dqkv, v_acc,
     v_s, v_k, v_dx, sem_w, sem_x, sem_d, sem_p, sem_o) = refs
    rows, width = v_x.shape
    hidden = v_up.shape[1]
    here = pl.ds(slot * rows, rows)
    tiles = hidden // WIDE

    first = lax.axis_index("section") == 0
    active, picked = chosen_tick(first, plan)

    def norm(k):
        return norms[:, k * width : (k + 1) * width]

    @pl.when(active)
    def _():
        length = spans[picked, 0]

        @pl.when(jnp.logical_not(first))
        def _():
            pltpu.make_async_copy(cot.at[picked, 0], v_dy, sem_x.at[0]).start()

        @pl.when(first)
        def _():
            pltpu.make_async_copy(recv, v_dy, sem_x.at[0]).start()

        def down_copy(i):
            return pltpu.make_async_copy(
                w_down.at[part(i, WIDE)], v_down.at[part(i, WIDE)], sem_w.at[i]
            )

        def up_copy(i):
            at = part(i, WIDE)
            return pltpu.make_async_copy(w_up.at[:, at], v_up.at[:, at], sem_w.at[tiles + i])

        def d_copy(i):
            return pltpu.make_async_copy(
                s_d.at[here, part(i, WIDE)], v_d.at[i % 2], sem_d.at[i % 2]
            )

        def p_copy(i):
            return pltpu.make_async_copy(
                s_p.at[slot, pl.ds(i * 4, 4)], v_p.at[i % 2], sem_p.at[i % 2]
            )

        loads = copies(
            [
                (s_x.at[here], v_x),
                (s_qkv.at[here], v_qkv),
                (s_c.at[here], v_c),
                (s_l.at[here], v_l),
                (s_h.at[here], v_h),
                (w_out, v_out),
                (w_in, v_in),
            ],
            sem_x.at[pl.ds(1, 7)],
        )
        d_copy(0).start()
        for i in range(tiles):
            down_copy(i).start()
            up_copy(i).start()
            if i == 0:
                d_copy(1).start()
        for k in (4, 5, 1, 2, 3):
            loads[k].start()
        p_copy(0).start()
        p_copy(1).start()
        loads[6].start()
        loads[0].start()
        pltpu.make_async_copy(recv, v_dy, sem_x.at[0]).wait()
        nothing = jnp.zeros((8, width), f32)

        def fold(values):
            return jnp.sum(values.reshape(-1, 8, width), axis=0)

        def enter(i, total):
            at = part(i, 64)
            place = lax.broadcasted_iota(jnp.int32, (64, 1), 0) + i * 64
            masked = jnp.where(place < length, v_dy[at, :].astype(f32), 0.0)
            v_dy[at, :] = masked.astype(bf16)
            v_acc[at, :] = jnp.zeros((64, width), f32)
            return total + fold(masked)

        total = lax.fori_loop(0, rows // 64, enter, nothing)
        smalls[7:8, :] = jnp.sum(total, axis=0, keepdims=True)
        if fed:
            feed_copy = pltpu.make_async_copy(v_dy, g_feed.at[here], sem_o.at[4])
            feed_copy.start()

        def feed(i):
            down_copy(i).wait()
            up_copy(i).wait()
            d_copy(i).wait()
            at = part(i, WIDE)
            half = rows // 2
            for r in range(2):
                rr = slice(r * half, (r + 1) * half)
                pre = nt(v_dy[rr, :], v_down[at, :]) * v_d[i % 2, rr, :].astype(f32)
                pre = pre.astype(bf16)
                v_du[rr, at] = pre
                v_acc[rr, :] += nt(pre, v_up[:, at])
            smalls[pl.ds(8 + i, 1), :] = jnp.sum(v_du[:, at].astype(f32), axis=0, keepdims=True)
            pltpu.make_async_copy(v_du.at[:, at], g_up.at[here, at], sem_o.at[3]).start()

            @pl.when(i + 2 < tiles)
            def _():
                d_copy(i + 2).start()

        loop(tiles, feed)
        loads[4].wait()
        loads[5].wait()

        def norm_back(source, grad, gain):
            normed, inverse = row_stats(source)
            scaled = grad * gain
            mean_one = jnp.mean(scaled, axis=-1, keepdims=True)
            mean_two = jnp.mean(scaled * normed, axis=-1, keepdims=True)
            return inverse * (scaled - mean_one - normed * mean_two), fold(grad * normed), fold(grad)

        def second_norm(i, carry):
            at = part(i, 64)
            rows_back, one, two = norm_back(v_h[at, :], v_acc[at, :], norm(2))
            middle = rows_back + v_dy[at, :].astype(f32)
            v_acc[at, :] = middle
            low = middle.astype(bf16)
            v_do[at, :] = low
            return carry[0] + one, carry[1] + two, carry[2] + fold(low.astype(f32))

        sums = lax.fori_loop(0, rows // 64, second_norm, (nothing,) * 3)
        for k, value in zip((2, 3, 6), sums):
            smalls[k : k + 1, :] = jnp.sum(value, axis=0, keepdims=True)
        do_copy = pltpu.make_async_copy(v_do, g_mid.at[here], sem_o.at[0])
        do_copy.start()
        v_dc[...] = nt(v_do[...], v_out[...]).astype(bf16)
        for k in (1, 2, 3):
            loads[k].wait()
        lane = lax.broadcasted_iota(jnp.int32, (1, GROUP), 1) // HEAD

        def attend(i):
            p_copy(i).wait()
            at = part(i, GROUP)
            key_at = pl.ds(pl.multiple_of(width + i * GROUP, GROUP), GROUP)
            value_at = pl.ds(pl.multiple_of(2 * width + i * GROUP, GROUP), GROUP)
            key = v_qkv[:, key_at]
            value = v_qkv[:, value_at]
            query = v_qkv[:, at]
            wide = v_dc[:, at].astype(f32) * v_l[:, at]
            low = wide.astype(bf16)
            dots = wide * v_c[:, at].astype(f32)
            for h in range(4):
                hs = slice(h * rows, (h + 1) * rows)
                v_k[hs, :] = jnp.where(lane == h, key, 0).astype(bf16)
                masked = jnp.where(lane == h, low, 0).astype(bf16)
                delta = jnp.sum(jnp.where(lane == h, dots, 0.0), axis=-1, keepdims=True)
                inner = nt(masked, value) - delta
                v_s[:, hs] = (v_p[i % 2, h].astype(f32) * inner).astype(bf16)
            grad_query = (nn(v_s[...], v_k[...]) * score_scale).astype(bf16)
            query_t = query.T
            low_t = low.T
            keys, values = [], []
            for h in range(4):
                hs = slice(h * HEAD, (h + 1) * HEAD)
                keys.append(nn(query_t[hs], v_s[:, h * rows : (h + 1) * rows]))
                values.append(nn(low_t[hs], v_p[i % 2, h]))
            grad_key = (jnp.concatenate(keys, axis=0) * score_scale).astype(bf16).T
            grad_value = jnp.concatenate(values, axis=0).astype(bf16).T
            v_dqkv[:, at] = grad_query
            v_dqkv[:, key_at] = grad_key
            v_dqkv[:, value_at] = grad_value
            smalls[4:5, at] = jnp.sum(grad_query.astype(f32), axis=0, keepdims=True)
            smalls[5:6, at] = jnp.sum(grad_value.astype(f32), axis=0, keepdims=True)

            @pl.when(i + 2 < width // GROUP)
            def _():
                p_copy(i + 2).start()

        loop(width // GROUP, attend)
        qkv_copy = pltpu.make_async_copy(v_dqkv, g_qkv.at[here], sem_o.at[1])
        qkv_copy.start()
        loads[6].wait()
        loads[0].wait()
        def enter_grad(i):
            at = part(i, TILE)
            v_h[:, at] = nt(v_dqkv[...], v_in[at, :])

        loop(width // TILE, enter_grad)

        def first_norm(i, carry):
            at = part(i, 64)
            rows_back, one, two = norm_back(v_x[at, :].astype(f32), v_h[at, :], norm(0))
            v_dx[at, :] = (rows_back + v_acc[at, :]).astype(bf16)
            return carry[0] + one, carry[1] + two

        sums = lax.fori_loop(0, rows // 64, first_norm, (nothing,) * 2)
        for k, value in enumerate(sums):
            smalls[k : k + 1, :] = jnp.sum(value, axis=0, keepdims=True)
        dx_copy = pltpu.make_async_copy(v_dx, dx_out, sem_o.at[2])
        dx_copy.start()
        input_copy = pltpu.make_async_copy(v_dx, inputs.at[0, picked, 0], sem_o.at[5])
        input_copy.start()
        for copy in (do_copy, qkv_copy, dx_copy, input_copy):
            copy.wait()
        if fed:
            feed_copy.wait()
        pltpu.make_async_copy(v_du, g_up.at[here], sem_o.at[3]).wait()

    @pl.when(jnp.logical_not(active))
    def _():
        smalls[...] = jnp.zeros_like(smalls)


def backward_call(slot, plan, spans, norms, cot, recv, weights, stash, grads=(), fed=True):
    rows, width = recv.shape
    hidden = weights[2].shape[1]
    any_ = pl.BlockSpec(memory_space=pl.ANY)
    vm = pl.BlockSpec(memory_space=pltpu.VMEM)
    shapes = [jax.ShapeDtypeStruct((2 * rows, n), bf16) for n in (hidden, width, 3 * width)]
    shapes.append(jax.ShapeDtypeStruct((1, 2, 1, rows, width), bf16))
    if fed:
        shapes.append(jax.ShapeDtypeStruct((2 * rows, width), bf16))
    s_x, s_a, s_qkv, s_c, s_l, s_h, s_b, s_g, s_d, s_p, _ = stash
    grads = grads[: len(shapes)]
    results = pl.pallas_call(
        functools.partial(backward_kernel, slot, plan, len(grads), int(fed)),
        in_specs=[pl.BlockSpec(memory_space=pltpu.SMEM), vm] + [any_] * (13 + len(grads)),
        out_specs=[any_, vm] + [any_] * len(shapes),
        out_shape=[
            jax.ShapeDtypeStruct((rows, width), bf16),
            jax.ShapeDtypeStruct((8 + hidden // WIDE, width), f32),
        ] + shapes,
        input_output_aliases={15 + k: 2 + k for k in range(len(grads))},
        scratch_shapes=[pltpu.VMEM(w.shape, bf16) for w in weights] + [
            pltpu.VMEM((rows, width), bf16),
            pltpu.VMEM((rows, width), bf16),
            pltpu.VMEM((rows, 3 * width), bf16),
            pltpu.VMEM((rows, width), bf16),
            pltpu.VMEM((rows, width), f32),
            pltpu.VMEM((rows, width), f32),
            pltpu.VMEM((2, rows, WIDE), bf16),
            pltpu.VMEM((2, 4, rows, rows), bf16),
            pltpu.VMEM((rows, hidden), bf16),
            pltpu.VMEM((rows, width), bf16),
            pltpu.VMEM((rows, width), bf16),
            pltpu.VMEM((rows, 3 * width), bf16),
            pltpu.VMEM((rows, width), f32),
            pltpu.VMEM((rows, 4 * rows), bf16),
            pltpu.VMEM((4 * rows, GROUP), bf16),
            pltpu.VMEM((rows, width), bf16),
            pltpu.SemaphoreType.DMA((2 * hidden // WIDE,)),
            pltpu.SemaphoreType.DMA((8,)),
            pltpu.SemaphoreType.DMA((2,)),
            pltpu.SemaphoreType.DMA((2,)),
            pltpu.SemaphoreType.DMA((6,)),
        ],
        compiler_params=pltpu.CompilerParams(vmem_limit_bytes=62 * 2**20),
        cost_estimate=pl.CostEstimate(flops=18 * 10**9, bytes_accessed=60 * 10**6, transcendentals=0),
        name="layer_backward",
    )(spans, norms, cot, recv, *weights, s_x, s_qkv, s_c, s_l, s_h, s_d, s_p, *grads)
    return results[0], results[1], results[2:]


def turned_blocks(source, target, block):
    half = target.shape[0] // 2
    flat = source[...].T
    for core in range(2):

        @pl.when(lax.axis_index("dp") % 2 == core)
        def _(core=core):
            for k in range(half // block):
                other = (2 * k + 1 - core) * block
                own = (2 * k + core) * block
                target[k * block : (k + 1) * block, :] = flat[other : other + block]
                target[half + k * block : half + (k + 1) * block, :] = flat[own : own + block]


def weight_kernel(block, left, right, theirs, mine, turned):
    half = left.shape[1] // 2

    @pl.when(pl.program_id(1) == 0)
    def _():
        turned_blocks(left, turned, block)

    theirs[...] = nn(turned[:half, :], right[...]).astype(bf16)
    mine[...] = nn(turned[half:, :], right[...]).astype(bf16)


def feed_weight_kernel(block, left, right, late, theirs, mine, turned):
    half = left.shape[1] // 2
    rows = late.shape[0]
    turned_blocks(left, turned, block)
    second = jnp.where(lax.axis_index("section") == 0, late[...], right[rows:, :])
    for at, out in ((slice(0, half), theirs), (slice(half, 2 * half), mine)):
        out[...] = (nn(turned[at, :rows], right[:rows, :]) + nn(turned[at, rows:], second)).astype(bf16)


def weight_call(left, right, start, columns, late=None):
    rows, height = left.shape
    tall = min(height, WIDE)
    wide = min(columns, WIDE)
    block = height // lax.axis_size("dp")
    shape = jax.ShapeDtypeStruct((height // 2, columns), bf16)
    specs = [
        pl.BlockSpec((rows, tall), lambda i, j: (0, i)),
        pl.BlockSpec((rows, wide), lambda i, j: (0, start // wide + j)),
    ]
    operands = (left, right)
    if late is not None:
        assert wide == columns
        specs.append(pl.BlockSpec((rows // 2, wide), lambda i, j: (0, start // wide + j)))
        operands += (late,)
    return pl.pallas_call(
        functools.partial(weight_kernel if late is None else feed_weight_kernel, block),
        grid=(height // tall, columns // wide),
        in_specs=specs,
        out_specs=[pl.BlockSpec((tall // 2, wide), lambda i, j: (i, j))] * 2,
        out_shape=[shape] * 2,
        scratch_shapes=[pltpu.VMEM((tall, rows), bf16)],
        compiler_params=pltpu.CompilerParams(vmem_limit_bytes=40 * 2**20),
        cost_estimate=pl.CostEstimate(
            flops=2 * rows * height * columns,
            bytes_accessed=2 * (rows * height + rows * columns + height * columns),
            transcendentals=0,
        ),
        name="weight_product",
    )(*operands)


highest = lax.Precision.HIGHEST


def added(terms):
    total = terms[0].astype(f32)
    for term in terms[1:]:
        total = total + term.astype(f32)
    return total


def pick(array, axis, index):
    return lax.dynamic_index_in_dim(array, index, axis, keepdims=False)


class Line:
    def __init__(self):
        self.last = None

    def after(self, values):
        if self.last is not None:
            values = lax.optimization_barrier(tuple(values) + (self.last,))[:-1]
        return list(values)

    def done(self, value):
        self.last = value


class Exchange:
    def __init__(self, line, terms, left, order):
        self.line = line
        self.terms = terms
        self.left = sorted(left, reverse=True)
        self.order = list(order)
        self.kind = terms[0].dtype

    def step(self):
        bit = self.order.pop(0)
        axis = self.left.index(bit)
        self.left.pop(axis)
        mine = (lax.axis_index("dp") >> bit) & 1
        self.terms = self.line.after(self.terms)
        theirs = added([pick(term, axis, 1 - mine) for term in self.terms]).astype(self.kind)
        self.line.done(theirs)
        self.terms = [pick(term, axis, mine) for term in self.terms] + [crossed(theirs, bit)]

    def finish(self):
        while self.order:
            self.step()
        self.terms = self.line.after(self.terms)
        total = added(self.terms)
        self.line.done(total)
        return total


def crossed(value, bit):
    return lax.ppermute(value, "dp", [(i, i ^ (1 << bit)) for i in range(lax.axis_size("dp"))])


def weight_sum(line, left, right, start, columns, order, late=None):
    left, right = line.after((left, right))
    theirs, mine = weight_call(left, right, start, columns, late)
    line.done(theirs)
    size = lax.axis_size("dp")
    bits = size.bit_length() - 1
    shape = [2] * (bits - 1) + [left.shape[1] // size, columns]
    received = crossed(theirs, 0)
    terms = [half.reshape(shape) for half in (mine, received)]
    return Exchange(line, terms, range(1, bits), order)


def shards(
    features,
    cotangent,
    lengths,
    codebook_index,
    attention_in,
    attention_out,
    feed_up,
    feed_down,
    vectors,
    adaptive_weight,
    codebook_table,
):
    is_first = lax.axis_index("section") == 0
    adaptive = jnp.where(is_first, 0.0, 1.0)
    rows, width = features.shape[2:]
    hidden = feed_up.shape[2]
    size = lax.axis_size("dp")
    bits = size.bit_length() - 1
    weights = (attention_in[0], attention_out[0], feed_up[0], feed_down[0])

    def send(value, to):
        return lax.ppermute(value, "section", [(1 - to, to)])

    nowhere = jnp.zeros((rows, width), bf16)

    def forward(slot, plan, norms, recv, stash=()):
        return forward_call(slot, plan, lengths, norms, vectors, features, recv, weights, stash)

    def backward(slot, plan, norms, recv, stash, grads=(), fed=True):
        return backward_call(
            slot, plan, lengths, norms, cotangent, recv, weights, stash, grads, fed
        )

    z_one, squares_one, stash = forward(0, (0, None), vectors, nowhere)
    received_one = send(z_one, 1)
    table, z_one = lax.optimization_barrier((codebook_table, z_one))
    condition_table = jnp.dot(table, adaptive_weight, preferred_element_type=f32)
    one_hot = (
        codebook_index[:, 0][:, None]
        == jnp.arange(codebook_table.shape[0], dtype=jnp.int32)[None, :]
    ).astype(f32)
    norms = vectors[:, : 4 * width] + adaptive * jnp.dot(
        one_hot, condition_table, precision=highest
    )
    norms_one, norms_two = norms[:1], norms[1:]
    z_two, squares_two, stash = forward(1, (1, 0), norms_one, received_one, stash)
    received_two = send(z_two, 1)
    dx_one, smalls_one, grads = backward(1, (None, 0), norms_one, nowhere, stash)
    back_one = send(dx_one, 0)
    z_three, squares_three, stash = forward(0, (None, 1), norms_two, received_two, stash)
    dx_two, smalls_two, grads = backward(0, (0, 1), norms_two, back_one, stash, grads)
    back_two = send(dx_two, 0)

    s_x, s_a, s_qkv, s_c, s_l, s_h, s_b, s_g, s_d, s_p, layer_outputs = stash
    side_first = list(range(1, bits))
    line_first = side_first[1:] + side_first[:1]
    line = Line()
    half = width // 2
    g_feed = grads[4]
    down_one = weight_sum(line, s_g, g_feed, 0, half, line_first, back_two)
    down_two = weight_sum(line, s_g, g_feed, half, half, side_first, back_two)
    down_one.step()
    down_two.step()
    (back_two,) = line.after((back_two,))
    _, smalls_three, grads = backward(
        1, (1, None), vectors, back_two, stash, grads[:4], fed=False
    )
    line.done(smalls_three)
    g_up, g_mid, g_qkv, input_grads = grads
    down_one.step()
    down_two.step()
    up_one = weight_sum(line, s_b, g_up, 0, hidden // 2, side_first)
    up_two = weight_sum(line, s_b, g_up, hidden // 2, hidden // 2, side_first)
    up_one.step()
    down_two.step()
    down_one.step()

    smalls = smalls_one + smalls_two + smalls_three
    table_grad = one_hot[0][:, None] * smalls_one[:4].reshape(1, -1) + one_hot[1][:, None] * (
        smalls_two[:4].reshape(1, -1) * adaptive
    )
    codes = table_grad.shape[0]
    share = table_grad.shape[1] // (2 * size)
    table_blocks = table_grad.reshape(codes, 2, size, share).transpose(2, 1, 0, 3)
    squares = jnp.sum(squares_one + squares_two + squares_three, axis=(1, 2))
    counted = jnp.sum(lengths).astype(f32)
    totals = jnp.concatenate([squares, counted[None], jnp.zeros((123,), f32)])
    packed = jnp.concatenate(
        [
            smalls.reshape(size, -1),
            table_blocks.reshape(size, -1),
            jnp.broadcast_to(totals[None], (size, 128)),
        ],
        axis=1,
    )
    small = Exchange(
        line, [packed.reshape([2] * bits + [packed.shape[1]])], range(bits), range(bits)
    )
    small.step()
    in_one = weight_sum(line, s_a, g_qkv, 0, 2 * width, side_first)
    small.step()
    up_two.step()
    in_two = weight_sum(line, s_a, g_qkv, 2 * width, width, side_first)
    out_one = weight_sum(line, s_c, g_mid, 0, width, side_first)
    small.step()
    up_one.step()
    in_one.step()
    down_sum = [down_one.finish(), down_two.finish()]
    small.step()
    up_one.step()
    up_two.step()
    in_two.step()
    out_one.step()
    small_sum = small.finish()
    vector_share = small_sum[: smalls.size // size]
    table_share = small_sum[smalls.size // size : -128].reshape(2, codes, share)
    totals = small_sum[-128:]
    table_own = jnp.where(is_first, send(table_share[0], 0), table_share[1])
    up_two.step()
    in_one.step()
    up_one_sum = up_one.finish()
    in_one.step()
    up_sum = [up_one_sum, up_two.finish()]
    in_two.step()
    in_one_sum = in_one.finish()
    in_two.step()
    out_one.step()
    out_one.step()
    in_sum = [in_one_sum, in_two.finish()]
    out_sum = [out_one.finish()]
    grad_adaptive = lax.dot_general(
        codebook_table.astype(f32),
        table_own,
        (((0,), (0,)), ((), ())),
        precision=highest,
        preferred_element_type=f32,
    )
    residual_rms = jnp.sqrt(totals[:4] / (totals[4] * width))[None]

    def joined(parts):
        return jnp.concatenate(parts, axis=-1)[None]

    return (
        layer_outputs,
        input_grads,
        joined(in_sum),
        joined(out_sum),
        joined(up_sum),
        joined(down_sum),
        vector_share[None],
        grad_adaptive,
        residual_rms,
    )


def solution(mesh):
    placed = (
        P(None, "dp", None, None),
        P(None, "dp", None, None),
        P(None, "dp"),
        P(None, "dp"),
        P("section", None, None),
        P("section", None, None),
        P("section", None, None),
        P("section", None, None),
        P("section", None),
        P(),
        P(),
    )
    return jax.shard_map(
        shards,
        mesh=mesh,
        in_specs=placed,
        out_specs=(
            P("section", None, "dp", None, None),
            P("section", None, "dp", None, None),
            P("section", "dp", None),
            P("section", "dp", None),
            P("section", "dp", None),
            P("section", "dp", None),
            P("section", "dp"),
            P(None, ("section", "dp")),
            P("section", None),
        ),
        check_vma=False,
    )
```

```python
import functools
import itertools

import jax
import jax.numpy as jnp
from jax import lax
from jax.experimental import pallas as pl
from jax.experimental.pallas import tpu as pltpu
from jax.sharding import PartitionSpec as P

HEAD = 64
norm_eps = 1e-05
root_half = 0.7071067811865476
slope_scale = 0.3989422804014327
score_scale = 0.125
big_negative = -1e30
f32 = jnp.float32
bf16 = jnp.bfloat16
GROUP = 4 * HEAD
TILE = 512
WIDE = 1024
VMEM = 62 * 2**20
SMALL = 10**6
LARGE = 10**11
LESS = 40 * 2**20


def nn(a, b):
    return lax.dot_general(a, b, (((1,), (0,)), ((), ())), preferred_element_type=f32)


def nt(a, b):
    return lax.dot_general(a, b, (((1,), (1,)), ((), ())), preferred_element_type=f32)


def row_stats(rows):
    average = jnp.mean(rows, axis=-1, keepdims=True)
    centered = rows - average
    inverse = lax.rsqrt(jnp.mean(centered * centered, axis=-1, keepdims=True) + norm_eps)
    return centered * inverse, inverse


def gate(values):
    bell = jnp.exp(-0.5 * values * values)
    upper = 0.5 * (1.0 + lax.erf(values * root_half))
    return values * upper, upper + values * bell * slope_scale


def loop(count, body, unroll=1):
    def run(i, carry):
        body(i)
        return carry

    lax.fori_loop(0, count, run, 0, unroll=unroll)


def part(i, size):
    return pl.ds(pl.multiple_of(i * size, size), size)


def copies(pairs, sem):
    return [pltpu.make_async_copy(a, b, sem.at[i]) for i, (a, b) in enumerate(pairs)]


def chosen_tick(first, plan):
    picked = jnp.where(first, plan[0] or 0, plan[1] or 0)
    active = jnp.where(first, int(plan[0] is not None), int(plan[1] is not None)) == 1
    return active, picked


def forward_kernel(slot, plan, aliased, *refs):
    spans, norms, vectors, feat, recv, w_in, w_out, w_up, w_down = refs[:9]
    refs = refs[9 + aliased :]
    z_out, squares_out = refs[:2]
    s_x, s_a, s_qkv, s_c, s_l, s_h, s_b, s_g, s_d, s_p, layers = refs[2:13]
    (v_in, v_out, v_up, v_down, v_x, v_a, v_qkv, v_c, v_l, v_h, v_b, v_g, v_d, v_p, v_bias, v_acc, v_z,
     sem_w, sem_x, sem_o, sem_p, sem_g, sem_d) = refs[13:]
    rows, width = v_x.shape
    hidden = v_up.shape[1]
    here = pl.ds(slot * rows, rows)
    first = lax.axis_index("section") == 0
    active, picked = chosen_tick(first, plan)

    def norm(k):
        return norms[:, k * width : (k + 1) * width]

    def bias(k):
        return vectors[:, k * width : (k + 1) * width]

    @pl.when(active)
    def _():
        length = spans[picked, 0]
        causal = first

        @pl.when(first)
        def _():
            pltpu.make_async_copy(feat.at[picked, 0], v_x, sem_x.at[0]).start()

        @pl.when(jnp.logical_not(first))
        def _():
            pltpu.make_async_copy(recv, v_x, sem_x.at[0]).start()

        def column(source, target, index):
            def at(i):
                return pltpu.make_async_copy(
                    source.at[:, part(i, WIDE)], target.at[:, part(i, WIDE)], sem_w.at[index + i]
                )

            return at

        def down_copy(i):
            return pltpu.make_async_copy(
                w_down.at[part(i, WIDE)], v_down.at[part(i, WIDE)], sem_w.at[3 + 1 + hidden // WIDE + i]
            )

        in_copy, out_copy, up_copy = column(w_in, v_in, 0), column(w_out, v_out, 3), column(w_up, v_up, 4)
        for i in range(3):
            in_copy(i).start()
        out_copy(0).start()
        for i in range(hidden // WIDE):
            up_copy(i).start()
            down_copy(i).start()

        def bias_rows(i):
            at = part(i, 128)
            query = lax.broadcasted_iota(jnp.int32, (128, rows), 0) + i * 128
            key = lax.broadcasted_iota(jnp.int32, (128, rows), 1)
            open_ = (key < length) & ((key <= query) | jnp.logical_not(causal))
            v_bias[at, :] = jnp.where(open_, 0.0, big_negative)

        loop(rows // 128, bias_rows)
        pltpu.make_async_copy(recv, v_x, sem_x.at[0]).wait()

        def first_norm(i):
            at = part(i, 64)
            normed, _ = row_stats(v_x[at, :].astype(f32))
            v_a[at, :] = (normed * norm(0) + norm(1)).astype(bf16)

        loop(rows // 64, first_norm)
        outs = []

        def send(source, target, index):
            copy = pltpu.make_async_copy(source, target, sem_o.at[index])
            copy.start()
            outs.append(copy)

        send(v_x, s_x.at[here], 0)
        send(v_a, s_a.at[here], 1)
        def project(i):
            in_copy(i).wait()
            at = part(i, WIDE)
            shift = vectors[:, pl.ds(pl.multiple_of((4 + i // 2) * width, width), width)]
            tile = nn(v_a[...], v_in[:, at]) + jnp.where(i == 1, 0.0, shift)
            v_qkv[:, at] = tile.astype(bf16)

        loop(3 * width // WIDE, project)
        send(v_qkv, s_qkv.at[here], 2)
        lane = lax.broadcasted_iota(jnp.int32, (1, GROUP), 1) // HEAD
        groups = width // GROUP

        def p_copy(i):
            return pltpu.make_async_copy(
                v_p.at[i % 2], s_p.at[slot, pl.ds(i * 4, 4)], sem_p.at[i % 2]
            )

        def attend(i):
            at = part(i, GROUP)
            query = v_qkv[:, at]
            key = v_qkv[:, pl.ds(pl.multiple_of(width + i * GROUP, GROUP), GROUP)]
            value = v_qkv[:, pl.ds(pl.multiple_of(2 * width + i * GROUP, GROUP), GROUP)]

            @pl.when(i >= 2)
            def _():
                p_copy(i - 2).wait()

            half = rows // 2
            for r in range(2):
                picked_rows = slice(r * half, (r + 1) * half)
                scaled = query[picked_rows] * score_scale
                total = jnp.zeros((half, GROUP), f32)
                sums = jnp.ones((half, GROUP), f32)
                for h in range(4):
                    masked = jnp.where(lane == h, scaled, 0).astype(bf16)
                    scores = nt(masked, key) + v_bias[picked_rows, :]
                    top = jnp.max(scores, axis=-1, keepdims=True)
                    raised = jnp.exp(scores - top).astype(bf16)
                    v_p[i % 2, h, picked_rows, :] = raised
                    product = nn(raised, jnp.where(lane == h, value, 1).astype(bf16))
                    total = jnp.where(lane == h, product, total)
                    sums = jnp.where(lane == (h ^ 1), product, sums)
                inverse = 1.0 / jnp.concatenate(
                    [pltpu.roll(sums[:, k : k + 128], HEAD, 1) for k in (0, 128)], axis=1
                )
                v_l[picked_rows, at] = inverse
                v_c[picked_rows, at] = (total * inverse).astype(bf16)
            p_copy(i).start()

        loop(groups, attend)
        send(v_c, s_c.at[here], 8)
        send(v_l, s_l.at[here], 9)
        out_copy(0).wait()
        def mix(i):
            at = part(i, WIDE)
            v_acc[:, at] = nn(v_c[...], v_out[:, at]) + bias(6)

        loop(width // WIDE, mix)

        valid = lambda i, n: (lax.broadcasted_iota(jnp.int32, (n, 1), 0) + i * n < length).astype(f32)

        def square(values, mask):
            return jnp.sum((values * values * mask).reshape(-1, 8, width), axis=0)

        def second_norm(i, carry):
            at = part(i, 64)
            branch = v_acc[at, :]
            middle = v_x[at, :].astype(f32) + branch
            v_h[at, :] = middle
            normed, _ = row_stats(middle)
            v_b[at, :] = (normed * norm(2) + norm(3)).astype(bf16)
            v_acc[at, :] = jnp.broadcast_to(bias(7), (64, width))
            mask = valid(i, 64)
            return (carry[0] + square(middle, mask), carry[1] + square(branch, mask))

        nothing = jnp.zeros((8, width), f32)
        sums_one = (nothing, nothing)
        sums_one = lax.fori_loop(0, rows // 64, second_norm, sums_one)
        send(v_h, s_h.at[here], 3)
        send(v_b, s_b.at[here], 4)

        def feed(i):
            up_copy(i).wait()
            down_copy(i).wait()
            at = part(i, WIDE)
            half = rows // 2
            for r in range(2):
                rr = slice(r * half, (r + 1) * half)
                shift = vectors[:, pl.ds(pl.multiple_of(8 * width + i * WIDE, WIDE), WIDE)]
                pre = nn(v_b[rr, :], v_up[:, at]) + shift
                act, slope = gate(pre)
                act = act.astype(bf16)
                v_g[rr, at] = act
                v_d[rr, at] = slope.astype(bf16)
                v_acc[rr, :] += nn(act, v_down[at, :])
            g_copy(i).start()
            d_copy(i).start()

        def g_copy(i):
            at = part(i, WIDE)
            return pltpu.make_async_copy(v_g.at[:, at], s_g.at[here, at], sem_g.at[i])

        def d_copy(i):
            at = part(i, WIDE)
            return pltpu.make_async_copy(v_d.at[:, at], s_d.at[here, at], sem_d.at[i])

        loop(hidden // WIDE, feed)

        def finish(i, carry):
            at = part(i, 64)
            branch = v_acc[at, :]
            output = v_h[at, :] + branch
            v_z[at, :] = output.astype(bf16)
            mask = valid(i, 64)
            return (carry[0] + square(output, mask), carry[1] + square(branch, mask))

        sums_two = (nothing, nothing)
        sums_two = lax.fori_loop(0, rows // 64, finish, sums_two)
        send(v_z, z_out, 7)
        send(v_z, layers.at[0, picked, 0], 5)
        for k, value in enumerate((sums_one[0], sums_two[0], sums_one[1], sums_two[1])):
            squares_out[k] = value
        for copy in outs:
            copy.wait()
        for i in range(hidden // WIDE):
            g_copy(i).wait()
            d_copy(i).wait()
        p_copy(groups - 2).wait()
        p_copy(groups - 1).wait()

    @pl.when(jnp.logical_not(active))
    def _():
        squares_out[...] = jnp.zeros_like(squares_out)


def stash_shapes(rows, width, hidden):
    heads = width // HEAD
    return [
        jax.ShapeDtypeStruct((2 * rows, width), bf16),
        jax.ShapeDtypeStruct((2 * rows, width), bf16),
        jax.ShapeDtypeStruct((2 * rows, 3 * width), bf16),
        jax.ShapeDtypeStruct((2 * rows, width), bf16),
        jax.ShapeDtypeStruct((2 * rows, width), f32),
        jax.ShapeDtypeStruct((2 * rows, width), f32),
        jax.ShapeDtypeStruct((2 * rows, width), bf16),
        jax.ShapeDtypeStruct((2 * rows, hidden), bf16),
        jax.ShapeDtypeStruct((2 * rows, hidden), bf16),
        jax.ShapeDtypeStruct((2, heads, rows, rows), bf16),
        jax.ShapeDtypeStruct((1, 2, 1, rows, width), bf16),
    ]


def forward_call(slot, plan, spans, norms, vectors, feat, recv, weights, stash=()):
    rows, width = recv.shape
    hidden = weights[2].shape[1]
    any_ = pl.BlockSpec(memory_space=pl.ANY)
    vm = pl.BlockSpec(memory_space=pltpu.VMEM)
    shapes = stash_shapes(rows, width, hidden)
    results = pl.pallas_call(
        functools.partial(forward_kernel, slot, plan, len(stash)),
        in_specs=[pl.BlockSpec(memory_space=pltpu.SMEM), vm, vm] + [any_] * (6 + len(stash)),
        out_specs=[any_, vm] + [any_] * len(shapes),
        out_shape=[jax.ShapeDtypeStruct((rows, width), bf16), jax.ShapeDtypeStruct((4, 8, width), f32)] + shapes,
        input_output_aliases={9 + k: 2 + k for k in range(len(stash))},
        scratch_shapes=[
            pltpu.VMEM(w.shape, bf16) for w in weights
        ] + [
            pltpu.VMEM((rows, width), bf16),
            pltpu.VMEM((rows, width), bf16),
            pltpu.VMEM((rows, 3 * width), bf16),
            pltpu.VMEM((rows, width), bf16),
            pltpu.VMEM((rows, width), f32),
            pltpu.VMEM((rows, width), f32),
            pltpu.VMEM((rows, width), bf16),
            pltpu.VMEM((rows, hidden), bf16),
            pltpu.VMEM((rows, hidden), bf16),
            pltpu.VMEM((2, 4, rows, rows), bf16),
            pltpu.VMEM((rows, rows), f32),
            pltpu.VMEM((rows, width), f32),
            pltpu.VMEM((rows, width), bf16),
            pltpu.SemaphoreType.DMA((4 + 2 * hidden // WIDE,)),
            pltpu.SemaphoreType.DMA((1,)),
            pltpu.SemaphoreType.DMA((10,)),
            pltpu.SemaphoreType.DMA((2,)),
            pltpu.SemaphoreType.DMA((hidden // WIDE,)),
            pltpu.SemaphoreType.DMA((hidden // WIDE,)),
        ],
        compiler_params=pltpu.CompilerParams(vmem_limit_bytes=VMEM),
        cost_estimate=pl.CostEstimate(flops=LARGE, bytes_accessed=1, transcendentals=0),
        name="layer_forward",
    )(spans, norms, vectors, feat, recv, *weights, *stash)
    return results[0], results[1], results[2:]


BOTH, FIRST, SECOND = range(3)


def backward_kernel(slot, plan, stage, aliased, given, *refs):
    feeds, attends = stage != SECOND, stage != FIRST
    spans, norms, cot, recv, w_in, w_out, w_up, w_down = refs[:8]
    s_x, s_qkv, s_c, s_l, s_h, s_d, s_p = refs[8:15]
    if stage == SECOND:
        mid_in, middle_in = refs[15:17]
    refs = refs[15 + given + aliased :]
    smalls = refs[0]
    refs = refs[1:]
    if feeds:
        g_up, g_mid = refs[:2]
        refs = refs[2:]
    if attends:
        dx_out, g_qkv, inputs = refs[:3]
        refs = refs[3:]
    if stage == BOTH:
        g_feed = refs[0]
        refs = refs[1:]
    if stage == FIRST:
        middle_out = refs[0]
        refs = refs[1:]
    (v_in, v_out, v_up, v_down, v_x, v_dy, v_qkv, v_c, v_l, v_h, v_d, v_p, v_du, v_do, v_dc, v_dqkv, v_acc,
     v_s, v_k, v_dx, sem_w, sem_x, sem_d, sem_p, sem_o) = refs
    rows, width = v_x.shape
    hidden = v_up.shape[1]
    here = pl.ds(slot * rows, rows)
    tiles = hidden // WIDE

    first = lax.axis_index("section") == 0
    active, picked = chosen_tick(first, plan)

    def norm(k):
        return norms[:, k * width : (k + 1) * width]

    @pl.when(active)
    def _():
        length = spans[picked, 0]
        if stage != BOTH:
            smalls[...] = jnp.zeros_like(smalls)

        if feeds:

            @pl.when(jnp.logical_not(first))
            def _():
                pltpu.make_async_copy(cot.at[picked, 0], v_dy, sem_x.at[0]).start()

            @pl.when(first)
            def _():
                pltpu.make_async_copy(recv, v_dy, sem_x.at[0]).start()

        def down_copy(i):
            return pltpu.make_async_copy(
                w_down.at[part(i, WIDE)], v_down.at[part(i, WIDE)], sem_w.at[i]
            )

        def up_copy(i):
            at = part(i, WIDE)
            return pltpu.make_async_copy(w_up.at[:, at], v_up.at[:, at], sem_w.at[tiles + i])

        def d_copy(i):
            return pltpu.make_async_copy(
                s_d.at[here, part(i, WIDE)], v_d.at[i % 2], sem_d.at[i % 2]
            )

        def p_copy(i):
            return pltpu.make_async_copy(
                s_p.at[slot, pl.ds(i * 4, 4)], v_p.at[i % 2], sem_p.at[i % 2]
            )

        loads = copies(
            [
                (s_x.at[here], v_x),
                (s_qkv.at[here], v_qkv),
                (s_c.at[here], v_c),
                (s_l.at[here], v_l),
                (s_h.at[here], v_h),
                (w_out, v_out),
                (w_in, v_in),
            ],
            sem_x.at[pl.ds(1, 7)],
        )
        if feeds:
            d_copy(0).start()
            for i in range(tiles):
                down_copy(i).start()
                up_copy(i).start()
                if i == 0:
                    d_copy(1).start()
            loads[4].start()
        if stage == SECOND:
            entries = [
                pltpu.make_async_copy(mid_in.at[here], v_do, sem_o.at[0]),
                pltpu.make_async_copy(middle_in, v_acc, sem_o.at[3]),
            ]
            for copy in entries:
                copy.start()
        if attends:
            for k in (5, 1, 2, 3):
                loads[k].start()
            p_copy(0).start()
            p_copy(1).start()
            loads[6].start()
            loads[0].start()
        nothing = jnp.zeros((8, width), f32)

        def fold(values):
            return jnp.sum(values.reshape(-1, 8, width), axis=0)

        def enter(i, total):
            at = part(i, 64)
            place = lax.broadcasted_iota(jnp.int32, (64, 1), 0) + i * 64
            masked = jnp.where(place < length, v_dy[at, :].astype(f32), 0.0)
            v_dy[at, :] = masked.astype(bf16)
            v_acc[at, :] = jnp.zeros((64, width), f32)
            return total + fold(masked)

        if feeds:
            pltpu.make_async_copy(recv, v_dy, sem_x.at[0]).wait()
            total = lax.fori_loop(0, rows // 64, enter, nothing)
            smalls[7:8, :] = jnp.sum(total, axis=0, keepdims=True)
        if stage == BOTH:
            feed_copy = pltpu.make_async_copy(v_dy, g_feed.at[here], sem_o.at[4])
            feed_copy.start()

        def feed(i):
            down_copy(i).wait()
            up_copy(i).wait()
            d_copy(i).wait()
            at = part(i, WIDE)
            half = rows // 2
            for r in range(2):
                rr = slice(r * half, (r + 1) * half)
                pre = nt(v_dy[rr, :], v_down[at, :]) * v_d[i % 2, rr, :].astype(f32)
                pre = pre.astype(bf16)
                v_du[rr, at] = pre
                v_acc[rr, :] += nt(pre, v_up[:, at])
            smalls[pl.ds(8 + i, 1), :] = jnp.sum(v_du[:, at].astype(f32), axis=0, keepdims=True)
            pltpu.make_async_copy(v_du.at[:, at], g_up.at[here, at], sem_o.at[3]).start()

            @pl.when(i + 2 < tiles)
            def _():
                d_copy(i + 2).start()

        if feeds:
            loop(tiles, feed)
            loads[4].wait()

        def norm_back(source, grad, gain):
            normed, inverse = row_stats(source)
            scaled = grad * gain
            mean_one = jnp.mean(scaled, axis=-1, keepdims=True)
            mean_two = jnp.mean(scaled * normed, axis=-1, keepdims=True)
            return inverse * (scaled - mean_one - normed * mean_two), fold(grad * normed), fold(grad)

        def second_norm(i, carry):
            at = part(i, 64)
            rows_back, one, two = norm_back(v_h[at, :], v_acc[at, :], norm(2))
            middle = rows_back + v_dy[at, :].astype(f32)
            v_acc[at, :] = middle
            low = middle.astype(bf16)
            v_do[at, :] = low
            return carry[0] + one, carry[1] + two, carry[2] + fold(low.astype(f32))

        if feeds:
            sums = lax.fori_loop(0, rows // 64, second_norm, (nothing,) * 3)
            for k, value in zip((2, 3, 6), sums):
                smalls[k : k + 1, :] = jnp.sum(value, axis=0, keepdims=True)
            outs = [pltpu.make_async_copy(v_do, g_mid.at[here], sem_o.at[0])]
            if stage == FIRST:
                outs.append(pltpu.make_async_copy(v_acc, middle_out, sem_o.at[1]))
            for copy in outs:
                copy.start()
        if stage == SECOND:
            for copy in entries:
                copy.wait()
        if attends:
            loads[5].wait()
            v_dc[...] = nt(v_do[...], v_out[...]).astype(bf16)
            for k in (1, 2, 3):
                loads[k].wait()
        lane = lax.broadcasted_iota(jnp.int32, (1, GROUP), 1) // HEAD

        def attend(i):
            p_copy(i).wait()
            at = part(i, GROUP)
            key_at = pl.ds(pl.multiple_of(width + i * GROUP, GROUP), GROUP)
            value_at = pl.ds(pl.multiple_of(2 * width + i * GROUP, GROUP), GROUP)
            key = v_qkv[:, key_at]
            value = v_qkv[:, value_at]
            query = v_qkv[:, at]
            wide = v_dc[:, at].astype(f32) * v_l[:, at]
            low = wide.astype(bf16)
            dots = wide * v_c[:, at].astype(f32)
            for h in range(4):
                hs = slice(h * rows, (h + 1) * rows)
                v_k[hs, :] = jnp.where(lane == h, key, 0).astype(bf16)
                masked = jnp.where(lane == h, low, 0).astype(bf16)
                delta = jnp.sum(jnp.where(lane == h, dots, 0.0), axis=-1, keepdims=True)
                inner = nt(masked, value) - delta
                v_s[:, hs] = (v_p[i % 2, h].astype(f32) * inner).astype(bf16)
            grad_query = (nn(v_s[...], v_k[...]) * score_scale).astype(bf16)
            query_t = query.T
            low_t = low.T
            keys, values = [], []
            for h in range(4):
                hs = slice(h * HEAD, (h + 1) * HEAD)
                keys.append(nn(query_t[hs], v_s[:, h * rows : (h + 1) * rows]))
                values.append(nn(low_t[hs], v_p[i % 2, h]))
            grad_key = (jnp.concatenate(keys, axis=0) * score_scale).astype(bf16).T
            grad_value = jnp.concatenate(values, axis=0).astype(bf16).T
            v_dqkv[:, at] = grad_query
            v_dqkv[:, key_at] = grad_key
            v_dqkv[:, value_at] = grad_value
            smalls[4:5, at] = jnp.sum(grad_query.astype(f32), axis=0, keepdims=True)
            smalls[5:6, at] = jnp.sum(grad_value.astype(f32), axis=0, keepdims=True)

            @pl.when(i + 2 < width // GROUP)
            def _():
                p_copy(i + 2).start()

        if attends:
            loop(width // GROUP, attend)
            qkv_copy = pltpu.make_async_copy(v_dqkv, g_qkv.at[here], sem_o.at[1])
            qkv_copy.start()
            loads[6].wait()
            loads[0].wait()

            def enter_grad(i):
                at = part(i, TILE)
                v_h[:, at] = nt(v_dqkv[...], v_in[at, :])

            loop(width // TILE, enter_grad)

        def first_norm(i, carry):
            at = part(i, 64)
            rows_back, one, two = norm_back(v_x[at, :].astype(f32), v_h[at, :], norm(0))
            v_dx[at, :] = (rows_back + v_acc[at, :]).astype(bf16)
            return carry[0] + one, carry[1] + two

        if attends:
            sums = lax.fori_loop(0, rows // 64, first_norm, (nothing,) * 2)
            for k, value in enumerate(sums):
                smalls[k : k + 1, :] = jnp.sum(value, axis=0, keepdims=True)
            dx_copy = pltpu.make_async_copy(v_dx, dx_out, sem_o.at[2])
            dx_copy.start()
            input_copy = pltpu.make_async_copy(v_dx, inputs.at[0, picked, 0], sem_o.at[5])
            input_copy.start()
            for copy in (qkv_copy, dx_copy, input_copy):
                copy.wait()
        if stage == BOTH:
            feed_copy.wait()
        if feeds:
            for copy in outs:
                copy.wait()
            pltpu.make_async_copy(v_du, g_up.at[here], sem_o.at[3]).wait()

    @pl.when(jnp.logical_not(active))
    def _():
        smalls[...] = jnp.zeros_like(smalls)


def backward_call(slot, plan, stage, spans, norms, cot, recv, weights, stash, given, grads):
    rows, width = recv.shape
    hidden = weights[2].shape[1]
    any_ = pl.BlockSpec(memory_space=pl.ANY)
    vm = pl.BlockSpec(memory_space=pltpu.VMEM)
    shape = jax.ShapeDtypeStruct
    outs = {"smalls": shape((8 + hidden // WIDE, width), f32)}
    if stage != SECOND:
        outs["up"] = shape((2 * rows, hidden), bf16)
        outs["mid"] = shape((2 * rows, width), bf16)
    if stage != FIRST:
        outs["dx"] = shape((rows, width), bf16)
        outs["qkv"] = shape((2 * rows, 3 * width), bf16)
        outs["inputs"] = shape((1, 2, 1, rows, width), bf16)
    if stage == BOTH:
        outs["feed"] = shape((2 * rows, width), bf16)
    if stage == FIRST:
        outs["middle"] = shape((rows, width), f32)
    names = list(outs)
    kept = [name for name in names if name in grads and name not in ("smalls", "dx")]
    s_x, s_a, s_qkv, s_c, s_l, s_h, s_b, s_g, s_d, s_p, _ = stash
    results = pl.pallas_call(
        functools.partial(backward_kernel, slot, plan, stage, len(kept), len(given)),
        in_specs=[pl.BlockSpec(memory_space=pltpu.SMEM), vm] + [any_] * (13 + len(given) + len(kept)),
        out_specs=[vm] + [any_] * (len(names) - 1),
        out_shape=list(outs.values()),
        input_output_aliases={15 + len(given) + k: names.index(n) for k, n in enumerate(kept)},
        scratch_shapes=[pltpu.VMEM(w.shape, bf16) for w in weights] + [
            pltpu.VMEM((rows, width), bf16),
            pltpu.VMEM((rows, width), bf16),
            pltpu.VMEM((rows, 3 * width), bf16),
            pltpu.VMEM((rows, width), bf16),
            pltpu.VMEM((rows, width), f32),
            pltpu.VMEM((rows, width), f32),
            pltpu.VMEM((2, rows, WIDE), bf16),
            pltpu.VMEM((2, 4, rows, rows), bf16),
            pltpu.VMEM((rows, hidden), bf16),
            pltpu.VMEM((rows, width), bf16),
            pltpu.VMEM((rows, width), bf16),
            pltpu.VMEM((rows, 3 * width), bf16),
            pltpu.VMEM((rows, width), f32),
            pltpu.VMEM((rows, 4 * rows), bf16),
            pltpu.VMEM((4 * rows, GROUP), bf16),
            pltpu.VMEM((rows, width), bf16),
            pltpu.SemaphoreType.DMA((2 * hidden // WIDE,)),
            pltpu.SemaphoreType.DMA((8,)),
            pltpu.SemaphoreType.DMA((2,)),
            pltpu.SemaphoreType.DMA((2,)),
            pltpu.SemaphoreType.DMA((6,)),
        ],
        compiler_params=pltpu.CompilerParams(vmem_limit_bytes=VMEM),
        cost_estimate=pl.CostEstimate(flops=LARGE, bytes_accessed=1, transcendentals=0),
        name="layer_backward",
    )(
        spans, norms, cot, recv, *weights, s_x, s_qkv, s_c, s_l, s_h, s_d, s_p, *given,
        *[grads[name] for name in kept],
    )
    return {**grads, **dict(zip(names, results))}


def turn_kernel(blocks, *refs):
    count = len(blocks)
    for k, block in enumerate(blocks):
        source, target = refs[k], refs[count + k]

        @pl.when((pl.program_id(0) == k) if k + 1 < count else (pl.program_id(0) >= k))
        def _(source=source, target=target, block=block):
            flat = source[...].T
            pairs = flat.shape[0] // (2 * block)
            for core in range(2):

                @pl.when(lax.axis_index("dp") % 2 == core)
                def _(core=core):
                    for j in range(pairs):
                        at = slice(j * block, (j + 1) * block)
                        other = (2 * j + 1 - core) * block
                        own = (2 * j + core) * block
                        target[0, at, :] = flat[other : other + block]
                        target[1, at, :] = flat[own : own + block]


def turn_call(sources):
    rows = sources[0].shape[0]
    count = len(sources)
    size = lax.axis_size("dp")
    steps = count - 1 + sources[-1].shape[1] // WIDE

    def last(i):
        return jnp.maximum(i - (count - 1), 0)

    ins = [pl.BlockSpec((rows, WIDE), lambda i: (0, 0))] * (count - 1)
    ins.append(pl.BlockSpec((rows, WIDE), lambda i: (0, last(i))))
    outs = [pl.BlockSpec((2, WIDE // 2, rows), lambda i: (0, 0, 0))] * (count - 1)
    outs.append(pl.BlockSpec((2, WIDE // 2, rows), lambda i: (0, last(i), 0)))
    return pl.pallas_call(
        functools.partial(turn_kernel, [s.shape[1] // size for s in sources]),
        grid=(steps,),
        in_specs=ins,
        out_specs=outs,
        out_shape=[jax.ShapeDtypeStruct((2, s.shape[1] // 2, rows), bf16) for s in sources],
        compiler_params=pltpu.CompilerParams(vmem_limit_bytes=VMEM),
        cost_estimate=pl.CostEstimate(flops=1, bytes_accessed=1, transcendentals=0),
        name="turn",
    )(*sources)


def weight_kernel(widths, half, left, right, *rest):
    late, outs = rest[: -len(widths)], rest[-len(widths) :]
    if late:
        rows = late[0].shape[0]
        second = jnp.where(lax.axis_index("section") == 0, late[0][...], right[rows:, :])
        total = nn(left[0, :, :rows], right[:rows, :]) + nn(left[0, :, rows:], second)
    else:
        total = nn(left[0], right[...])
    total = total.astype(bf16)
    at = 0
    for width, out in zip(widths, outs):
        step, offset = divmod(at, right.shape[1])
        if len(widths) == 1:
            out[...] = total
        else:

            @pl.when(pl.program_id(1) == step)
            def _(out=out, cut=slice(offset, offset + width)):
                out[...] = total[:, cut]

        at += width


def weight_call(left, right, start, widths, half, late=None):
    _, height, rows = left.shape
    columns = sum(widths)
    tall = min(height, 512)
    wide = min(columns, WIDE)
    specs = [
        pl.BlockSpec((1, tall, rows), lambda i, j: (half, i, 0)),
        pl.BlockSpec((rows, wide), lambda i, j: (0, start // wide + j)),
    ]
    operands = (left, right)
    if late is not None:
        specs.append(pl.BlockSpec((rows // 2, wide), lambda i, j: (0, j)))
        operands += (late,)

    def out(width):
        if width > wide:
            return pl.BlockSpec((tall, wide), lambda i, j: (i, j))
        return pl.BlockSpec((tall, width), lambda i, j: (i, 0))

    return pl.pallas_call(
        functools.partial(weight_kernel, widths, half),
        grid=(height // tall, columns // wide),
        in_specs=specs,
        out_specs=[out(width) for width in widths],
        out_shape=[jax.ShapeDtypeStruct((height, width), bf16) for width in widths],
        compiler_params=pltpu.CompilerParams(vmem_limit_bytes=VMEM),
        cost_estimate=pl.CostEstimate(flops=1, bytes_accessed=1, transcendentals=0),
        name="weight_product",
    )(*operands)


def sum_kernel(layout, lefts, fixed, free, place, *refs):
    count = sum(len(arrays) for arrays in layout)
    sources = iter(refs[:count])
    terms = [[next(sources) for _ in arrays] for arrays in layout]
    out, held, total, sem, out_sem = refs[-5:]
    me = lax.axis_index("dp")
    cells = list(itertools.product(range(2), repeat=len(free)))
    loads, slot = [], 0
    for cell in cells:
        loads.append([])
        for arrays, left, widths in zip(terms, lefts, layout):
            index = []
            for bit in left:
                if bit in free:
                    index.append(cell[free.index(bit)])
                else:
                    own = (me >> bit) & 1
                    index.append(own if fixed[bit] else 1 - own)
            at = 0
            for ref, (start, width) in zip(arrays, widths):
                copy = pltpu.make_async_copy(
                    ref.at[(*index, slice(None), pl.ds(start, width))],
                    held.at[slot, :, pl.ds(at, width)],
                    sem.at[len(loads[-1]), len(loads) - 1],
                )
                copy.start()
                loads[-1].append(copy)
                at += width
            slot += 1
    stores = []
    for k, cell in enumerate(cells):
        for copy in loads[k]:
            copy.wait()
        value = added([held[k * len(terms) + j] for j in range(len(terms))])
        total[k] = value.astype(total.dtype)
        stores.append(pltpu.make_async_copy(total.at[k], place(out, cell), out_sem.at[k]))
        stores[-1].start()
    for copy in stores:
        copy.wait()


def sum_call(terms, fixed, kind, into=None, start=0):
    rows = terms[0][0][0][0].shape[-2]
    layout = [[(at, width) for _, at, width in arrays] for arrays, _ in terms]
    lefts = [left for _, left in terms]
    columns = sum(width for _, width in layout[0])
    free = [bit for bit in lefts[0] if bit not in fixed]
    operands = [array for arrays, _ in terms for array, _, _ in arrays]
    cells = 2 ** len(free)
    aliases = {}
    wide = 0
    if into is None:
        shape = jax.ShapeDtypeStruct((2,) * len(free) + (rows, columns), kind)
    else:
        wide, into = into
        shape = jax.ShapeDtypeStruct((1, rows, wide), kind)
        if into is not None:
            aliases = {len(operands): 0}
            operands.append(into)

    given = len(operands)

    def place(out, cell):
        if wide:
            return out.at[0, :, pl.ds(start, columns)]
        return out.at[cell] if cell else out

    def kernel(*refs):
        refs = refs[: given - len(aliases)] + refs[given:]
        sum_kernel(layout, lefts, fixed, free, place, *refs)

    any_ = pl.BlockSpec(memory_space=pl.ANY)
    return pl.pallas_call(
        kernel,
        in_specs=[any_] * len(operands),
        out_specs=any_,
        out_shape=shape,
        input_output_aliases=aliases,
        scratch_shapes=[
            pltpu.VMEM((cells * len(terms), rows, columns), terms[0][0][0][0].dtype),
            pltpu.VMEM((cells, rows, columns), kind),
            pltpu.SemaphoreType.DMA((max(sum(len(arrays) for arrays, _ in terms), 1), cells)),
            pltpu.SemaphoreType.DMA((cells,)),
        ],
        compiler_params=pltpu.CompilerParams(vmem_limit_bytes=VMEM),
        cost_estimate=pl.CostEstimate(flops=SMALL, bytes_accessed=1, transcendentals=0),
        name="sum_terms",
    )(*operands)


highest = lax.Precision.HIGHEST


def added(terms):
    total = terms[0].astype(f32)
    for term in terms[1:]:
        total = total + term.astype(f32)
    return total


class Line:
    def __init__(self):
        self.last = None

    def after(self, values):
        if self.last is not None:
            values = lax.optimization_barrier(tuple(values) + (self.last,))[:-1]
        return list(values)

    def done(self, value):
        self.last = value


class Exchange:
    def __init__(self, line, terms, left, order):
        self.line = line
        self.terms = [(arrays, sorted(left, reverse=True)) for arrays in terms]
        self.fixed = {}
        self.order = list(order)
        self.kind = terms[0][0][0].dtype

    def total(self, fixed, kind, **where):
        values = iter(self.line.after([array for arrays, _ in self.terms for array, _, _ in arrays]))
        self.terms = [
            ([(next(values), at, width) for _, at, width in arrays], left)
            for arrays, left in self.terms
        ]
        total = sum_call(self.terms, fixed, kind, **where)
        self.line.done(total)
        return total

    def step(self):
        bit = self.order.pop(0)
        theirs = self.total({**self.fixed, bit: False}, self.kind)
        self.fixed[bit] = True
        left = [k for k in self.terms[0][1] if k not in self.fixed]
        self.terms.append((whole(crossed(theirs, bit)), left))

    def cut(self, widths):
        parts = []
        low = 0
        for width in widths:
            high = low + width
            terms = []
            for arrays, left in self.terms:
                chosen, at = [], 0
                for array, start, columns in arrays:
                    a, b = max(low, at), min(high, at + columns)
                    if a < b:
                        chosen.append((array, start + a - at, b - a))
                    at += columns
                terms.append((chosen, left))
            part_ = Exchange(self.line, [terms[0][0]], (), self.order)
            part_.terms = terms
            part_.fixed = dict(self.fixed)
            parts.append(part_)
            low = high
        return parts

    def finish(self, **where):
        while self.order:
            self.step()
        return self.total(self.fixed, f32, **where)


def crossed(value, bit):
    return lax.ppermute(value, "dp", [(i, i ^ (1 << bit)) for i in range(lax.axis_size("dp"))])


def whole(array):
    return [(array, 0, array.shape[-1])]


def whole(array):
    return [(array, 0, array.shape[-1])]


class WeightSum(Exchange):
    def __init__(self, line, left, right, start, widths, order, late=None):
        size = lax.axis_size("dp")
        bits = size.bit_length() - 1
        shape = [2] * (bits - 1) + [2 * left.shape[1] // size, -1]
        left, right = line.after((left, right))
        theirs = weight_call(left, right, start, widths, 0, late)
        line.done(theirs[-1])
        received = [whole(crossed(array, 0).reshape(shape)) for array in theirs]
        self.product = (left, right, start, [sum(widths)], 1, late)
        self.shape = shape
        super().__init__(line, (sum(received, []),), range(1, bits), order)

    def own(self):
        left, right = self.line.after(self.product[:2])
        (mine,) = weight_call(left, right, *self.product[2:])
        self.line.done(mine)
        self.terms.append((whole(mine.reshape(self.shape)), self.terms[0][1]))
        return self


def shards(
    features,
    cotangent,
    lengths,
    codebook_index,
    attention_in,
    attention_out,
    feed_up,
    feed_down,
    vectors,
    adaptive_weight,
    codebook_table,
):
    is_first = lax.axis_index("section") == 0
    adaptive = jnp.where(is_first, 0.0, 1.0)
    rows, width = features.shape[2:]
    hidden = feed_up.shape[2]
    size = lax.axis_size("dp")
    bits = size.bit_length() - 1
    weights = (attention_in[0], attention_out[0], feed_up[0], feed_down[0])

    def send(value, to):
        return lax.ppermute(value, "section", [(1 - to, to)])

    nowhere = jnp.zeros((rows, width), bf16)

    def forward(slot, plan, norms, recv, stash=()):
        return forward_call(slot, plan, lengths, norms, vectors, features, recv, weights, stash)

    def backward(slot, plan, stage, norms, recv, stash, grads, given=()):
        return backward_call(
            slot, plan, stage, lengths, norms, cotangent, recv, weights, stash, given, grads
        )

    z_one, squares_one, stash = forward(0, (0, None), vectors, nowhere)
    received_one = send(z_one, 1)
    table, z_one = lax.optimization_barrier((codebook_table, z_one))
    condition_table = jnp.dot(table, adaptive_weight, preferred_element_type=f32)
    one_hot = (
        codebook_index[:, 0][:, None]
        == jnp.arange(codebook_table.shape[0], dtype=jnp.int32)[None, :]
    ).astype(f32)
    norms = vectors[:, : 4 * width] + adaptive * jnp.dot(
        one_hot, condition_table, precision=highest
    )
    norms_one, norms_two = norms[:1], norms[1:]
    z_two, squares_two, stash = forward(1, (1, 0), norms_one, received_one, stash)
    received_two = send(z_two, 1)
    grads = backward(1, (None, 0), BOTH, norms_one, nowhere, stash, {})
    smalls_one = grads["smalls"]
    back_one = send(grads["dx"], 0)
    z_three, squares_three, stash = forward(0, (None, 1), norms_two, received_two, stash)
    grads = backward(0, (0, 1), BOTH, norms_two, back_one, stash, grads)
    smalls_two = grads["smalls"]
    back_two = send(grads["dx"], 0)

    s_x, s_a, s_qkv, s_c, s_l, s_h, s_b, s_g, s_d, s_p, layer_outputs = stash
    side_first = list(range(1, bits))
    line_first = side_first[1:] + side_first[:1]
    line = Line()
    line.done(smalls_two)
    squares = jnp.sum(squares_one + squares_two + squares_three, axis=(1, 2))
    counted = jnp.sum(lengths).astype(f32)
    (totals,) = line.after((jnp.concatenate([squares, counted[None], jnp.zeros((123,), f32)]),))
    for bit in range(bits):
        totals = totals + crossed(totals, bit)
    t_a, t_b, t_c, t_g = turn_call(line.after((s_a, s_b, s_c, s_g)))
    line.done(t_a)
    (totals,) = line.after((totals,))
    line.done(totals)
    down = WeightSum(line, t_g, grads["feed"], 0, [width], side_first, back_two).own()
    down.step()
    (back_two,) = line.after((back_two,))
    grads = backward(1, (1, None), FIRST, vectors, back_two, stash, grads)
    smalls_three = grads["smalls"]
    line.done(smalls_three)
    up = WeightSum(line, t_b, grads["up"], 0, [WIDE] * (hidden // WIDE), side_first).own()
    up.step()
    down.step()
    out = WeightSum(line, t_c, grads["mid"], 0, [width], side_first).own()
    (middle,) = line.after((grads["middle"],))
    grads = backward(
        1, (1, None), SECOND, vectors, back_two, stash, grads, (grads["mid"], middle)
    )
    smalls_four = grads["smalls"]
    line.done(smalls_four)
    g_qkv, input_grads = grads["qkv"], grads["inputs"]
    down.step()
    into_one = WeightSum(line, t_a, g_qkv, 0, [width] * 3, side_first).own()

    smalls = smalls_one + smalls_two + smalls_three + smalls_four
    table_grad = one_hot[0][:, None] * smalls_one[:4].reshape(1, -1) + one_hot[1][:, None] * (
        smalls_two[:4].reshape(1, -1) * adaptive
    )
    codes = table_grad.shape[0]
    share = table_grad.shape[1] // (2 * size)
    table_blocks = table_grad.reshape(codes, 2, size, share).transpose(2, 1, 0, 3)
    packed = jnp.concatenate([smalls.reshape(size, -1), table_blocks.reshape(size, -1)], axis=1)
    count = packed.shape[1]
    block = width // size
    packed = jnp.pad(packed.reshape(size, block, -1), ((0, 0), (0, 0), (0, 128 - count // block)))
    packed = packed.astype(bf16).reshape([2] * bits + [block, 128])
    core = lax.axis_index("dp") & 1
    (other, own) = [
        lax.dynamic_index_in_dim(packed, which, bits - 1, keepdims=False)
        for which in (1 - core, core)
    ]
    other = crossed(other, 0)
    into_one, into_two = into_one.cut([2 * width, width])
    up_one, up_two = up.cut([hidden // 2] * 2)
    into_two.terms = [
        (arrays + whole(extra), left)
        for (arrays, left), extra in zip(into_two.terms, (other, own))
    ]
    into_one.step()
    up_one.step()
    up_two.step()
    into_two.step()
    out.step()
    down = down.finish(into=(width, None))
    up_one.step()
    into_one.step()
    up_two.step()
    into_two.step()
    up = up_one.finish(into=(hidden, None))
    into_one.step()
    out.step()
    up = up_two.finish(into=(hidden, up), start=hidden // 2)
    into_two.step()
    into = into_one.finish(into=(3 * width, None))
    out.step()
    last = into_two.finish()
    out = out.finish(into=(width, None))
    into = lax.dynamic_update_slice(into, last[None, :, :width], (0, 0, 2 * width))
    small_sum = last[:, width : width + count // block].reshape(-1)
    vector_share = small_sum[: smalls.size // size]
    table_share = small_sum[smalls.size // size :].reshape(2, codes, share)
    table_own = jnp.where(is_first, send(table_share[0], 0), table_share[1])
    grad_adaptive = lax.dot_general(
        codebook_table.astype(f32),
        table_own,
        (((0,), (0,)), ((), ())),
        precision=highest,
        preferred_element_type=f32,
    )
    residual_rms = jnp.sqrt(totals[:4] / (totals[4] * width))[None]

    return (
        layer_outputs,
        input_grads,
        into,
        out,
        up,
        down,
        vector_share[None],
        grad_adaptive,
        residual_rms,
    )


def solution(mesh):
    placed = (
        P(None, "dp", None, None),
        P(None, "dp", None, None),
        P(None, "dp"),
        P(None, "dp"),
        P("section", None, None),
        P("section", None, None),
        P("section", None, None),
        P("section", None, None),
        P("section", None),
        P(),
        P(),
    )
    return jax.shard_map(
        shards,
        mesh=mesh,
        in_specs=placed,
        out_specs=(
            P("section", None, "dp", None, None),
            P("section", None, "dp", None, None),
            P("section", "dp", None),
            P("section", "dp", None),
            P("section", "dp", None),
            P("section", "dp", None),
            P("section", "dp"),
            P(None, ("section", "dp")),
            P("section", None),
        ),
        check_vma=False,
    )
```

```python
import functools
import itertools

import jax
import jax.numpy as jnp
from jax import lax
from jax.experimental import pallas as pl
from jax.experimental.pallas import tpu as pltpu
from jax.sharding import PartitionSpec as P

HEAD = 64
norm_eps = 1e-05
root_half = 0.7071067811865476
slope_scale = 0.3989422804014327
score_scale = 0.125
big_negative = -1e30
f32 = jnp.float32
bf16 = jnp.bfloat16
GROUP = 4 * HEAD
TILE = 512
WIDE = 1024
BROAD = 2048
VMEM = 62 * 2**20
SMALL = 10**6
LARGE = 10**11
LESS = 40 * 2**20


def nn(a, b):
    return lax.dot_general(a, b, (((1,), (0,)), ((), ())), preferred_element_type=f32)


def nt(a, b):
    return lax.dot_general(a, b, (((1,), (1,)), ((), ())), preferred_element_type=f32)


def row_stats(rows):
    average = jnp.mean(rows, axis=-1, keepdims=True)
    centered = rows - average
    inverse = lax.rsqrt(jnp.mean(centered * centered, axis=-1, keepdims=True) + norm_eps)
    return centered * inverse, inverse


def gate(values):
    bell = jnp.exp(-0.5 * values * values)
    upper = 0.5 * (1.0 + lax.erf(values * root_half))
    return values * upper, upper + values * bell * slope_scale


def loop(count, body, unroll=1):
    def run(i, carry):
        body(i)
        return carry

    lax.fori_loop(0, count, run, 0, unroll=unroll)


def part(i, size):
    return pl.ds(pl.multiple_of(i * size, size), size)


def copies(pairs, sem):
    return [pltpu.make_async_copy(a, b, sem.at[i]) for i, (a, b) in enumerate(pairs)]


def chosen_tick(first, plan):
    picked = jnp.where(first, plan[0] or 0, plan[1] or 0)
    active = jnp.where(first, int(plan[0] is not None), int(plan[1] is not None)) == 1
    return active, picked


def forward_kernel(slot, plan, aliased, *refs):
    spans, norms, vectors, feat, recv, w_in, w_out, w_up, w_down = refs[:9]
    refs = refs[9 + aliased :]
    z_out, squares_out = refs[:2]
    s_x, s_a, s_qkv, s_c, s_l, s_h, s_b, s_g, s_d, s_p, layers = refs[2:13]
    (v_in, v_out, v_up, v_down, v_x, v_a, v_qkv, v_c, v_l, v_h, v_b, v_g, v_d, v_p, v_bias, v_acc, v_z,
     sem_w, sem_x, sem_o, sem_p, sem_g, sem_d) = refs[13:]
    rows, width = v_x.shape
    hidden = v_up.shape[1]
    here = pl.ds(slot * rows, rows)
    first = lax.axis_index("section") == 0
    active, picked = chosen_tick(first, plan)

    def norm(k):
        return norms[:, k * width : (k + 1) * width]

    def bias(k):
        return vectors[:, k * width : (k + 1) * width]

    @pl.when(active)
    def _():
        length = spans[picked, 0]
        causal = first

        @pl.when(first)
        def _():
            pltpu.make_async_copy(feat.at[picked, 0], v_x, sem_x.at[0]).start()

        @pl.when(jnp.logical_not(first))
        def _():
            pltpu.make_async_copy(recv, v_x, sem_x.at[0]).start()

        def column(source, target, index, size):
            def at(i):
                return pltpu.make_async_copy(
                    source.at[:, part(i, size)], target.at[:, part(i, size)], sem_w.at[index + i]
                )

            return at

        def down_copy(i):
            return pltpu.make_async_copy(
                w_down.at[part(i, BROAD)], v_down.at[part(i, BROAD)], sem_w.at[3 + 1 + hidden // BROAD + i]
            )

        in_copy = column(w_in, v_in, 0, WIDE)
        out_copy = column(w_out, v_out, 3, WIDE)
        up_copy = column(w_up, v_up, 4, BROAD)
        for i in range(3):
            in_copy(i).start()

        def bias_rows(i):
            at = part(i, 128)
            query = lax.broadcasted_iota(jnp.int32, (128, rows), 0) + i * 128
            key = lax.broadcasted_iota(jnp.int32, (128, rows), 1)
            open_ = (key < length) & ((key <= query) | jnp.logical_not(causal))
            v_bias[at, :] = jnp.where(open_, 0.0, big_negative)

        loop(rows // 128, bias_rows)
        pltpu.make_async_copy(recv, v_x, sem_x.at[0]).wait()

        def first_norm(i):
            at = part(i, 64)
            normed, _ = row_stats(v_x[at, :].astype(f32))
            v_a[at, :] = (normed * norm(0) + norm(1)).astype(bf16)

        loop(rows // 64, first_norm, 2)
        outs = []

        def send(source, target, index):
            copy = pltpu.make_async_copy(source, target, sem_o.at[index])
            copy.start()
            outs.append(copy)

        send(v_x, s_x.at[here], 0)
        send(v_a, s_a.at[here], 1)
        def project(i):
            in_copy(i).wait()
            at = part(i, WIDE)
            shift = vectors[:, pl.ds(pl.multiple_of((4 + i // 2) * width, width), width)]
            tile = nn(v_a[...], v_in[:, at]) + jnp.where(i == 1, 0.0, shift)
            v_qkv[:, at] = tile.astype(bf16)

        loop(3 * width // WIDE, project)
        out_copy(0).start()
        for i in range(hidden // BROAD):
            up_copy(i).start()
            down_copy(i).start()
        send(v_qkv, s_qkv.at[here], 2)
        lane = lax.broadcasted_iota(jnp.int32, (1, GROUP), 1) // HEAD
        groups = width // GROUP

        def p_copy(i):
            return pltpu.make_async_copy(
                v_p.at[i % 2], s_p.at[slot, pl.ds(i * 4, 4)], sem_p.at[i % 2]
            )

        def attend(i):
            at = part(i, GROUP)
            query = v_qkv[:, at]
            key = v_qkv[:, pl.ds(pl.multiple_of(width + i * GROUP, GROUP), GROUP)]
            value = v_qkv[:, pl.ds(pl.multiple_of(2 * width + i * GROUP, GROUP), GROUP)]

            @pl.when(i >= 2)
            def _():
                p_copy(i - 2).wait()

            half = rows // 2

            def rows_part(r, keys):
                picked_rows = slice(r * half, (r + 1) * half)
                scaled = query[picked_rows] * score_scale
                total = jnp.zeros((half, GROUP), f32)
                sums = jnp.ones((half, GROUP), f32)
                for h in range(4):
                    masked = jnp.where(lane == h, scaled, 0).astype(bf16)
                    scores = nt(masked, key[:keys]) + v_bias[picked_rows, :keys]
                    top = jnp.max(scores, axis=-1, keepdims=True)
                    raised = jnp.exp(scores - top).astype(bf16)
                    v_p[i % 2, h, picked_rows, :keys] = raised
                    if keys < rows:
                        v_p[i % 2, h, picked_rows, keys:] = jnp.zeros((half, rows - keys), bf16)
                    product = nn(raised, jnp.where(lane == h, value[:keys], 1).astype(bf16))
                    total = jnp.where(lane == h, product, total)
                    sums = jnp.where(lane == (h ^ 1), product, sums)
                inverse = 1.0 / jnp.concatenate(
                    [pltpu.roll(sums[:, k : k + 128], HEAD, 1) for k in (0, 128)], axis=1
                )
                v_l[picked_rows, at] = inverse
                v_c[picked_rows, at] = (total * inverse).astype(bf16)

            @pl.when(causal)
            def _():
                rows_part(0, half)
                rows_part(1, rows)

            @pl.when(jnp.logical_not(causal))
            def _():
                rows_part(0, rows)
                rows_part(1, rows)

            p_copy(i).start()

        loop(groups, attend)
        send(v_c, s_c.at[here], 8)
        send(v_l, s_l.at[here], 9)
        out_copy(0).wait()
        def mix(i):
            at = part(i, WIDE)
            v_acc[:, at] = nn(v_c[...], v_out[:, at]) + bias(6)

        loop(width // WIDE, mix)

        valid = lambda i, n: (lax.broadcasted_iota(jnp.int32, (n, 1), 0) + i * n < length).astype(f32)

        def square(values, mask):
            return jnp.sum((values * values * mask).reshape(-1, 8, width), axis=0)

        def second_norm(i, carry):
            at = part(i, 64)
            branch = v_acc[at, :]
            middle = v_x[at, :].astype(f32) + branch
            v_h[at, :] = middle
            normed, _ = row_stats(middle)
            v_b[at, :] = (normed * norm(2) + norm(3)).astype(bf16)
            v_acc[at, :] = jnp.broadcast_to(bias(7), (64, width))
            mask = valid(i, 64)
            return (carry[0] + square(middle, mask), carry[1] + square(branch, mask))

        nothing = jnp.zeros((8, width), f32)
        sums_one = (nothing, nothing)
        sums_one = lax.fori_loop(0, rows // 64, second_norm, sums_one, unroll=2)
        send(v_h, s_h.at[here], 3)
        send(v_b, s_b.at[here], 4)

        def feed(i):
            up_copy(i).wait()
            down_copy(i).wait()
            at = part(i, BROAD)
            shift = vectors[:, pl.ds(pl.multiple_of(8 * width + i * BROAD, BROAD), BROAD)]
            act, slope = gate(nn(v_b[...], v_up[:, at]) + shift)
            act = act.astype(bf16)
            v_g[:, at] = act
            v_d[:, at] = slope.astype(bf16)
            v_acc[...] += nn(act, v_down[at, :])
            g_copy(i).start()
            d_copy(i).start()

        def g_copy(i):
            at = part(i, BROAD)
            return pltpu.make_async_copy(v_g.at[:, at], s_g.at[here, at], sem_g.at[i])

        def d_copy(i):
            at = part(i, BROAD)
            return pltpu.make_async_copy(v_d.at[:, at], s_d.at[here, at], sem_d.at[i])

        loop(hidden // BROAD, feed)

        def finish(i, carry):
            at = part(i, 64)
            branch = v_acc[at, :]
            output = v_h[at, :] + branch
            v_z[at, :] = output.astype(bf16)
            mask = valid(i, 64)
            return (carry[0] + square(output, mask), carry[1] + square(branch, mask))

        sums_two = (nothing, nothing)
        sums_two = lax.fori_loop(0, rows // 64, finish, sums_two, unroll=2)
        send(v_z, z_out, 7)
        send(v_z, layers.at[0, picked, 0], 5)
        for k, value in enumerate((sums_one[0], sums_two[0], sums_one[1], sums_two[1])):
            squares_out[k] = value
        for copy in outs:
            copy.wait()
        for i in range(hidden // BROAD):
            g_copy(i).wait()
            d_copy(i).wait()
        p_copy(groups - 2).wait()
        p_copy(groups - 1).wait()

    @pl.when(jnp.logical_not(active))
    def _():
        squares_out[...] = jnp.zeros_like(squares_out)


def stash_shapes(rows, width, hidden):
    heads = width // HEAD
    return [
        jax.ShapeDtypeStruct((2 * rows, width), bf16),
        jax.ShapeDtypeStruct((2 * rows, width), bf16),
        jax.ShapeDtypeStruct((2 * rows, 3 * width), bf16),
        jax.ShapeDtypeStruct((2 * rows, width), bf16),
        jax.ShapeDtypeStruct((2 * rows, width), f32),
        jax.ShapeDtypeStruct((2 * rows, width), f32),
        jax.ShapeDtypeStruct((2 * rows, width), bf16),
        jax.ShapeDtypeStruct((2 * rows, hidden), bf16),
        jax.ShapeDtypeStruct((2 * rows, hidden), bf16),
        jax.ShapeDtypeStruct((2, heads, rows, rows), bf16),
        jax.ShapeDtypeStruct((1, 2, 1, rows, width), bf16),
    ]


def forward_call(slot, plan, spans, norms, vectors, feat, recv, weights, stash=()):
    rows, width = recv.shape
    hidden = weights[2].shape[1]
    any_ = pl.BlockSpec(memory_space=pl.ANY)
    vm = pl.BlockSpec(memory_space=pltpu.VMEM)
    shapes = stash_shapes(rows, width, hidden)
    results = pl.pallas_call(
        functools.partial(forward_kernel, slot, plan, len(stash)),
        in_specs=[pl.BlockSpec(memory_space=pltpu.SMEM), vm, vm] + [any_] * (6 + len(stash)),
        out_specs=[any_, vm] + [any_] * len(shapes),
        out_shape=[jax.ShapeDtypeStruct((rows, width), bf16), jax.ShapeDtypeStruct((4, 8, width), f32)] + shapes,
        input_output_aliases={9 + k: 2 + k for k in range(len(stash))},
        scratch_shapes=[
            pltpu.VMEM(w.shape, bf16) for w in weights
        ] + [
            pltpu.VMEM((rows, width), bf16),
            pltpu.VMEM((rows, width), bf16),
            pltpu.VMEM((rows, 3 * width), bf16),
            pltpu.VMEM((rows, width), bf16),
            pltpu.VMEM((rows, width), f32),
            pltpu.VMEM((rows, width), f32),
            pltpu.VMEM((rows, width), bf16),
            pltpu.VMEM((rows, hidden), bf16),
            pltpu.VMEM((rows, hidden), bf16),
            pltpu.VMEM((2, 4, rows, rows), bf16),
            pltpu.VMEM((rows, rows), f32),
            pltpu.VMEM((rows, width), f32),
            pltpu.VMEM((rows, width), bf16),
            pltpu.SemaphoreType.DMA((4 + 2 * hidden // WIDE,)),
            pltpu.SemaphoreType.DMA((1,)),
            pltpu.SemaphoreType.DMA((10,)),
            pltpu.SemaphoreType.DMA((2,)),
            pltpu.SemaphoreType.DMA((hidden // WIDE,)),
            pltpu.SemaphoreType.DMA((hidden // WIDE,)),
        ],
        compiler_params=pltpu.CompilerParams(vmem_limit_bytes=VMEM),
        cost_estimate=pl.CostEstimate(flops=LARGE, bytes_accessed=1, transcendentals=0),
        name="layer_forward",
    )(spans, norms, vectors, feat, recv, *weights, *stash)
    return results[0], results[1], results[2:]


BOTH, FIRST, SECOND = range(3)


def backward_kernel(slot, plan, stage, aliased, given, *refs):
    feeds, attends = stage != SECOND, stage != FIRST
    spans, norms, cot, recv, w_in, w_out, w_up, w_down = refs[:8]
    s_x, s_qkv, s_c, s_l, s_h, s_d, s_p = refs[8:15]
    if stage == SECOND:
        mid_in, middle_in = refs[15:17]
    refs = refs[15 + given + aliased :]
    smalls = refs[0]
    refs = refs[1:]
    if feeds:
        g_up, g_mid = refs[:2]
        refs = refs[2:]
    if attends:
        dx_out, g_qkv, inputs = refs[:3]
        refs = refs[3:]
    if stage == BOTH:
        g_feed = refs[0]
        refs = refs[1:]
    if stage == FIRST:
        middle_out = refs[0]
        refs = refs[1:]
    (v_in, v_out, v_up, v_down, v_x, v_dy, v_qkv, v_c, v_l, v_h, v_d, v_p, v_du, v_do, v_dc, v_dqkv, v_acc,
     v_s, v_k, v_dx, sem_w, sem_x, sem_d, sem_p, sem_o) = refs
    rows, width = v_x.shape
    hidden = v_up.shape[1]
    here = pl.ds(slot * rows, rows)
    tiles = hidden // WIDE

    first = lax.axis_index("section") == 0
    active, picked = chosen_tick(first, plan)

    def norm(k):
        return norms[:, k * width : (k + 1) * width]

    @pl.when(active)
    def _():
        length = spans[picked, 0]
        if stage != BOTH:
            smalls[...] = jnp.zeros_like(smalls)

        if feeds:

            @pl.when(jnp.logical_not(first))
            def _():
                pltpu.make_async_copy(cot.at[picked, 0], v_dy, sem_x.at[0]).start()

            @pl.when(first)
            def _():
                pltpu.make_async_copy(recv, v_dy, sem_x.at[0]).start()

        def down_copy(i):
            return pltpu.make_async_copy(
                w_down.at[part(i, WIDE)], v_down.at[part(i, WIDE)], sem_w.at[i]
            )

        def up_copy(i):
            at = part(i, WIDE)
            return pltpu.make_async_copy(w_up.at[:, at], v_up.at[:, at], sem_w.at[tiles + i])

        def d_copy(i):
            return pltpu.make_async_copy(
                s_d.at[here, part(i, WIDE)], v_d.at[i % 2], sem_d.at[i % 2]
            )

        def p_copy(i):
            return pltpu.make_async_copy(
                s_p.at[slot, pl.ds(i * 4, 4)], v_p.at[i % 2], sem_p.at[i % 2]
            )

        loads = copies(
            [
                (s_x.at[here], v_x),
                (s_qkv.at[here], v_qkv),
                (s_c.at[here], v_c),
                (s_l.at[here], v_l),
                (s_h.at[here], v_h),
                (w_out, v_out),
                (w_in, v_in),
            ],
            sem_x.at[pl.ds(1, 7)],
        )
        if feeds:
            d_copy(0).start()
            for i in range(tiles):
                down_copy(i).start()
                up_copy(i).start()
                if i == 0:
                    d_copy(1).start()
            loads[4].start()
        if stage == SECOND:
            entries = [
                pltpu.make_async_copy(mid_in.at[here], v_do, sem_o.at[0]),
                pltpu.make_async_copy(middle_in, v_acc, sem_o.at[3]),
            ]
            for copy in entries:
                copy.start()
        def enter_attention():
            for k in (5, 1, 2, 3):
                loads[k].start()
            p_copy(0).start()
            p_copy(1).start()

        def enter_last():
            loads[6].start()
            loads[0].start()

        if stage == SECOND:
            enter_attention()
            enter_last()
        nothing = jnp.zeros((8, width), f32)

        def fold(values):
            return jnp.sum(values.reshape(-1, 8, width), axis=0)

        def enter(i, total):
            at = part(i, 64)
            place = lax.broadcasted_iota(jnp.int32, (64, 1), 0) + i * 64
            masked = jnp.where(place < length, v_dy[at, :].astype(f32), 0.0)
            v_dy[at, :] = masked.astype(bf16)
            v_acc[at, :] = jnp.zeros((64, width), f32)
            return total + fold(masked)

        if feeds:
            pltpu.make_async_copy(recv, v_dy, sem_x.at[0]).wait()
            total = lax.fori_loop(0, rows // 64, enter, nothing, unroll=2)
            smalls[7:8, :] = jnp.sum(total, axis=0, keepdims=True)
        if stage == BOTH:
            feed_copy = pltpu.make_async_copy(v_dy, g_feed.at[here], sem_o.at[4])
            feed_copy.start()

        def feed(i):
            down_copy(i).wait()
            up_copy(i).wait()
            d_copy(i).wait()
            if stage == BOTH:
                pl.when(i == tiles - 2)(enter_attention)
                pl.when(i == tiles - 1)(enter_last)
            at = part(i, WIDE)
            pre = (nt(v_dy[...], v_down[at, :]) * v_d[i % 2].astype(f32)).astype(bf16)
            v_du[:, at] = pre
            v_acc[...] += nt(pre, v_up[:, at])
            smalls[pl.ds(8 + i, 1), :] = jnp.sum(v_du[:, at].astype(f32), axis=0, keepdims=True)
            pltpu.make_async_copy(v_du.at[:, at], g_up.at[here, at], sem_o.at[3]).start()

            @pl.when(i + 2 < tiles)
            def _():
                d_copy(i + 2).start()

        if feeds:
            loop(tiles, feed)
            loads[4].wait()

        def norm_back(source, grad, gain):
            normed, inverse = row_stats(source)
            scaled = grad * gain
            mean_one = jnp.mean(scaled, axis=-1, keepdims=True)
            mean_two = jnp.mean(scaled * normed, axis=-1, keepdims=True)
            return inverse * (scaled - mean_one - normed * mean_two), fold(grad * normed), fold(grad)

        def second_norm(i, carry):
            at = part(i, 64)
            rows_back, one, two = norm_back(v_h[at, :], v_acc[at, :], norm(2))
            middle = rows_back + v_dy[at, :].astype(f32)
            v_acc[at, :] = middle
            low = middle.astype(bf16)
            v_do[at, :] = low
            return carry[0] + one, carry[1] + two, carry[2] + fold(low.astype(f32))

        if feeds:
            sums = lax.fori_loop(0, rows // 64, second_norm, (nothing,) * 3, unroll=2)
            for k, value in zip((2, 3, 6), sums):
                smalls[k : k + 1, :] = jnp.sum(value, axis=0, keepdims=True)
            outs = [pltpu.make_async_copy(v_do, g_mid.at[here], sem_o.at[0])]
            if stage == FIRST:
                outs.append(pltpu.make_async_copy(v_acc, middle_out, sem_o.at[1]))
            for copy in outs:
                copy.start()
        if stage == SECOND:
            for copy in entries:
                copy.wait()
        if attends:
            loads[5].wait()
            v_dc[...] = nt(v_do[...], v_out[...]).astype(bf16)
            for k in (1, 2, 3):
                loads[k].wait()
        lane = lax.broadcasted_iota(jnp.int32, (1, GROUP), 1) // HEAD

        def attend(i):
            p_copy(i).wait()
            at = part(i, GROUP)
            key_at = pl.ds(pl.multiple_of(width + i * GROUP, GROUP), GROUP)
            value_at = pl.ds(pl.multiple_of(2 * width + i * GROUP, GROUP), GROUP)
            key = v_qkv[:, key_at]
            value = v_qkv[:, value_at]
            query = v_qkv[:, at]
            wide = v_dc[:, at].astype(f32) * v_l[:, at]
            low = wide.astype(bf16)
            dots = wide * v_c[:, at].astype(f32)
            for h in range(4):
                hs = slice(h * rows, (h + 1) * rows)
                v_k[hs, :] = jnp.where(lane == h, key, 0).astype(bf16)
                masked = jnp.where(lane == h, low, 0).astype(bf16)
                delta = jnp.sum(jnp.where(lane == h, dots, 0.0), axis=-1, keepdims=True)
                inner = nt(masked, value) - delta
                v_s[:, hs] = (v_p[i % 2, h].astype(f32) * inner).astype(bf16)
            grad_query = (nn(v_s[...], v_k[...]) * score_scale).astype(bf16)
            query_t = query.T
            low_t = low.T
            keys, values = [], []
            for h in range(4):
                hs = slice(h * HEAD, (h + 1) * HEAD)
                keys.append(nn(query_t[hs], v_s[:, h * rows : (h + 1) * rows]))
                values.append(nn(low_t[hs], v_p[i % 2, h]))
            grad_key = (jnp.concatenate(keys, axis=0) * score_scale).astype(bf16).T
            grad_value = jnp.concatenate(values, axis=0).astype(bf16).T
            v_dqkv[:, at] = grad_query
            v_dqkv[:, key_at] = grad_key
            v_dqkv[:, value_at] = grad_value
            smalls[4:5, at] = jnp.sum(grad_query.astype(f32), axis=0, keepdims=True)
            smalls[5:6, at] = jnp.sum(grad_value.astype(f32), axis=0, keepdims=True)

            @pl.when(i + 2 < width // GROUP)
            def _():
                p_copy(i + 2).start()

        if attends:
            loop(width // GROUP, attend)
            qkv_copy = pltpu.make_async_copy(v_dqkv, g_qkv.at[here], sem_o.at[1])
            qkv_copy.start()
            loads[6].wait()
            loads[0].wait()

            v_h[...] = nt(v_dqkv[...], v_in[...])

        def first_norm(i, carry):
            at = part(i, 64)
            rows_back, one, two = norm_back(v_x[at, :].astype(f32), v_h[at, :], norm(0))
            v_dx[at, :] = (rows_back + v_acc[at, :]).astype(bf16)
            return carry[0] + one, carry[1] + two

        if attends:
            sums = lax.fori_loop(0, rows // 64, first_norm, (nothing,) * 2, unroll=2)
            for k, value in enumerate(sums):
                smalls[k : k + 1, :] = jnp.sum(value, axis=0, keepdims=True)
            dx_copy = pltpu.make_async_copy(v_dx, dx_out, sem_o.at[2])
            dx_copy.start()
            input_copy = pltpu.make_async_copy(v_dx, inputs.at[0, picked, 0], sem_o.at[5])
            input_copy.start()
            for copy in (qkv_copy, dx_copy, input_copy):
                copy.wait()
        if stage == BOTH:
            feed_copy.wait()
        if feeds:
            for copy in outs:
                copy.wait()
            pltpu.make_async_copy(v_du, g_up.at[here], sem_o.at[3]).wait()

    @pl.when(jnp.logical_not(active))
    def _():
        smalls[...] = jnp.zeros_like(smalls)


def backward_call(slot, plan, stage, spans, norms, cot, recv, weights, stash, given, grads):
    rows, width = recv.shape
    hidden = weights[2].shape[1]
    any_ = pl.BlockSpec(memory_space=pl.ANY)
    vm = pl.BlockSpec(memory_space=pltpu.VMEM)
    shape = jax.ShapeDtypeStruct
    outs = {"smalls": shape((8 + hidden // WIDE, width), f32)}
    if stage != SECOND:
        outs["up"] = shape((2 * rows, hidden), bf16)
        outs["mid"] = shape((2 * rows, width), bf16)
    if stage != FIRST:
        outs["dx"] = shape((rows, width), bf16)
        outs["qkv"] = shape((2 * rows, 3 * width), bf16)
        outs["inputs"] = shape((1, 2, 1, rows, width), bf16)
    if stage == BOTH:
        outs["feed"] = shape((2 * rows, width), bf16)
    if stage == FIRST:
        outs["middle"] = shape((rows, width), f32)
    names = list(outs)
    kept = [name for name in names if name in grads and name not in ("smalls", "dx")]
    s_x, s_a, s_qkv, s_c, s_l, s_h, s_b, s_g, s_d, s_p, _ = stash
    results = pl.pallas_call(
        functools.partial(backward_kernel, slot, plan, stage, len(kept), len(given)),
        in_specs=[pl.BlockSpec(memory_space=pltpu.SMEM), vm] + [any_] * (13 + len(given) + len(kept)),
        out_specs=[vm] + [any_] * (len(names) - 1),
        out_shape=list(outs.values()),
        input_output_aliases={15 + len(given) + k: names.index(n) for k, n in enumerate(kept)},
        scratch_shapes=[pltpu.VMEM(w.shape, bf16) for w in weights] + [
            pltpu.VMEM((rows, width), bf16),
            pltpu.VMEM((rows, width), bf16),
            pltpu.VMEM((rows, 3 * width), bf16),
            pltpu.VMEM((rows, width), bf16),
            pltpu.VMEM((rows, width), f32),
            pltpu.VMEM((rows, width), f32),
            pltpu.VMEM((2, rows, WIDE), bf16),
            pltpu.VMEM((2, 4, rows, rows), bf16),
            pltpu.VMEM((rows, hidden), bf16),
            pltpu.VMEM((rows, width), bf16),
            pltpu.VMEM((rows, width), bf16),
            pltpu.VMEM((rows, 3 * width), bf16),
            pltpu.VMEM((rows, width), f32),
            pltpu.VMEM((rows, 4 * rows), bf16),
            pltpu.VMEM((4 * rows, GROUP), bf16),
            pltpu.VMEM((rows, width), bf16),
            pltpu.SemaphoreType.DMA((2 * hidden // WIDE,)),
            pltpu.SemaphoreType.DMA((8,)),
            pltpu.SemaphoreType.DMA((2,)),
            pltpu.SemaphoreType.DMA((2,)),
            pltpu.SemaphoreType.DMA((6,)),
        ],
        compiler_params=pltpu.CompilerParams(vmem_limit_bytes=VMEM),
        cost_estimate=pl.CostEstimate(flops=LARGE, bytes_accessed=1, transcendentals=0),
        name="layer_backward",
    )(
        spans, norms, cot, recv, *weights, s_x, s_qkv, s_c, s_l, s_h, s_d, s_p, *given,
        *[grads[name] for name in kept],
    )
    return {**grads, **dict(zip(names, results))}


def turn_kernel(blocks, *refs):
    count = len(blocks)
    for k, block in enumerate(blocks):
        source, target = refs[k], refs[count + k]

        @pl.when((pl.program_id(0) == k) if k + 1 < count else (pl.program_id(0) >= k))
        def _(source=source, target=target, block=block):
            flat = source[...].T
            pairs = flat.shape[0] // (2 * block)
            for core in range(2):

                @pl.when(lax.axis_index("dp") % 2 == core)
                def _(core=core):
                    for j in range(pairs):
                        at = slice(j * block, (j + 1) * block)
                        other = (2 * j + 1 - core) * block
                        own = (2 * j + core) * block
                        target[0, at, :] = flat[other : other + block]
                        target[1, at, :] = flat[own : own + block]


def turn_call(sources):
    rows = sources[0].shape[0]
    count = len(sources)
    size = lax.axis_size("dp")
    steps = count - 1 + sources[-1].shape[1] // WIDE

    def last(i):
        return jnp.maximum(i - (count - 1), 0)

    ins = [pl.BlockSpec((rows, WIDE), lambda i: (0, 0))] * (count - 1)
    ins.append(pl.BlockSpec((rows, WIDE), lambda i: (0, last(i))))
    outs = [pl.BlockSpec((2, WIDE // 2, rows), lambda i: (0, 0, 0))] * (count - 1)
    outs.append(pl.BlockSpec((2, WIDE // 2, rows), lambda i: (0, last(i), 0)))
    return pl.pallas_call(
        functools.partial(turn_kernel, [s.shape[1] // size for s in sources]),
        grid=(steps,),
        in_specs=ins,
        out_specs=outs,
        out_shape=[jax.ShapeDtypeStruct((2, s.shape[1] // 2, rows), bf16) for s in sources],
        compiler_params=pltpu.CompilerParams(vmem_limit_bytes=VMEM),
        cost_estimate=pl.CostEstimate(flops=1, bytes_accessed=1, transcendentals=0),
        name="turn",
    )(*sources)


def weight_kernel(widths, half, left, right, *rest):
    late, outs = rest[: -len(widths)], rest[-len(widths) :]
    if late:
        rows = late[0].shape[0]
        second = jnp.where(lax.axis_index("section") == 0, late[0][...], right[rows:, :])
        total = nn(left[0, :, :rows], right[:rows, :]) + nn(left[0, :, rows:], second)
    else:
        total = nn(left[0], right[...])
    total = total.astype(bf16)
    at = 0
    for width, out in zip(widths, outs):
        step, offset = divmod(at, right.shape[1])
        if len(widths) == 1:
            out[...] = total
        else:

            @pl.when(pl.program_id(1) == step)
            def _(out=out, cut=slice(offset, offset + width)):
                out[...] = total[:, cut]

        at += width


def weight_call(left, right, start, widths, half, late=None):
    _, height, rows = left.shape
    columns = sum(widths)
    tall = min(height, 512)
    wide = min(columns, WIDE)
    specs = [
        pl.BlockSpec((1, tall, rows), lambda i, j: (half, i, 0)),
        pl.BlockSpec((rows, wide), lambda i, j: (0, start // wide + j)),
    ]
    operands = (left, right)
    if late is not None:
        specs.append(pl.BlockSpec((rows // 2, wide), lambda i, j: (0, j)))
        operands += (late,)

    def out(width):
        if width > wide:
            return pl.BlockSpec((tall, wide), lambda i, j: (i, j))
        return pl.BlockSpec((tall, width), lambda i, j: (i, 0))

    return pl.pallas_call(
        functools.partial(weight_kernel, widths, half),
        grid=(height // tall, columns // wide),
        in_specs=specs,
        out_specs=[out(width) for width in widths],
        out_shape=[jax.ShapeDtypeStruct((height, width), bf16) for width in widths],
        compiler_params=pltpu.CompilerParams(vmem_limit_bytes=VMEM),
        cost_estimate=pl.CostEstimate(flops=1, bytes_accessed=1, transcendentals=0),
        name="weight_product",
    )(*operands)


def sum_kernel(layout, lefts, fixed, free, place, *refs):
    count = sum(len(arrays) for arrays in layout)
    sources = iter(refs[:count])
    terms = [[next(sources) for _ in arrays] for arrays in layout]
    out, held, total, sem, out_sem = refs[-5:]
    me = lax.axis_index("dp")
    cells = list(itertools.product(range(2), repeat=len(free)))
    loads, slot = [], 0
    for cell in cells:
        loads.append([])
        for arrays, left, widths in zip(terms, lefts, layout):
            index = []
            for bit in left:
                if bit in free:
                    index.append(cell[free.index(bit)])
                else:
                    own = (me >> bit) & 1
                    index.append(own if fixed[bit] else 1 - own)
            at = 0
            for ref, (start, width) in zip(arrays, widths):
                copy = pltpu.make_async_copy(
                    ref.at[(*index, slice(None), pl.ds(start, width))],
                    held.at[slot, :, pl.ds(at, width)],
                    sem.at[len(loads[-1]), len(loads) - 1],
                )
                copy.start()
                loads[-1].append(copy)
                at += width
            slot += 1
    stores = []
    for k, cell in enumerate(cells):
        for copy in loads[k]:
            copy.wait()
        value = added([held[k * len(terms) + j] for j in range(len(terms))])
        total[k] = value.astype(total.dtype)
        stores.append(pltpu.make_async_copy(total.at[k], place(out, cell), out_sem.at[k]))
        stores[-1].start()
    for copy in stores:
        copy.wait()


def sum_call(terms, fixed, kind, into=None, start=0):
    rows = terms[0][0][0][0].shape[-2]
    layout = [[(at, width) for _, at, width in arrays] for arrays, _ in terms]
    lefts = [left for _, left in terms]
    columns = sum(width for _, width in layout[0])
    free = [bit for bit in lefts[0] if bit not in fixed]
    operands = [array for arrays, _ in terms for array, _, _ in arrays]
    cells = 2 ** len(free)
    aliases = {}
    wide = 0
    if into is None:
        shape = jax.ShapeDtypeStruct((2,) * len(free) + (rows, columns), kind)
    else:
        wide, into = into
        shape = jax.ShapeDtypeStruct((1, rows, wide), kind)
        if into is not None:
            aliases = {len(operands): 0}
            operands.append(into)

    given = len(operands)

    def place(out, cell):
        if wide:
            return out.at[0, :, pl.ds(start, columns)]
        return out.at[cell] if cell else out

    def kernel(*refs):
        refs = refs[: given - len(aliases)] + refs[given:]
        sum_kernel(layout, lefts, fixed, free, place, *refs)

    any_ = pl.BlockSpec(memory_space=pl.ANY)
    return pl.pallas_call(
        kernel,
        in_specs=[any_] * len(operands),
        out_specs=any_,
        out_shape=shape,
        input_output_aliases=aliases,
        scratch_shapes=[
            pltpu.VMEM((cells * len(terms), rows, columns), terms[0][0][0][0].dtype),
            pltpu.VMEM((cells, rows, columns), kind),
            pltpu.SemaphoreType.DMA((max(sum(len(arrays) for arrays, _ in terms), 1), cells)),
            pltpu.SemaphoreType.DMA((cells,)),
        ],
        compiler_params=pltpu.CompilerParams(vmem_limit_bytes=VMEM),
        cost_estimate=pl.CostEstimate(flops=SMALL, bytes_accessed=1, transcendentals=0),
        name="sum_terms",
    )(*operands)


highest = lax.Precision.HIGHEST


def added(terms):
    total = terms[0].astype(f32)
    for term in terms[1:]:
        total = total + term.astype(f32)
    return total


class Line:
    def __init__(self):
        self.last = None

    def after(self, values):
        if self.last is not None:
            values = lax.optimization_barrier(tuple(values) + (self.last,))[:-1]
        return list(values)

    def done(self, value):
        self.last = value


class Exchange:
    def __init__(self, line, terms, left, order):
        self.line = line
        self.terms = [(arrays, sorted(left, reverse=True)) for arrays in terms]
        self.fixed = {}
        self.order = list(order)
        self.kind = terms[0][0][0].dtype

    def total(self, fixed, kind, **where):
        values = iter(self.line.after([array for arrays, _ in self.terms for array, _, _ in arrays]))
        self.terms = [
            ([(next(values), at, width) for _, at, width in arrays], left)
            for arrays, left in self.terms
        ]
        total = sum_call(self.terms, fixed, kind, **where)
        self.line.done(total)
        return total

    def step(self):
        bit = self.order.pop(0)
        theirs = self.total({**self.fixed, bit: False}, self.kind)
        self.fixed[bit] = True
        left = [k for k in self.terms[0][1] if k not in self.fixed]
        self.terms.append((whole(crossed(theirs, bit)), left))

    def cut(self, widths):
        parts = []
        low = 0
        for width in widths:
            high = low + width
            terms = []
            for arrays, left in self.terms:
                chosen, at = [], 0
                for array, start, columns in arrays:
                    a, b = max(low, at), min(high, at + columns)
                    if a < b:
                        chosen.append((array, start + a - at, b - a))
                    at += columns
                terms.append((chosen, left))
            part_ = Exchange(self.line, [terms[0][0]], (), self.order)
            part_.terms = terms
            part_.fixed = dict(self.fixed)
            parts.append(part_)
            low = high
        return parts

    def finish(self, **where):
        while self.order:
            self.step()
        return self.total(self.fixed, f32, **where)


def crossed(value, bit):
    return lax.ppermute(value, "dp", [(i, i ^ (1 << bit)) for i in range(lax.axis_size("dp"))])


def whole(array):
    return [(array, 0, array.shape[-1])]


def whole(array):
    return [(array, 0, array.shape[-1])]


class WeightSum(Exchange):
    def __init__(self, line, left, right, start, widths, order, late=None):
        size = lax.axis_size("dp")
        bits = size.bit_length() - 1
        shape = [2] * (bits - 1) + [2 * left.shape[1] // size, -1]
        left, right = line.after((left, right))
        theirs = weight_call(left, right, start, widths, 0, late)
        line.done(theirs[-1])
        received = [whole(crossed(array, 0).reshape(shape)) for array in theirs]
        self.product = (left, right, start, [sum(widths)], 1, late)
        self.shape = shape
        super().__init__(line, (sum(received, []),), range(1, bits), order)

    def own(self):
        left, right = self.line.after(self.product[:2])
        (mine,) = weight_call(left, right, *self.product[2:])
        self.line.done(mine)
        self.terms.append((whole(mine.reshape(self.shape)), self.terms[0][1]))
        return self


def shards(
    features,
    cotangent,
    lengths,
    codebook_index,
    attention_in,
    attention_out,
    feed_up,
    feed_down,
    vectors,
    adaptive_weight,
    codebook_table,
):
    is_first = lax.axis_index("section") == 0
    adaptive = jnp.where(is_first, 0.0, 1.0)
    rows, width = features.shape[2:]
    hidden = feed_up.shape[2]
    size = lax.axis_size("dp")
    bits = size.bit_length() - 1
    weights = (attention_in[0], attention_out[0], feed_up[0], feed_down[0])

    def send(value, to):
        return lax.ppermute(value, "section", [(1 - to, to)])

    nowhere = jnp.zeros((rows, width), bf16)

    def forward(slot, plan, norms, recv, stash=()):
        return forward_call(slot, plan, lengths, norms, vectors, features, recv, weights, stash)

    def backward(slot, plan, stage, norms, recv, stash, grads, given=()):
        return backward_call(
            slot, plan, stage, lengths, norms, cotangent, recv, weights, stash, given, grads
        )

    z_one, squares_one, stash = forward(0, (0, None), vectors, nowhere)
    received_one = send(z_one, 1)
    table, z_one = lax.optimization_barrier((codebook_table, z_one))
    condition_table = jnp.dot(table, adaptive_weight, preferred_element_type=f32)
    one_hot = (
        codebook_index[:, 0][:, None]
        == jnp.arange(codebook_table.shape[0], dtype=jnp.int32)[None, :]
    ).astype(f32)
    norms = vectors[:, : 4 * width] + adaptive * jnp.dot(
        one_hot, condition_table, precision=highest
    )
    norms_one, norms_two = norms[:1], norms[1:]
    z_two, squares_two, stash = forward(1, (1, 0), norms_one, received_one, stash)
    received_two = send(z_two, 1)
    grads = backward(1, (None, 0), BOTH, norms_one, nowhere, stash, {})
    smalls_one = grads["smalls"]
    back_one = send(grads["dx"], 0)
    z_three, squares_three, stash = forward(0, (None, 1), norms_two, received_two, stash)
    grads = backward(0, (0, 1), BOTH, norms_two, back_one, stash, grads)
    smalls_two = grads["smalls"]
    back_two = send(grads["dx"], 0)

    s_x, s_a, s_qkv, s_c, s_l, s_h, s_b, s_g, s_d, s_p, layer_outputs = stash
    side_first = list(range(1, bits))
    line_first = side_first[1:] + side_first[:1]
    line = Line()
    line.done(smalls_two)
    squares = jnp.sum(squares_one + squares_two + squares_three, axis=(1, 2))
    counted = jnp.sum(lengths).astype(f32)
    (totals,) = line.after((jnp.concatenate([squares, counted[None], jnp.zeros((123,), f32)]),))
    for bit in range(bits):
        totals = totals + crossed(totals, bit)
    t_a, t_b, t_c, t_g = turn_call(line.after((s_a, s_b, s_c, s_g)))
    line.done(t_a)
    (totals,) = line.after((totals,))
    line.done(totals)
    down = WeightSum(line, t_g, grads["feed"], 0, [width], side_first, back_two).own()
    down.step()
    (back_two,) = line.after((back_two,))
    grads = backward(1, (1, None), FIRST, vectors, back_two, stash, grads)
    smalls_three = grads["smalls"]
    line.done(smalls_three)
    up = WeightSum(line, t_b, grads["up"], 0, [WIDE] * (hidden // WIDE), side_first).own()
    up.step()
    down.step()
    out = WeightSum(line, t_c, grads["mid"], 0, [width], side_first).own()
    (middle,) = line.after((grads["middle"],))
    grads = backward(
        1, (1, None), SECOND, vectors, back_two, stash, grads, (grads["mid"], middle)
    )
    smalls_four = grads["smalls"]
    line.done(smalls_four)
    g_qkv, input_grads = grads["qkv"], grads["inputs"]
    down.step()
    into_one = WeightSum(line, t_a, g_qkv, 0, [width] * 3, side_first).own()

    smalls = smalls_one + smalls_two + smalls_three + smalls_four
    table_grad = one_hot[0][:, None] * smalls_one[:4].reshape(1, -1) + one_hot[1][:, None] * (
        smalls_two[:4].reshape(1, -1) * adaptive
    )
    codes = table_grad.shape[0]
    share = table_grad.shape[1] // (2 * size)
    table_blocks = table_grad.reshape(codes, 2, size, share).transpose(2, 1, 0, 3)
    packed = jnp.concatenate([smalls.reshape(size, -1), table_blocks.reshape(size, -1)], axis=1)
    count = packed.shape[1]
    block = width // size
    packed = jnp.pad(packed.reshape(size, block, -1), ((0, 0), (0, 0), (0, 128 - count // block)))
    packed = packed.astype(bf16).reshape([2] * bits + [block, 128])
    core = lax.axis_index("dp") & 1
    (other, own) = [
        lax.dynamic_index_in_dim(packed, which, bits - 1, keepdims=False)
        for which in (1 - core, core)
    ]
    other = crossed(other, 0)
    into_one, into_two = into_one.cut([2 * width, width])
    up_one, up_two = up.cut([hidden // 2] * 2)
    into_two.terms = [
        (arrays + whole(extra), left)
        for (arrays, left), extra in zip(into_two.terms, (other, own))
    ]
    into_one.step()
    up_one.step()
    up_two.step()
    into_two.step()
    out.step()
    down = down.finish(into=(width, None))
    up_one.step()
    into_one.step()
    up_two.step()
    into_two.step()
    up = up_one.finish(into=(hidden, None))
    into_one.step()
    out.step()
    up = up_two.finish(into=(hidden, up), start=hidden // 2)
    into_two.step()
    into = into_one.finish(into=(3 * width, None))
    out.step()
    last = into_two.finish()
    out = out.finish(into=(width, None))
    into = lax.dynamic_update_slice(into, last[None, :, :width], (0, 0, 2 * width))
    small_sum = last[:, width : width + count // block].reshape(-1)
    vector_share = small_sum[: smalls.size // size]
    table_share = small_sum[smalls.size // size :].reshape(2, codes, share)
    table_own = jnp.where(is_first, send(table_share[0], 0), table_share[1])
    grad_adaptive = lax.dot_general(
        codebook_table.astype(f32),
        table_own,
        (((0,), (0,)), ((), ())),
        precision=highest,
        preferred_element_type=f32,
    )
    residual_rms = jnp.sqrt(totals[:4] / (totals[4] * width))[None]

    return (
        layer_outputs,
        input_grads,
        into,
        out,
        up,
        down,
        vector_share[None],
        grad_adaptive,
        residual_rms,
    )


def solution(mesh):
    placed = (
        P(None, "dp", None, None),
        P(None, "dp", None, None),
        P(None, "dp"),
        P(None, "dp"),
        P("section", None, None),
        P("section", None, None),
        P("section", None, None),
        P("section", None, None),
        P("section", None),
        P(),
        P(),
    )
    return jax.shard_map(
        shards,
        mesh=mesh,
        in_specs=placed,
        out_specs=(
            P("section", None, "dp", None, None),
            P("section", None, "dp", None, None),
            P("section", "dp", None),
            P("section", "dp", None),
            P("section", "dp", None),
            P("section", "dp", None),
            P("section", "dp"),
            P(None, ("section", "dp")),
            P("section", None),
        ),
        check_vma=False,
    )
```

```python
import functools
import itertools

import jax
import jax.numpy as jnp
from jax import lax
from jax.experimental import pallas as pl
from jax.experimental.pallas import tpu as pltpu
from jax.sharding import PartitionSpec as P

HEAD = 64
norm_eps = 1e-05
root_half = 0.7071067811865476
slope_scale = 0.3989422804014327
score_scale = 0.125
big_negative = -1e30
f32 = jnp.float32
bf16 = jnp.bfloat16
GROUP = 4 * HEAD
TILE = 512
WIDE = 1024
BROAD = 2048
VMEM = 62 * 2**20
SMALL = 10**6
LARGE = 10**11
BOTH, FIRST, SECOND = range(3)
LESS = 16 * 2**20


def nn(a, b):
    return lax.dot_general(a, b, (((1,), (0,)), ((), ())), preferred_element_type=f32)


def nt(a, b):
    return lax.dot_general(a, b, (((1,), (1,)), ((), ())), preferred_element_type=f32)


def row_stats(rows):
    average = jnp.mean(rows, axis=-1, keepdims=True)
    centered = rows - average
    inverse = lax.rsqrt(jnp.mean(centered * centered, axis=-1, keepdims=True) + norm_eps)
    return centered * inverse, inverse


def gate(values):
    bell = jnp.exp(-0.5 * values * values)
    upper = 0.5 * (1.0 + lax.erf(values * root_half))
    return values * upper, upper + values * bell * slope_scale


def loop(count, body, unroll=1):
    def run(i, carry):
        body(i)
        return carry

    lax.fori_loop(0, count, run, 0, unroll=unroll)


def part(i, size):
    return pl.ds(pl.multiple_of(i * size, size), size)


def copies(pairs, sem):
    return [pltpu.make_async_copy(a, b, sem.at[i]) for i, (a, b) in enumerate(pairs)]


def chosen_tick(first, plan):
    picked = jnp.where(first, plan[0] or 0, plan[1] or 0)
    active = jnp.where(first, int(plan[0] is not None), int(plan[1] is not None)) == 1
    return active, picked


def early_rows(rows):
    return 3 * rows // 4


def forward_kernel(slot, plan, stage, aliased, pieces, *refs):
    starts, ends = stage != SECOND, stage != FIRST
    spans, norms, vectors, feat, w_in, w_out, w_up, w_down = refs[:8]
    recv = refs[8 : 8 + pieces]
    refs = refs[8 + pieces :]
    kept = refs[:aliased]
    refs = refs[aliased:]
    z_out, squares_out = refs[:2]
    s_x, s_a, s_qkv, s_c, s_l, s_h, s_b, s_g, s_d, s_p, layers = refs[2:13]
    (v_in, v_out, v_up, v_down, v_x, v_a, v_qkv, v_c, v_l, v_h, v_b, v_g, v_d, v_p, v_bias, v_acc, v_z,
     sem_w, sem_x, sem_o, sem_p, sem_g, sem_d) = refs[13:]
    rows, width = v_x.shape
    hidden = v_up.shape[1]
    here = pl.ds(slot * rows, rows)
    first = lax.axis_index("section") == 0
    active, picked = chosen_tick(first, plan)

    def norm(k):
        return norms[:, k * width : (k + 1) * width]

    def bias(k):
        return vectors[:, k * width : (k + 1) * width]

    @pl.when(active)
    def _():
        length = spans[picked]
        causal = first

        loaded = pltpu.make_async_copy(feat.at[picked, 0], v_x, sem_x.at[0])
        if starts:
            pl.when(first)(loaded.start)

            @pl.when(jnp.logical_not(first))
            def _():
                at = 0
                for piece in recv:
                    pltpu.make_async_copy(
                        piece, v_x.at[pl.ds(at, piece.shape[0])], sem_x.at[0]
                    ).start()
                    at += piece.shape[0]

        def column(source, target, index, size):
            def at(i):
                return pltpu.make_async_copy(
                    source.at[:, part(i, size)], target.at[:, part(i, size)], sem_w.at[index + i]
                )

            return at

        def down_copy(i):
            return pltpu.make_async_copy(
                w_down.at[part(i, BROAD)], v_down.at[part(i, BROAD)], sem_w.at[3 + 1 + hidden // BROAD + i]
            )

        in_copy = column(w_in, v_in, 0, WIDE)
        out_copy = column(w_out, v_out, 3, WIDE)
        up_copy = column(w_up, v_up, 4, BROAD)
        if starts:
            for i in range(3):
                in_copy(i).start()

        outs = []

        def send(source, target, index):
            copy = pltpu.make_async_copy(source, target, sem_o.at[index])
            copy.start()
            outs.append(copy)

        valid = lambda i, n: (lax.broadcasted_iota(jnp.int32, (n, 1), 0) + i * n < length).astype(f32)

        def square(values, mask):
            return jnp.sum((values * values * mask).reshape(-1, 8, width), axis=0)

        nothing = jnp.zeros((8, width), f32)
        sums_one = (nothing, nothing)
        groups = width // GROUP

        def p_copy(i):
            return pltpu.make_async_copy(
                v_p.at[i % 2], s_p.at[slot, pl.ds(i * 4, 4)], sem_p.at[i % 2]
            )

        def start_feed():
            for i in range(hidden // BROAD):
                up_copy(i).start()
                down_copy(i).start()

        half = rows // 2
        low = early_rows(rows) if stage == SECOND else 0
        high = early_rows(rows) if stage == FIRST else rows
        these = slice(low, high)
        count = high - low
        there = pl.ds(slot * rows + low, count)
        if stage == SECOND:
            start_feed()
            entries = [
                pltpu.make_async_copy(kept[5].at[there], v_h.at[pl.ds(low, count)], sem_o.at[0]),
                pltpu.make_async_copy(kept[6].at[there], v_b.at[pl.ds(low, count)], sem_o.at[1]),
            ]
            for copy in entries:
                copy.start()
            for copy in entries:
                copy.wait()
            v_acc[these, :] = jnp.broadcast_to(bias(7), (count, width))
        if starts:
            def bias_rows(i):
                at = part(i, 128)
                query = lax.broadcasted_iota(jnp.int32, (128, rows), 0) + i * 128
                key = lax.broadcasted_iota(jnp.int32, (128, rows), 1)
                open_ = (key < length) & ((key <= query) | jnp.logical_not(causal))
                v_bias[at, :] = jnp.where(open_, 0.0, big_negative)

            loop(rows // 128, bias_rows)
            loaded.wait()

            def first_norm(i):
                at = part(i, 64)
                normed, _ = row_stats(v_x[at, :].astype(f32))
                v_a[at, :] = (normed * norm(0) + norm(1)).astype(bf16)

            loop(rows // 64, first_norm, 2)
            send(v_x, s_x.at[here], 0)
            send(v_a, s_a.at[here], 1)
            def project(i):
                in_copy(i).wait()
                at = part(i, WIDE)
                shift = vectors[:, pl.ds(pl.multiple_of((4 + i // 2) * width, width), width)]
                tile = nn(v_a[...], v_in[:, at]) + jnp.where(i == 1, 0.0, shift)
                v_qkv[:, at] = tile.astype(bf16)

            loop(3 * width // WIDE, project)
            out_copy(0).start()
            start_feed()
            send(v_qkv, s_qkv.at[here], 2)
            lane = lax.broadcasted_iota(jnp.int32, (1, GROUP), 1) // HEAD

            def attend(i):
                at = part(i, GROUP)
                query = v_qkv[:, at]
                key = v_qkv[:, pl.ds(pl.multiple_of(width + i * GROUP, GROUP), GROUP)]
                value = v_qkv[:, pl.ds(pl.multiple_of(2 * width + i * GROUP, GROUP), GROUP)]

                @pl.when(i >= 2)
                def _():
                    p_copy(i - 2).wait()

                half = rows // 2

                def rows_part(r, keys):
                    picked_rows = slice(r * half, (r + 1) * half)
                    scaled = query[picked_rows] * score_scale
                    total = jnp.zeros((half, GROUP), f32)
                    sums = jnp.ones((half, GROUP), f32)
                    for h in range(4):
                        masked = jnp.where(lane == h, scaled, 0).astype(bf16)
                        scores = nt(masked, key[:keys]) + v_bias[picked_rows, :keys]
                        top = jnp.max(scores, axis=-1, keepdims=True)
                        raised = jnp.exp(scores - top).astype(bf16)
                        v_p[i % 2, h, picked_rows, :keys] = raised
                        if keys < rows:
                            v_p[i % 2, h, picked_rows, keys:] = jnp.zeros((half, rows - keys), bf16)
                        product = nn(raised, jnp.where(lane == h, value[:keys], 1).astype(bf16))
                        total = jnp.where(lane == h, product, total)
                        sums = jnp.where(lane == (h ^ 1), product, sums)
                    inverse = 1.0 / jnp.concatenate(
                        [pltpu.roll(sums[:, k : k + 128], HEAD, 1) for k in (0, 128)], axis=1
                    )
                    v_l[picked_rows, at] = inverse
                    v_c[picked_rows, at] = (total * inverse).astype(bf16)

                @pl.when(causal)
                def _():
                    rows_part(0, half)
                    rows_part(1, rows)

                @pl.when(jnp.logical_not(causal))
                def _():
                    rows_part(0, rows)
                    rows_part(1, rows)

                p_copy(i).start()

            loop(groups, attend)
            send(v_c, s_c.at[here], 8)
            send(v_l, s_l.at[here], 9)
            out_copy(0).wait()
            def mix(i):
                at = part(i, WIDE)
                v_acc[:, at] = nn(v_c[...], v_out[:, at]) + bias(6)

            loop(width // WIDE, mix)

            def second_norm(i, carry):
                at = part(i, 64)
                branch = v_acc[at, :]
                middle = v_x[at, :].astype(f32) + branch
                v_h[at, :] = middle
                normed, _ = row_stats(middle)
                v_b[at, :] = (normed * norm(2) + norm(3)).astype(bf16)
                v_acc[at, :] = jnp.broadcast_to(bias(7), (64, width))
                mask = valid(i, 64)
                return (carry[0] + square(middle, mask), carry[1] + square(branch, mask))

            sums_one = lax.fori_loop(0, rows // 64, second_norm, sums_one, unroll=2)
            send(v_h, s_h.at[here], 3)
            send(v_b, s_b.at[here], 4)

        def feed(i):
            up_copy(i).wait()
            down_copy(i).wait()
            at = part(i, BROAD)
            shift = vectors[:, pl.ds(pl.multiple_of(8 * width + i * BROAD, BROAD), BROAD)]
            act, slope = gate(nn(v_b[these, :], v_up[:, at]) + shift)
            act = act.astype(bf16)
            v_g[these, at] = act
            v_d[these, at] = slope.astype(bf16)
            v_acc[these, :] += nn(act, v_down[at, :])
            g_copy(i).start()
            d_copy(i).start()

        def g_copy(i):
            at = part(i, BROAD)
            return pltpu.make_async_copy(v_g.at[pl.ds(low, count), at], s_g.at[there, at], sem_g.at[i])

        def d_copy(i):
            at = part(i, BROAD)
            return pltpu.make_async_copy(v_d.at[pl.ds(low, count), at], s_d.at[there, at], sem_d.at[i])

        loop(hidden // BROAD, feed)

        def finish(i, carry):
            at = part(i, 64)
            branch = v_acc[at, :]
            output = v_h[at, :] + branch
            v_z[at, :] = output.astype(bf16)
            mask = valid(i, 64)
            return (carry[0] + square(output, mask), carry[1] + square(branch, mask))

        sums_two = lax.fori_loop(low // 64, high // 64, finish, (nothing, nothing), unroll=2)
        send(v_z.at[pl.ds(low, count)], z_out, 7)
        send(v_z.at[pl.ds(low, count)], layers.at[0, picked, 0, pl.ds(low, count)], 5)
        for k, value in enumerate((sums_one[0], sums_two[0], sums_one[1], sums_two[1])):
            squares_out[k] = value
        for copy in outs:
            copy.wait()
        for i in range(hidden // BROAD):
            g_copy(i).wait()
            d_copy(i).wait()
        if starts:
            p_copy(groups - 2).wait()
            p_copy(groups - 1).wait()

    @pl.when(jnp.logical_not(active))
    def _():
        squares_out[...] = jnp.zeros_like(squares_out)


def stash_shapes(rows, width, hidden):
    heads = width // HEAD
    return [
        jax.ShapeDtypeStruct((2 * rows, width), bf16),
        jax.ShapeDtypeStruct((2 * rows, width), bf16),
        jax.ShapeDtypeStruct((2 * rows, 3 * width), bf16),
        jax.ShapeDtypeStruct((2 * rows, width), bf16),
        jax.ShapeDtypeStruct((2 * rows, width), f32),
        jax.ShapeDtypeStruct((2 * rows, width), f32),
        jax.ShapeDtypeStruct((2 * rows, width), bf16),
        jax.ShapeDtypeStruct((2 * rows, hidden), bf16),
        jax.ShapeDtypeStruct((2 * rows, hidden), bf16),
        jax.ShapeDtypeStruct((2, heads, rows, rows), bf16),
        jax.ShapeDtypeStruct((1, 2, 1, rows, width), bf16),
    ]


def forward_call(slot, plan, stage, spans, norms, vectors, feat, recv, weights, stash=()):
    rows, width = feat.shape[2:]
    count = {BOTH: rows, FIRST: early_rows(rows), SECOND: rows - early_rows(rows)}[stage]
    hidden = weights[2].shape[1]
    any_ = pl.BlockSpec(memory_space=pl.ANY)
    vm = pl.BlockSpec(memory_space=pltpu.VMEM)
    shapes = stash_shapes(rows, width, hidden)
    results = pl.pallas_call(
        functools.partial(forward_kernel, slot, plan, stage, len(stash), len(recv)),
        in_specs=[pl.BlockSpec(memory_space=pltpu.SMEM), vm, vm] + [any_] * (5 + len(recv) + len(stash)),
        out_specs=[any_, vm] + [any_] * len(shapes),
        out_shape=[jax.ShapeDtypeStruct((count, width), bf16), jax.ShapeDtypeStruct((4, 8, width), f32)] + shapes,
        input_output_aliases={8 + len(recv) + k: 2 + k for k in range(len(stash))},
        scratch_shapes=[
            pltpu.VMEM(w.shape, bf16) for w in weights
        ] + [
            pltpu.VMEM((rows, width), bf16),
            pltpu.VMEM((rows, width), bf16),
            pltpu.VMEM((rows, 3 * width), bf16),
            pltpu.VMEM((rows, width), bf16),
            pltpu.VMEM((rows, width), f32),
            pltpu.VMEM((rows, width), f32),
            pltpu.VMEM((rows, width), bf16),
            pltpu.VMEM((rows, hidden), bf16),
            pltpu.VMEM((rows, hidden), bf16),
            pltpu.VMEM((2, 4, rows, rows), bf16),
            pltpu.VMEM((rows, rows), f32),
            pltpu.VMEM((rows, width), f32),
            pltpu.VMEM((rows, width), bf16),
            pltpu.SemaphoreType.DMA((4 + 2 * hidden // WIDE,)),
            pltpu.SemaphoreType.DMA((1,)),
            pltpu.SemaphoreType.DMA((10,)),
            pltpu.SemaphoreType.DMA((2,)),
            pltpu.SemaphoreType.DMA((hidden // WIDE,)),
            pltpu.SemaphoreType.DMA((hidden // WIDE,)),
        ],
        compiler_params=pltpu.CompilerParams(vmem_limit_bytes=VMEM),
        cost_estimate=pl.CostEstimate(flops=LARGE, bytes_accessed=1, transcendentals=0),
        name="layer_forward",
    )(spans, norms, vectors, feat, *weights, *recv, *stash)
    return results[0], results[1], results[2:]


def backward_kernel(slot, plan, stage, aliased, given, *refs):
    feeds, attends = stage != SECOND, stage != FIRST
    spans, norms, cot, recv, w_in, w_out, w_up, w_down = refs[:8]
    s_x, s_qkv, s_c, s_l, s_h, s_d, s_p = refs[8:15]
    if stage == SECOND:
        mid_in, middle_in = refs[15:17]
    refs = refs[15 + given + aliased :]
    smalls = refs[0]
    refs = refs[1:]
    if feeds:
        g_up, g_mid = refs[:2]
        refs = refs[2:]
    if attends:
        dx_out, g_qkv, inputs = refs[:3]
        refs = refs[3:]
    if stage == BOTH:
        g_feed = refs[0]
        refs = refs[1:]
    if stage == FIRST:
        middle_out = refs[0]
        refs = refs[1:]
    (v_in, v_out, v_up, v_down, v_x, v_dy, v_qkv, v_c, v_l, v_h, v_d, v_p, v_du, v_do, v_dc, v_dqkv, v_acc,
     v_s, v_k, v_dx, sem_w, sem_x, sem_d, sem_p, sem_o) = refs
    rows, width = v_x.shape
    hidden = v_up.shape[1]
    here = pl.ds(slot * rows, rows)
    tiles = hidden // WIDE

    first = lax.axis_index("section") == 0
    active, picked = chosen_tick(first, plan)

    def norm(k):
        return norms[:, k * width : (k + 1) * width]

    @pl.when(active)
    def _():
        length = spans[picked]
        if stage != BOTH:
            smalls[...] = jnp.zeros_like(smalls)

        if feeds:

            @pl.when(jnp.logical_not(first))
            def _():
                pltpu.make_async_copy(cot.at[picked, 0], v_dy, sem_x.at[0]).start()

            @pl.when(first)
            def _():
                pltpu.make_async_copy(recv, v_dy, sem_x.at[0]).start()

        def down_copy(i):
            return pltpu.make_async_copy(
                w_down.at[part(i, WIDE)], v_down.at[part(i, WIDE)], sem_w.at[i]
            )

        def up_copy(i):
            at = part(i, WIDE)
            return pltpu.make_async_copy(w_up.at[:, at], v_up.at[:, at], sem_w.at[tiles + i])

        def d_copy(i):
            return pltpu.make_async_copy(
                s_d.at[here, part(i, WIDE)], v_d.at[i % 2], sem_d.at[i % 2]
            )

        def p_copy(i):
            return pltpu.make_async_copy(
                s_p.at[slot, pl.ds(i * 4, 4)], v_p.at[i % 2], sem_p.at[i % 2]
            )

        loads = copies(
            [
                (s_x.at[here], v_x),
                (s_qkv.at[here], v_qkv),
                (s_c.at[here], v_c),
                (s_l.at[here], v_l),
                (s_h.at[here], v_h),
                (w_out, v_out),
                (w_in, v_in),
            ],
            sem_x.at[pl.ds(1, 7)],
        )
        if feeds:
            d_copy(0).start()
            for i in range(tiles):
                down_copy(i).start()
                up_copy(i).start()
                if i == 0:
                    d_copy(1).start()
            loads[4].start()
        if stage == SECOND:
            entries = [
                pltpu.make_async_copy(mid_in.at[here], v_do, sem_o.at[0]),
                pltpu.make_async_copy(middle_in, v_acc, sem_o.at[3]),
            ]
            for copy in entries:
                copy.start()
        def enter_attention():
            for k in (5, 1, 2, 3):
                loads[k].start()
            p_copy(0).start()
            p_copy(1).start()

        def enter_last():
            loads[6].start()
            loads[0].start()

        if stage == SECOND:
            enter_attention()
            enter_last()
        nothing = jnp.zeros((8, width), f32)

        def fold(values):
            return jnp.sum(values.reshape(-1, 8, width), axis=0)

        def enter(i, total):
            at = part(i, 64)
            place = lax.broadcasted_iota(jnp.int32, (64, 1), 0) + i * 64
            masked = jnp.where(place < length, v_dy[at, :].astype(f32), 0.0)
            v_dy[at, :] = masked.astype(bf16)
            v_acc[at, :] = jnp.zeros((64, width), f32)
            return total + fold(masked)

        if feeds:
            pltpu.make_async_copy(recv, v_dy, sem_x.at[0]).wait()
            total = lax.fori_loop(0, rows // 64, enter, nothing, unroll=2)
            smalls[7:8, :] = jnp.sum(total, axis=0, keepdims=True)
        if stage == BOTH:
            feed_copy = pltpu.make_async_copy(v_dy, g_feed.at[here], sem_o.at[4])
            feed_copy.start()

        def feed(i):
            down_copy(i).wait()
            up_copy(i).wait()
            d_copy(i).wait()
            if stage == BOTH:
                pl.when(i == tiles - 2)(enter_attention)
                pl.when(i == tiles - 1)(enter_last)
            at = part(i, WIDE)
            pre = (nt(v_dy[...], v_down[at, :]) * v_d[i % 2].astype(f32)).astype(bf16)
            v_du[:, at] = pre
            v_acc[...] += nt(pre, v_up[:, at])
            smalls[pl.ds(8 + i, 1), :] = jnp.sum(v_du[:, at].astype(f32), axis=0, keepdims=True)
            pltpu.make_async_copy(v_du.at[:, at], g_up.at[here, at], sem_o.at[3]).start()

            @pl.when(i + 2 < tiles)
            def _():
                d_copy(i + 2).start()

        if feeds:
            loop(tiles, feed)
            loads[4].wait()

        def norm_back(source, grad, gain):
            normed, inverse = row_stats(source)
            scaled = grad * gain
            mean_one = jnp.mean(scaled, axis=-1, keepdims=True)
            mean_two = jnp.mean(scaled * normed, axis=-1, keepdims=True)
            return inverse * (scaled - mean_one - normed * mean_two), fold(grad * normed), fold(grad)

        def second_norm(i, carry):
            at = part(i, 64)
            rows_back, one, two = norm_back(v_h[at, :], v_acc[at, :], norm(2))
            middle = rows_back + v_dy[at, :].astype(f32)
            v_acc[at, :] = middle
            low = middle.astype(bf16)
            v_do[at, :] = low
            return carry[0] + one, carry[1] + two, carry[2] + fold(low.astype(f32))

        if feeds:
            sums = lax.fori_loop(0, rows // 64, second_norm, (nothing,) * 3, unroll=2)
            for k, value in zip((2, 3, 6), sums):
                smalls[k : k + 1, :] = jnp.sum(value, axis=0, keepdims=True)
            outs = [pltpu.make_async_copy(v_do, g_mid.at[here], sem_o.at[0])]
            if stage == FIRST:
                outs.append(pltpu.make_async_copy(v_acc, middle_out, sem_o.at[1]))
            for copy in outs:
                copy.start()
        if stage == SECOND:
            for copy in entries:
                copy.wait()
        if attends:
            loads[5].wait()
            v_dc[...] = nt(v_do[...], v_out[...]).astype(bf16)
            for k in (1, 2, 3):
                loads[k].wait()
        lane = lax.broadcasted_iota(jnp.int32, (1, GROUP), 1) // HEAD

        def attend(i):
            p_copy(i).wait()
            at = part(i, GROUP)
            key_at = pl.ds(pl.multiple_of(width + i * GROUP, GROUP), GROUP)
            value_at = pl.ds(pl.multiple_of(2 * width + i * GROUP, GROUP), GROUP)
            key = v_qkv[:, key_at]
            value = v_qkv[:, value_at]
            query = v_qkv[:, at]
            wide = v_dc[:, at].astype(f32) * v_l[:, at]
            low = wide.astype(bf16)
            dots = wide * v_c[:, at].astype(f32)
            for h in range(4):
                hs = slice(h * rows, (h + 1) * rows)
                v_k[hs, :] = jnp.where(lane == h, key, 0).astype(bf16)
                masked = jnp.where(lane == h, low, 0).astype(bf16)
                delta = jnp.sum(jnp.where(lane == h, dots, 0.0), axis=-1, keepdims=True)
                inner = nt(masked, value) - delta
                v_s[:, hs] = (v_p[i % 2, h].astype(f32) * inner).astype(bf16)
            grad_query = (nn(v_s[...], v_k[...]) * score_scale).astype(bf16)
            query_t = query.T
            low_t = low.T
            keys, values = [], []
            for h in range(4):
                hs = slice(h * HEAD, (h + 1) * HEAD)
                keys.append(nn(query_t[hs], v_s[:, h * rows : (h + 1) * rows]))
                values.append(nn(low_t[hs], v_p[i % 2, h]))
            grad_key = (jnp.concatenate(keys, axis=0) * score_scale).astype(bf16).T
            grad_value = jnp.concatenate(values, axis=0).astype(bf16).T
            v_dqkv[:, at] = grad_query
            v_dqkv[:, key_at] = grad_key
            v_dqkv[:, value_at] = grad_value
            smalls[4:5, at] = jnp.sum(grad_query.astype(f32), axis=0, keepdims=True)
            smalls[5:6, at] = jnp.sum(grad_value.astype(f32), axis=0, keepdims=True)

            @pl.when(i + 2 < width // GROUP)
            def _():
                p_copy(i + 2).start()

        if attends:
            loop(width // GROUP, attend)
            qkv_copy = pltpu.make_async_copy(v_dqkv, g_qkv.at[here], sem_o.at[1])
            qkv_copy.start()
            loads[6].wait()
            loads[0].wait()

            v_h[...] = nt(v_dqkv[...], v_in[...])

        def first_norm(i, carry):
            at = part(i, 64)
            rows_back, one, two = norm_back(v_x[at, :].astype(f32), v_h[at, :], norm(0))
            v_dx[at, :] = (rows_back + v_acc[at, :]).astype(bf16)
            return carry[0] + one, carry[1] + two

        if attends:
            sums = lax.fori_loop(0, rows // 64, first_norm, (nothing,) * 2, unroll=2)
            for k, value in enumerate(sums):
                smalls[k : k + 1, :] = jnp.sum(value, axis=0, keepdims=True)
            dx_copy = pltpu.make_async_copy(v_dx, dx_out, sem_o.at[2])
            dx_copy.start()
            input_copy = pltpu.make_async_copy(v_dx, inputs.at[0, picked, 0], sem_o.at[5])
            input_copy.start()
            for copy in (qkv_copy, dx_copy, input_copy):
                copy.wait()
        if stage == BOTH:
            feed_copy.wait()
        if feeds:
            for copy in outs:
                copy.wait()
            pltpu.make_async_copy(v_du, g_up.at[here], sem_o.at[3]).wait()

    @pl.when(jnp.logical_not(active))
    def _():
        smalls[...] = jnp.zeros_like(smalls)


def backward_call(slot, plan, stage, spans, norms, cot, recv, weights, stash, given, grads):
    rows, width = recv.shape
    hidden = weights[2].shape[1]
    any_ = pl.BlockSpec(memory_space=pl.ANY)
    vm = pl.BlockSpec(memory_space=pltpu.VMEM)
    shape = jax.ShapeDtypeStruct
    outs = {"smalls": shape((8 + hidden // WIDE, width), f32)}
    if stage != SECOND:
        outs["up"] = shape((2 * rows, hidden), bf16)
        outs["mid"] = shape((2 * rows, width), bf16)
    if stage != FIRST:
        outs["dx"] = shape((rows, width), bf16)
        outs["qkv"] = shape((2 * rows, 3 * width), bf16)
        outs["inputs"] = shape((1, 2, 1, rows, width), bf16)
    if stage == BOTH:
        outs["feed"] = shape((2 * rows, width), bf16)
    if stage == FIRST:
        outs["middle"] = shape((rows, width), f32)
    names = list(outs)
    kept = [name for name in names if name in grads and name not in ("smalls", "dx")]
    s_x, s_a, s_qkv, s_c, s_l, s_h, s_b, s_g, s_d, s_p, _ = stash
    results = pl.pallas_call(
        functools.partial(backward_kernel, slot, plan, stage, len(kept), len(given)),
        in_specs=[pl.BlockSpec(memory_space=pltpu.SMEM), vm] + [any_] * (13 + len(given) + len(kept)),
        out_specs=[vm] + [any_] * (len(names) - 1),
        out_shape=list(outs.values()),
        input_output_aliases={15 + len(given) + k: names.index(n) for k, n in enumerate(kept)},
        scratch_shapes=[pltpu.VMEM(w.shape, bf16) for w in weights] + [
            pltpu.VMEM((rows, width), bf16),
            pltpu.VMEM((rows, width), bf16),
            pltpu.VMEM((rows, 3 * width), bf16),
            pltpu.VMEM((rows, width), bf16),
            pltpu.VMEM((rows, width), f32),
            pltpu.VMEM((rows, width), f32),
            pltpu.VMEM((2, rows, WIDE), bf16),
            pltpu.VMEM((2, 4, rows, rows), bf16),
            pltpu.VMEM((rows, hidden), bf16),
            pltpu.VMEM((rows, width), bf16),
            pltpu.VMEM((rows, width), bf16),
            pltpu.VMEM((rows, 3 * width), bf16),
            pltpu.VMEM((rows, width), f32),
            pltpu.VMEM((rows, 4 * rows), bf16),
            pltpu.VMEM((4 * rows, GROUP), bf16),
            pltpu.VMEM((rows, width), bf16),
            pltpu.SemaphoreType.DMA((2 * hidden // WIDE,)),
            pltpu.SemaphoreType.DMA((8,)),
            pltpu.SemaphoreType.DMA((2,)),
            pltpu.SemaphoreType.DMA((2,)),
            pltpu.SemaphoreType.DMA((6,)),
        ],
        compiler_params=pltpu.CompilerParams(vmem_limit_bytes=VMEM),
        cost_estimate=pl.CostEstimate(flops=LARGE, bytes_accessed=1, transcendentals=0),
        name="layer_backward",
    )(
        spans, norms, cot, recv, *weights, s_x, s_qkv, s_c, s_l, s_h, s_d, s_p, *given,
        *[grads[name] for name in kept],
    )
    return {**grads, **dict(zip(names, results))}


def turn_kernel(blocks, *refs):
    count = len(blocks)
    for k, block in enumerate(blocks):
        source, target = refs[k], refs[count + k]

        @pl.when((pl.program_id(0) == k) if k + 1 < count else (pl.program_id(0) >= k))
        def _(source=source, target=target, block=block):
            flat = source[...].T
            pairs = flat.shape[0] // (2 * block)
            for core in range(2):

                @pl.when(lax.axis_index("dp") % 2 == core)
                def _(core=core):
                    for j in range(pairs):
                        at = slice(j * block, (j + 1) * block)
                        other = (2 * j + 1 - core) * block
                        own = (2 * j + core) * block
                        target[0, at, :] = flat[other : other + block]
                        target[1, at, :] = flat[own : own + block]


def turn_call(sources):
    rows = sources[0].shape[0]
    count = len(sources)
    size = lax.axis_size("dp")
    steps = count - 1 + sources[-1].shape[1] // WIDE

    def last(i):
        return jnp.maximum(i - (count - 1), 0)

    ins = [pl.BlockSpec((rows, WIDE), lambda i: (0, 0))] * (count - 1)
    ins.append(pl.BlockSpec((rows, WIDE), lambda i: (0, last(i))))
    outs = [pl.BlockSpec((2, WIDE // 2, rows), lambda i: (0, 0, 0))] * (count - 1)
    outs.append(pl.BlockSpec((2, WIDE // 2, rows), lambda i: (0, last(i), 0)))
    return pl.pallas_call(
        functools.partial(turn_kernel, [s.shape[1] // size for s in sources]),
        grid=(steps,),
        in_specs=ins,
        out_specs=outs,
        out_shape=[jax.ShapeDtypeStruct((2, s.shape[1] // 2, rows), bf16) for s in sources],
        compiler_params=pltpu.CompilerParams(vmem_limit_bytes=VMEM),
        cost_estimate=pl.CostEstimate(flops=1, bytes_accessed=1, transcendentals=0),
        name="turn",
    )(*sources)


def weight_kernel(widths, half, left, right, *rest):
    late, outs = rest[: -len(widths)], rest[-len(widths) :]
    if late:
        rows = late[0].shape[0]
        second = jnp.where(lax.axis_index("section") == 0, late[0][...], right[rows:, :])
        total = nn(left[0, :, :rows], right[:rows, :]) + nn(left[0, :, rows:], second)
    else:
        total = nn(left[0], right[...])
    total = total.astype(bf16)
    at = 0
    for width, out in zip(widths, outs):
        step, offset = divmod(at, right.shape[1])
        if len(widths) == 1:
            out[...] = total
        else:

            @pl.when(pl.program_id(1) == step)
            def _(out=out, cut=slice(offset, offset + width)):
                out[...] = total[:, cut]

        at += width


def weight_call(left, right, start, widths, half, late=None):
    _, height, rows = left.shape
    columns = sum(widths)
    tall = min(height, 512)
    wide = min(columns, WIDE)
    specs = [
        pl.BlockSpec((1, tall, rows), lambda i, j: (half, i, 0)),
        pl.BlockSpec((rows, wide), lambda i, j: (0, start // wide + j)),
    ]
    operands = (left, right)
    if late is not None:
        specs.append(pl.BlockSpec((rows // 2, wide), lambda i, j: (0, j)))
        operands += (late,)

    def out(width):
        if width > wide:
            return pl.BlockSpec((tall, wide), lambda i, j: (i, j))
        return pl.BlockSpec((tall, width), lambda i, j: (i, 0))

    return pl.pallas_call(
        functools.partial(weight_kernel, widths, half),
        grid=(height // tall, columns // wide),
        in_specs=specs,
        out_specs=[out(width) for width in widths],
        out_shape=[jax.ShapeDtypeStruct((height, width), bf16) for width in widths],
        compiler_params=pltpu.CompilerParams(vmem_limit_bytes=VMEM),
        cost_estimate=pl.CostEstimate(flops=1, bytes_accessed=1, transcendentals=0),
        name="weight_product",
    )(*operands)


def sum_kernel(layout, lefts, fixed, free, place, *refs):
    count = sum(len(arrays) for arrays in layout)
    sources = iter(refs[:count])
    terms = [[next(sources) for _ in arrays] for arrays in layout]
    out, held, total, sem, out_sem = refs[-5:]
    me = lax.axis_index("dp")
    cells = list(itertools.product(range(2), repeat=len(free)))
    loads, slot = [], 0
    for cell in cells:
        loads.append([])
        for arrays, left, widths in zip(terms, lefts, layout):
            index = []
            for bit in left:
                if bit in free:
                    index.append(cell[free.index(bit)])
                else:
                    own = (me >> bit) & 1
                    index.append(own if fixed[bit] else 1 - own)
            at = 0
            for ref, (start, width) in zip(arrays, widths):
                copy = pltpu.make_async_copy(
                    ref.at[(*index, slice(None), pl.ds(start, width))],
                    held.at[slot, :, pl.ds(at, width)],
                    sem.at[len(loads[-1]), len(loads) - 1],
                )
                copy.start()
                loads[-1].append(copy)
                at += width
            slot += 1
    stores = []
    for k, cell in enumerate(cells):
        for copy in loads[k]:
            copy.wait()
        value = added([held[k * len(terms) + j] for j in range(len(terms))])
        total[k] = value.astype(total.dtype)
        stores.append(pltpu.make_async_copy(total.at[k], place(out, cell), out_sem.at[k]))
        stores[-1].start()
    for copy in stores:
        copy.wait()


def sum_call(terms, fixed, kind, into=None, start=0):
    rows = terms[0][0][0][0].shape[-2]
    layout = [[(at, width) for _, at, width in arrays] for arrays, _ in terms]
    lefts = [left for _, left in terms]
    columns = sum(width for _, width in layout[0])
    free = [bit for bit in lefts[0] if bit not in fixed]
    operands = [array for arrays, _ in terms for array, _, _ in arrays]
    cells = 2 ** len(free)
    aliases = {}
    wide = 0
    if into is None:
        shape = jax.ShapeDtypeStruct((2,) * len(free) + (rows, columns), kind)
    else:
        wide, into = into
        shape = jax.ShapeDtypeStruct((1, rows, wide), kind)
        if into is not None:
            aliases = {len(operands): 0}
            operands.append(into)

    given = len(operands)

    def place(out, cell):
        if wide:
            return out.at[0, :, pl.ds(start, columns)]
        return out.at[cell] if cell else out

    def kernel(*refs):
        refs = refs[: given - len(aliases)] + refs[given:]
        sum_kernel(layout, lefts, fixed, free, place, *refs)

    any_ = pl.BlockSpec(memory_space=pl.ANY)
    return pl.pallas_call(
        kernel,
        in_specs=[any_] * len(operands),
        out_specs=any_,
        out_shape=shape,
        input_output_aliases=aliases,
        scratch_shapes=[
            pltpu.VMEM((cells * len(terms), rows, columns), terms[0][0][0][0].dtype),
            pltpu.VMEM((cells, rows, columns), kind),
            pltpu.SemaphoreType.DMA((max(sum(len(arrays) for arrays, _ in terms), 1), cells)),
            pltpu.SemaphoreType.DMA((cells,)),
        ],
        compiler_params=pltpu.CompilerParams(
            vmem_limit_bytes=VMEM if len(free) > 1 or rows > columns // 8 else LESS
        ),
        cost_estimate=pl.CostEstimate(flops=SMALL, bytes_accessed=1, transcendentals=0),
        name="sum_terms",
    )(*operands)


highest = lax.Precision.HIGHEST


def added(terms):
    total = terms[0].astype(f32)
    for term in terms[1:]:
        total = total + term.astype(f32)
    return total


class Line:
    def __init__(self):
        self.last = None

    def after(self, values):
        if self.last is not None:
            values = lax.optimization_barrier(tuple(values) + (self.last,))[:-1]
        return list(values)

    def done(self, value):
        self.last = value


class Exchange:
    def __init__(self, line, terms, left, order):
        self.line = line
        self.terms = [(arrays, sorted(left, reverse=True)) for arrays in terms]
        self.fixed = {}
        self.order = list(order)
        self.kind = terms[0][0][0].dtype

    def total(self, fixed, kind, **where):
        values = iter(self.line.after([array for arrays, _ in self.terms for array, _, _ in arrays]))
        self.terms = [
            ([(next(values), at, width) for _, at, width in arrays], left)
            for arrays, left in self.terms
        ]
        total = sum_call(self.terms, fixed, kind, **where)
        self.line.done(total)
        return total

    def step(self):
        bit = self.order.pop(0)
        theirs = self.total({**self.fixed, bit: False}, self.kind)
        self.fixed[bit] = True
        left = [k for k in self.terms[0][1] if k not in self.fixed]
        self.terms.append((whole(crossed(theirs, bit)), left))

    def cut(self, widths):
        parts = []
        low = 0
        for width in widths:
            high = low + width
            terms = []
            for arrays, left in self.terms:
                chosen, at = [], 0
                for array, start, columns in arrays:
                    a, b = max(low, at), min(high, at + columns)
                    if a < b:
                        chosen.append((array, start + a - at, b - a))
                    at += columns
                terms.append((chosen, left))
            part_ = Exchange(self.line, [terms[0][0]], (), self.order)
            part_.terms = terms
            part_.fixed = dict(self.fixed)
            parts.append(part_)
            low = high
        return parts

    def finish(self, **where):
        while self.order:
            self.step()
        return self.total(self.fixed, f32, **where)


def crossed(value, bit):
    return lax.ppermute(value, "dp", [(i, i ^ (1 << bit)) for i in range(lax.axis_size("dp"))])


def whole(array):
    return [(array, 0, array.shape[-1])]


def whole(array):
    return [(array, 0, array.shape[-1])]


class WeightSum(Exchange):
    def __init__(self, line, left, right, start, widths, order, late=None):
        size = lax.axis_size("dp")
        bits = size.bit_length() - 1
        shape = [2] * (bits - 1) + [2 * left.shape[1] // size, -1]
        left, right = line.after((left, right))
        theirs = weight_call(left, right, start, widths, 0, late)
        line.done(theirs[-1])
        received = [whole(crossed(array, 0).reshape(shape)) for array in theirs]
        self.product = (left, right, start, [sum(widths)], 1, late)
        self.shape = shape
        super().__init__(line, (sum(received, []),), range(1, bits), order)

    def own(self):
        left, right = self.line.after(self.product[:2])
        (mine,) = weight_call(left, right, *self.product[2:])
        self.line.done(mine)
        self.terms.append((whole(mine.reshape(self.shape)), self.terms[0][1]))
        return self


def shards(
    features,
    cotangent,
    lengths,
    codebook_index,
    attention_in,
    attention_out,
    feed_up,
    feed_down,
    vectors,
    adaptive_weight,
    codebook_table,
):
    is_first = lax.axis_index("section") == 0
    adaptive = jnp.where(is_first, 0.0, 1.0)
    rows, width = features.shape[2:]
    hidden = feed_up.shape[2]
    size = lax.axis_size("dp")
    bits = size.bit_length() - 1
    weights = (attention_in[0], attention_out[0], feed_up[0], feed_down[0])

    def send(value, to):
        return lax.ppermute(value, "section", [(1 - to, to)])

    spans = lengths[:, 0]

    def forward(slot, plan, norms, recv, stash=(), stage=BOTH):
        return forward_call(
            slot, plan, stage, spans, norms, vectors, features, recv, weights, stash
        )

    def backward(slot, plan, stage, norms, recv, stash, grads, given=()):
        return backward_call(
            slot, plan, stage, spans, norms, cotangent, recv, weights, stash, given, grads
        )

    z_one, squares_one, stash = forward(0, (0, None), vectors, ())
    received_one = (send(z_one, 1),)
    table, z_one = lax.optimization_barrier((codebook_table, z_one))
    condition_table = jnp.dot(table, adaptive_weight, preferred_element_type=f32)
    one_hot = (
        codebook_index[:, 0][:, None]
        == jnp.arange(codebook_table.shape[0], dtype=jnp.int32)[None, :]
    ).astype(f32)
    norms = vectors[:, : 4 * width] + adaptive * jnp.dot(
        one_hot, condition_table, precision=highest
    )
    norms_one, norms_two = norms[:1], norms[1:]
    z_two, squares_two, stash = forward(1, (1, 0), norms_one, received_one, stash)
    received_two = send(z_two, 1)
    grads = backward(1, (None, 0), BOTH, norms_one, z_two, stash, {})
    smalls_one = grads["smalls"]
    back_one = send(grads["dx"], 0)
    z_three, squares_three, stash = forward(0, (None, 1), norms_two, (received_two,), stash)
    grads = backward(0, (0, 1), BOTH, norms_two, back_one, stash, grads)
    smalls_two = grads["smalls"]
    back_two = send(grads["dx"], 0)

    s_x, s_a, s_qkv, s_c, s_l, s_h, s_b, s_g, s_d, s_p, layer_outputs = stash
    side_first = list(range(1, bits))
    line_first = side_first[1:] + side_first[:1]
    line = Line()
    line.done(smalls_two)
    squares = jnp.sum(squares_one + squares_two + squares_three, axis=(1, 2))
    counted = jnp.sum(lengths).astype(f32)
    (totals,) = line.after((jnp.concatenate([squares, counted[None], jnp.zeros((123,), f32)]),))
    for bit in range(bits):
        totals = totals + crossed(totals, bit)
    t_a, t_b, t_c, t_g = turn_call(line.after((s_a, s_b, s_c, s_g)))
    line.done(t_a)
    (totals,) = line.after((totals,))
    line.done(totals)
    down = WeightSum(line, t_g, grads["feed"], 0, [width], side_first, back_two).own()
    down.step()
    (back_two,) = line.after((back_two,))
    grads = backward(1, (1, None), FIRST, vectors, back_two, stash, grads)
    smalls_three = grads["smalls"]
    line.done(smalls_three)
    up = WeightSum(line, t_b, grads["up"], 0, [WIDE] * (hidden // WIDE), side_first).own()
    up.step()
    down.step()
    out = WeightSum(line, t_c, grads["mid"], 0, [width], side_first).own()
    (middle,) = line.after((grads["middle"],))
    grads = backward(
        1, (1, None), SECOND, vectors, back_two, stash, grads, (grads["mid"], middle)
    )
    smalls_four = grads["smalls"]
    line.done(smalls_four)
    g_qkv, input_grads = grads["qkv"], grads["inputs"]
    down.step()
    into_one = WeightSum(line, t_a, g_qkv, 0, [width] * 3, side_first).own()

    smalls = smalls_one + smalls_two + smalls_three + smalls_four
    table_grad = one_hot[0][:, None] * smalls_one[:4].reshape(1, -1) + one_hot[1][:, None] * (
        smalls_two[:4].reshape(1, -1) * adaptive
    )
    codes = table_grad.shape[0]
    share = table_grad.shape[1] // (2 * size)
    table_blocks = table_grad.reshape(codes, 2, size, share).transpose(2, 1, 0, 3)
    packed = jnp.concatenate([smalls.reshape(size, -1), table_blocks.reshape(size, -1)], axis=1)
    count = packed.shape[1]
    block = width // size
    packed = jnp.pad(packed.reshape(size, block, -1), ((0, 0), (0, 0), (0, 128 - count // block)))
    packed = packed.astype(bf16).reshape([2] * bits + [block, 128])
    core = lax.axis_index("dp") & 1
    (other, own) = [
        lax.dynamic_index_in_dim(packed, which, bits - 1, keepdims=False)
        for which in (1 - core, core)
    ]
    other = crossed(other, 0)
    into_one, into_two = into_one.cut([2 * width, width])
    up_one, up_two = up.cut([hidden // 2] * 2)
    into_two.terms = [
        (arrays + whole(extra), left)
        for (arrays, left), extra in zip(into_two.terms, (other, own))
    ]
    into_one.step()
    up_one.step()
    up_two.step()
    into_two.step()
    out.step()
    down = down.finish(into=(width, None))
    up_one.step()
    into_one.step()
    up_two.step()
    into_two.step()
    up = up_one.finish(into=(hidden, None))
    into_one.step()
    out.step()
    up = up_two.finish(into=(hidden, up), start=hidden // 2)
    into_two.step()
    into = into_one.finish(into=(3 * width, None))
    out.step()
    last = into_two.finish()
    out = out.finish(into=(width, None))
    into = lax.dynamic_update_slice(into, last[None, :, :width], (0, 0, 2 * width))
    small_sum = last[:, width : width + count // block].reshape(-1)
    vector_share = small_sum[: smalls.size // size]
    table_share = small_sum[smalls.size // size :].reshape(2, codes, share)
    table_own = jnp.where(is_first, send(table_share[0], 0), table_share[1])
    grad_adaptive = lax.dot_general(
        codebook_table.astype(f32),
        table_own,
        (((0,), (0,)), ((), ())),
        precision=highest,
        preferred_element_type=f32,
    )
    residual_rms = jnp.sqrt(totals[:4] / (totals[4] * width))[None]

    return (
        layer_outputs,
        input_grads,
        into,
        out,
        up,
        down,
        vector_share[None],
        grad_adaptive,
        residual_rms,
    )


def solution(mesh):
    placed = (
        P(None, "dp", None, None),
        P(None, "dp", None, None),
        P(None, "dp"),
        P(None, "dp"),
        P("section", None, None),
        P("section", None, None),
        P("section", None, None),
        P("section", None, None),
        P("section", None),
        P(),
        P(),
    )
    return jax.shard_map(
        shards,
        mesh=mesh,
        in_specs=placed,
        out_specs=(
            P("section", None, "dp", None, None),
            P("section", None, "dp", None, None),
            P("section", "dp", None),
            P("section", "dp", None),
            P("section", "dp", None),
            P("section", "dp", None),
            P("section", "dp"),
            P(None, ("section", "dp")),
            P("section", None),
        ),
        check_vma=False,
    )
```

```python
import functools
import itertools

import jax
import jax.numpy as jnp
from jax import lax
from jax.experimental import pallas as pl
from jax.experimental.pallas import tpu as pltpu
from jax.sharding import PartitionSpec as P

HEAD = 64
norm_eps = 1e-05
root_half = 0.7071067811865476
slope_scale = 0.3989422804014327
score_scale = 0.125
big_negative = -1e30
f32 = jnp.float32
bf16 = jnp.bfloat16
GROUP = 4 * HEAD
TILE = 512
WIDE = 1024
BROAD = 2048
VMEM = 62 * 2**20
SMALL = 10**6
LARGE = 10**11
BOTH, FIRST, SECOND = range(3)
LESS = 16 * 2**20


def nn(a, b):
    return lax.dot_general(a, b, (((1,), (0,)), ((), ())), preferred_element_type=f32)


def nt(a, b):
    return lax.dot_general(a, b, (((1,), (1,)), ((), ())), preferred_element_type=f32)


def row_stats(rows):
    average = jnp.mean(rows, axis=-1, keepdims=True)
    centered = rows - average
    inverse = lax.rsqrt(jnp.mean(centered * centered, axis=-1, keepdims=True) + norm_eps)
    return centered * inverse, inverse


def gate(values):
    bell = jnp.exp(-0.5 * values * values)
    upper = 0.5 * (1.0 + lax.erf(values * root_half))
    return values * upper, upper + values * bell * slope_scale


def loop(count, body, unroll=1):
    def run(i, carry):
        body(i)
        return carry

    lax.fori_loop(0, count, run, 0, unroll=unroll)


def part(i, size):
    return pl.ds(pl.multiple_of(i * size, size), size)


def copies(pairs, sem):
    return [pltpu.make_async_copy(a, b, sem.at[i]) for i, (a, b) in enumerate(pairs)]


def chosen_tick(first, plan):
    picked = jnp.where(first, plan[0] or 0, plan[1] or 0)
    active = jnp.where(first, int(plan[0] is not None), int(plan[1] is not None)) == 1
    return active, picked


def early_rows(rows):
    return 3 * rows // 4


def forward_kernel(slot, plan, stage, aliased, pieces, *refs):
    starts, ends = stage != SECOND, stage != FIRST
    spans, norms, vectors, feat, w_in, w_out, w_up, w_down = refs[:8]
    recv = refs[8 : 8 + pieces]
    refs = refs[8 + pieces :]
    kept = refs[:aliased]
    refs = refs[aliased:]
    z_out, squares_out = refs[:2]
    s_x, s_a, s_qkv, s_c, s_l, s_h, s_b, s_g, s_d, s_p, layers = refs[2:13]
    (v_in, v_out, v_up, v_down, v_x, v_a, v_qkv, v_c, v_l, v_h, v_b, v_g, v_d, v_p, v_bias, v_acc, v_z,
     sem_w, sem_x, sem_o, sem_p, sem_g, sem_d) = refs[13:]
    rows, width = v_x.shape
    hidden = v_up.shape[1]
    here = pl.ds(slot * rows, rows)
    first = lax.axis_index("section") == 0
    active, picked = chosen_tick(first, plan)

    def norm(k):
        return norms[:, k * width : (k + 1) * width]

    def bias(k):
        return vectors[:, k * width : (k + 1) * width]

    @pl.when(active)
    def _():
        length = spans[picked]
        causal = first

        loaded = pltpu.make_async_copy(feat.at[picked, 0], v_x, sem_x.at[0])
        if starts:
            pl.when(first)(loaded.start)

            @pl.when(jnp.logical_not(first))
            def _():
                at = 0
                for piece in recv:
                    pltpu.make_async_copy(
                        piece, v_x.at[pl.ds(at, piece.shape[0])], sem_x.at[0]
                    ).start()
                    at += piece.shape[0]

        def column(source, target, index, size):
            def at(i):
                return pltpu.make_async_copy(
                    source.at[:, part(i, size)], target.at[:, part(i, size)], sem_w.at[index + i]
                )

            return at

        def down_copy(i):
            return pltpu.make_async_copy(
                w_down.at[part(i, BROAD)], v_down.at[part(i, BROAD)], sem_w.at[3 + 1 + hidden // BROAD + i]
            )

        in_copy = column(w_in, v_in, 0, WIDE)
        out_copy = column(w_out, v_out, 3, WIDE)
        up_copy = column(w_up, v_up, 4, BROAD)
        if starts:
            for i in range(3):
                in_copy(i).start()

        outs = []

        def send(source, target, index):
            copy = pltpu.make_async_copy(source, target, sem_o.at[index])
            copy.start()
            outs.append(copy)

        valid = lambda i, n: (lax.broadcasted_iota(jnp.int32, (n, 1), 0) + i * n < length).astype(f32)

        def square(values, mask):
            return jnp.sum((values * values * mask).reshape(-1, 8, width), axis=0)

        nothing = jnp.zeros((8, width), f32)
        sums_one = (nothing, nothing)
        groups = width // GROUP

        def p_copy(i):
            return pltpu.make_async_copy(
                v_p.at[i % 2], s_p.at[slot, pl.ds(i * 4, 4)], sem_p.at[i % 2]
            )

        def start_feed():
            for i in range(hidden // BROAD):
                up_copy(i).start()
                down_copy(i).start()

        half = rows // 2
        low = early_rows(rows) if stage == SECOND else 0
        high = early_rows(rows) if stage == FIRST else rows
        these = slice(low, high)
        count = high - low
        there = pl.ds(slot * rows + low, count)
        if stage == SECOND:
            start_feed()
            entries = [
                pltpu.make_async_copy(kept[5].at[there], v_h.at[pl.ds(low, count)], sem_o.at[0]),
                pltpu.make_async_copy(kept[6].at[there], v_b.at[pl.ds(low, count)], sem_o.at[1]),
            ]
            for copy in entries:
                copy.start()
            for copy in entries:
                copy.wait()
            v_acc[these, :] = jnp.broadcast_to(bias(7), (count, width))
        if starts:
            def bias_rows(i):
                at = part(i, 128)
                query = lax.broadcasted_iota(jnp.int32, (128, rows), 0) + i * 128
                key = lax.broadcasted_iota(jnp.int32, (128, rows), 1)
                open_ = (key < length) & ((key <= query) | jnp.logical_not(causal))
                v_bias[at, :] = jnp.where(open_, 0.0, big_negative)

            loop(rows // 128, bias_rows)
            loaded.wait()

            def first_norm(i):
                at = part(i, 64)
                normed, _ = row_stats(v_x[at, :].astype(f32))
                v_a[at, :] = (normed * norm(0) + norm(1)).astype(bf16)

            loop(rows // 64, first_norm, 2)
            send(v_x, s_x.at[here], 0)
            send(v_a, s_a.at[here], 1)
            def project(i):
                in_copy(i).wait()
                at = part(i, WIDE)
                shift = vectors[:, pl.ds(pl.multiple_of((4 + i // 2) * width, width), width)]
                tile = nn(v_a[...], v_in[:, at]) + jnp.where(i == 1, 0.0, shift)
                v_qkv[:, at] = tile.astype(bf16)

            loop(3 * width // WIDE, project)
            out_copy(0).start()
            start_feed()
            send(v_qkv, s_qkv.at[here], 2)
            lane = lax.broadcasted_iota(jnp.int32, (1, GROUP), 1) // HEAD

            def attend(i):
                at = part(i, GROUP)
                query = v_qkv[:, at]
                key = v_qkv[:, pl.ds(pl.multiple_of(width + i * GROUP, GROUP), GROUP)]
                value = v_qkv[:, pl.ds(pl.multiple_of(2 * width + i * GROUP, GROUP), GROUP)]

                @pl.when(i >= 2)
                def _():
                    p_copy(i - 2).wait()

                half = rows // 2

                def rows_part(r, keys):
                    picked_rows = slice(r * half, (r + 1) * half)
                    scaled = query[picked_rows] * score_scale
                    total = jnp.zeros((half, GROUP), f32)
                    sums = jnp.ones((half, GROUP), f32)
                    for h in range(4):
                        masked = jnp.where(lane == h, scaled, 0).astype(bf16)
                        scores = nt(masked, key[:keys]) + v_bias[picked_rows, :keys]
                        top = jnp.max(scores, axis=-1, keepdims=True)
                        raised = jnp.exp(scores - top).astype(bf16)
                        v_p[i % 2, h, picked_rows, :keys] = raised
                        if keys < rows:
                            v_p[i % 2, h, picked_rows, keys:] = jnp.zeros((half, rows - keys), bf16)
                        product = nn(raised, jnp.where(lane == h, value[:keys], 1).astype(bf16))
                        total = jnp.where(lane == h, product, total)
                        sums = jnp.where(lane == (h ^ 1), product, sums)
                    inverse = 1.0 / jnp.concatenate(
                        [pltpu.roll(sums[:, k : k + 128], HEAD, 1) for k in (0, 128)], axis=1
                    )
                    v_l[picked_rows, at] = inverse
                    v_c[picked_rows, at] = (total * inverse).astype(bf16)

                @pl.when(causal)
                def _():
                    rows_part(0, half)
                    rows_part(1, rows)

                @pl.when(jnp.logical_not(causal))
                def _():
                    rows_part(0, rows)
                    rows_part(1, rows)

                p_copy(i).start()

            loop(groups, attend)
            send(v_c, s_c.at[here], 8)
            send(v_l, s_l.at[here], 9)
            out_copy(0).wait()
            def mix(i):
                at = part(i, WIDE)
                v_acc[:, at] = nn(v_c[...], v_out[:, at]) + bias(6)

            loop(width // WIDE, mix)

            def second_norm(i, carry):
                at = part(i, 64)
                branch = v_acc[at, :]
                middle = v_x[at, :].astype(f32) + branch
                v_h[at, :] = middle
                normed, _ = row_stats(middle)
                v_b[at, :] = (normed * norm(2) + norm(3)).astype(bf16)
                v_acc[at, :] = jnp.broadcast_to(bias(7), (64, width))
                mask = valid(i, 64)
                return (carry[0] + square(middle, mask), carry[1] + square(branch, mask))

            sums_one = lax.fori_loop(0, rows // 64, second_norm, sums_one, unroll=2)
            send(v_h, s_h.at[here], 3)
            send(v_b, s_b.at[here], 4)

        def feed(i):
            up_copy(i).wait()
            down_copy(i).wait()
            at = part(i, BROAD)
            shift = vectors[:, pl.ds(pl.multiple_of(8 * width + i * BROAD, BROAD), BROAD)]
            act, slope = gate(nn(v_b[these, :], v_up[:, at]) + shift)
            act = act.astype(bf16)
            v_g[these, at] = act
            v_d[these, at] = slope.astype(bf16)
            v_acc[these, :] += nn(act, v_down[at, :])
            g_copy(i).start()
            d_copy(i).start()

        def g_copy(i):
            at = part(i, BROAD)
            return pltpu.make_async_copy(v_g.at[pl.ds(low, count), at], s_g.at[there, at], sem_g.at[i])

        def d_copy(i):
            at = part(i, BROAD)
            return pltpu.make_async_copy(v_d.at[pl.ds(low, count), at], s_d.at[there, at], sem_d.at[i])

        loop(hidden // BROAD, feed)

        def finish(i, carry):
            at = part(i, 64)
            branch = v_acc[at, :]
            output = v_h[at, :] + branch
            v_z[at, :] = output.astype(bf16)
            mask = valid(i, 64)
            return (carry[0] + square(output, mask), carry[1] + square(branch, mask))

        sums_two = lax.fori_loop(low // 64, high // 64, finish, (nothing, nothing), unroll=2)
        send(v_z.at[pl.ds(low, count)], z_out, 7)
        send(v_z.at[pl.ds(low, count)], layers.at[0, picked, 0, pl.ds(low, count)], 5)
        for k, value in enumerate((sums_one[0], sums_two[0], sums_one[1], sums_two[1])):
            squares_out[k] = value
        for copy in outs:
            copy.wait()
        for i in range(hidden // BROAD):
            g_copy(i).wait()
            d_copy(i).wait()
        if starts:
            p_copy(groups - 2).wait()
            p_copy(groups - 1).wait()

    @pl.when(jnp.logical_not(active))
    def _():
        squares_out[...] = jnp.zeros_like(squares_out)


def stash_shapes(rows, width, hidden):
    heads = width // HEAD
    return [
        jax.ShapeDtypeStruct((2 * rows, width), bf16),
        jax.ShapeDtypeStruct((2 * rows, width), bf16),
        jax.ShapeDtypeStruct((2 * rows, 3 * width), bf16),
        jax.ShapeDtypeStruct((2 * rows, width), bf16),
        jax.ShapeDtypeStruct((2 * rows, width), f32),
        jax.ShapeDtypeStruct((2 * rows, width), f32),
        jax.ShapeDtypeStruct((2 * rows, width), bf16),
        jax.ShapeDtypeStruct((2 * rows, hidden), bf16),
        jax.ShapeDtypeStruct((2 * rows, hidden), bf16),
        jax.ShapeDtypeStruct((2, heads, rows, rows), bf16),
        jax.ShapeDtypeStruct((1, 2, 1, rows, width), bf16),
    ]


def forward_call(slot, plan, stage, spans, norms, vectors, feat, recv, weights, stash=()):
    rows, width = feat.shape[2:]
    count = {BOTH: rows, FIRST: early_rows(rows), SECOND: rows - early_rows(rows)}[stage]
    hidden = weights[2].shape[1]
    any_ = pl.BlockSpec(memory_space=pl.ANY)
    vm = pl.BlockSpec(memory_space=pltpu.VMEM)
    shapes = stash_shapes(rows, width, hidden)
    results = pl.pallas_call(
        functools.partial(forward_kernel, slot, plan, stage, len(stash), len(recv)),
        in_specs=[pl.BlockSpec(memory_space=pltpu.SMEM), vm, vm] + [any_] * (5 + len(recv) + len(stash)),
        out_specs=[any_, vm] + [any_] * len(shapes),
        out_shape=[jax.ShapeDtypeStruct((count, width), bf16), jax.ShapeDtypeStruct((4, 8, width), f32)] + shapes,
        input_output_aliases={8 + len(recv) + k: 2 + k for k in range(len(stash))},
        scratch_shapes=[
            pltpu.VMEM(w.shape, bf16) for w in weights
        ] + [
            pltpu.VMEM((rows, width), bf16),
            pltpu.VMEM((rows, width), bf16),
            pltpu.VMEM((rows, 3 * width), bf16),
            pltpu.VMEM((rows, width), bf16),
            pltpu.VMEM((rows, width), f32),
            pltpu.VMEM((rows, width), f32),
            pltpu.VMEM((rows, width), bf16),
            pltpu.VMEM((rows, hidden), bf16),
            pltpu.VMEM((rows, hidden), bf16),
            pltpu.VMEM((2, 4, rows, rows), bf16),
            pltpu.VMEM((rows, rows), f32),
            pltpu.VMEM((rows, width), f32),
            pltpu.VMEM((rows, width), bf16),
            pltpu.SemaphoreType.DMA((4 + 2 * hidden // WIDE,)),
            pltpu.SemaphoreType.DMA((1,)),
            pltpu.SemaphoreType.DMA((10,)),
            pltpu.SemaphoreType.DMA((2,)),
            pltpu.SemaphoreType.DMA((hidden // WIDE,)),
            pltpu.SemaphoreType.DMA((hidden // WIDE,)),
        ],
        compiler_params=pltpu.CompilerParams(vmem_limit_bytes=VMEM),
        cost_estimate=pl.CostEstimate(flops=LARGE, bytes_accessed=1, transcendentals=0),
        name="layer_forward",
    )(spans, norms, vectors, feat, *weights, *recv, *stash)
    return results[0], results[1], results[2:]


def backward_kernel(slot, plan, stage, aliased, given, *refs):
    feeds, attends = stage != SECOND, stage != FIRST
    spans, norms, cot, recv, w_in, w_out, w_up, w_down = refs[:8]
    s_x, s_qkv, s_c, s_l, s_h, s_d, s_p = refs[8:15]
    if stage == SECOND:
        mid_in, middle_in = refs[15:17]
    refs = refs[15 + given + aliased :]
    smalls = refs[0]
    refs = refs[1:]
    if feeds:
        g_up, g_mid = refs[:2]
        refs = refs[2:]
    if attends:
        dx_out, g_qkv, inputs = refs[:3]
        refs = refs[3:]
    if stage == BOTH:
        g_feed = refs[0]
        refs = refs[1:]
    if stage == FIRST:
        middle_out = refs[0]
        refs = refs[1:]
    (v_in, v_out, v_up, v_down, v_x, v_dy, v_qkv, v_c, v_l, v_h, v_d, v_p, v_du, v_do, v_dc, v_dqkv, v_acc,
     v_s, v_k, v_dx, sem_w, sem_x, sem_d, sem_p, sem_o) = refs
    rows, width = v_x.shape
    hidden = v_up.shape[1]
    here = pl.ds(slot * rows, rows)
    tiles = hidden // WIDE

    first = lax.axis_index("section") == 0
    active, picked = chosen_tick(first, plan)

    def norm(k):
        return norms[:, k * width : (k + 1) * width]

    @pl.when(active)
    def _():
        length = spans[picked]
        if stage != BOTH:
            smalls[...] = jnp.zeros_like(smalls)

        if feeds:

            @pl.when(jnp.logical_not(first))
            def _():
                pltpu.make_async_copy(cot.at[picked, 0], v_dy, sem_x.at[0]).start()

            @pl.when(first)
            def _():
                pltpu.make_async_copy(recv, v_dy, sem_x.at[0]).start()

        def down_copy(i):
            return pltpu.make_async_copy(
                w_down.at[part(i, WIDE)], v_down.at[part(i, WIDE)], sem_w.at[i]
            )

        def up_copy(i):
            at = part(i, WIDE)
            return pltpu.make_async_copy(w_up.at[:, at], v_up.at[:, at], sem_w.at[tiles + i])

        def d_copy(i):
            return pltpu.make_async_copy(
                s_d.at[here, part(i, WIDE)], v_d.at[i % 2], sem_d.at[i % 2]
            )

        def p_copy(i):
            return pltpu.make_async_copy(
                s_p.at[slot, pl.ds(i * 4, 4)], v_p.at[i % 2], sem_p.at[i % 2]
            )

        loads = copies(
            [
                (s_x.at[here], v_x),
                (s_qkv.at[here], v_qkv),
                (s_c.at[here], v_c),
                (s_l.at[here], v_l),
                (s_h.at[here], v_h),
                (w_out, v_out),
                (w_in, v_in),
            ],
            sem_x.at[pl.ds(1, 7)],
        )
        if feeds:
            d_copy(0).start()
            for i in range(tiles):
                down_copy(i).start()
                up_copy(i).start()
                if i == 0:
                    d_copy(1).start()
            loads[4].start()
        if stage == SECOND:
            entries = [
                pltpu.make_async_copy(mid_in.at[here], v_do, sem_o.at[0]),
                pltpu.make_async_copy(middle_in, v_acc, sem_o.at[3]),
            ]
            for copy in entries:
                copy.start()
        def enter_attention():
            for k in (5, 1, 2, 3):
                loads[k].start()
            p_copy(0).start()
            p_copy(1).start()

        def enter_last():
            loads[6].start()
            loads[0].start()

        if stage == SECOND:
            enter_attention()
            enter_last()
        nothing = jnp.zeros((8, width), f32)

        def fold(values):
            return jnp.sum(values.reshape(-1, 8, width), axis=0)

        def enter(i, total):
            at = part(i, 64)
            place = lax.broadcasted_iota(jnp.int32, (64, 1), 0) + i * 64
            masked = jnp.where(place < length, v_dy[at, :].astype(f32), 0.0)
            v_dy[at, :] = masked.astype(bf16)
            v_acc[at, :] = jnp.zeros((64, width), f32)
            return total + fold(masked)

        if feeds:
            pltpu.make_async_copy(recv, v_dy, sem_x.at[0]).wait()
            total = lax.fori_loop(0, rows // 64, enter, nothing, unroll=2)
            smalls[7:8, :] = jnp.sum(total, axis=0, keepdims=True)
        if stage == BOTH:
            feed_copy = pltpu.make_async_copy(v_dy, g_feed.at[here], sem_o.at[4])
            feed_copy.start()

        def feed(i):
            down_copy(i).wait()
            up_copy(i).wait()
            d_copy(i).wait()
            if stage == BOTH:
                pl.when(i == tiles - 2)(enter_attention)
                pl.when(i == tiles - 1)(enter_last)
            at = part(i, WIDE)
            pre = (nt(v_dy[...], v_down[at, :]) * v_d[i % 2].astype(f32)).astype(bf16)
            v_du[:, at] = pre
            v_acc[...] += nt(pre, v_up[:, at])
            smalls[pl.ds(8 + i, 1), :] = jnp.sum(v_du[:, at].astype(f32), axis=0, keepdims=True)
            pltpu.make_async_copy(v_du.at[:, at], g_up.at[here, at], sem_o.at[3]).start()

            @pl.when(i + 2 < tiles)
            def _():
                d_copy(i + 2).start()

        if feeds:
            loop(tiles, feed)
            loads[4].wait()

        def norm_back(source, grad, gain):
            normed, inverse = row_stats(source)
            scaled = grad * gain
            mean_one = jnp.mean(scaled, axis=-1, keepdims=True)
            mean_two = jnp.mean(scaled * normed, axis=-1, keepdims=True)
            return inverse * (scaled - mean_one - normed * mean_two), fold(grad * normed), fold(grad)

        def second_norm(i, carry):
            at = part(i, 64)
            rows_back, one, two = norm_back(v_h[at, :], v_acc[at, :], norm(2))
            middle = rows_back + v_dy[at, :].astype(f32)
            v_acc[at, :] = middle
            low = middle.astype(bf16)
            v_do[at, :] = low
            return carry[0] + one, carry[1] + two, carry[2] + fold(low.astype(f32))

        if feeds:
            sums = lax.fori_loop(0, rows // 64, second_norm, (nothing,) * 3, unroll=2)
            for k, value in zip((2, 3, 6), sums):
                smalls[k : k + 1, :] = jnp.sum(value, axis=0, keepdims=True)
            outs = [pltpu.make_async_copy(v_do, g_mid.at[here], sem_o.at[0])]
            if stage == FIRST:
                outs.append(pltpu.make_async_copy(v_acc, middle_out, sem_o.at[1]))
            for copy in outs:
                copy.start()
        if stage == SECOND:
            for copy in entries:
                copy.wait()
        if attends:
            loads[5].wait()
            v_dc[...] = nt(v_do[...], v_out[...]).astype(bf16)
            for k in (1, 2, 3):
                loads[k].wait()
        lane = lax.broadcasted_iota(jnp.int32, (1, GROUP), 1) // HEAD

        def attend(i):
            p_copy(i).wait()
            at = part(i, GROUP)
            key_at = pl.ds(pl.multiple_of(width + i * GROUP, GROUP), GROUP)
            value_at = pl.ds(pl.multiple_of(2 * width + i * GROUP, GROUP), GROUP)
            key = v_qkv[:, key_at]
            value = v_qkv[:, value_at]
            query = v_qkv[:, at]
            wide = v_dc[:, at].astype(f32) * v_l[:, at]
            low = wide.astype(bf16)
            dots = wide * v_c[:, at].astype(f32)
            for h in range(4):
                hs = slice(h * rows, (h + 1) * rows)
                v_k[hs, :] = jnp.where(lane == h, key, 0).astype(bf16)
                masked = jnp.where(lane == h, low, 0).astype(bf16)
                delta = jnp.sum(jnp.where(lane == h, dots, 0.0), axis=-1, keepdims=True)
                inner = nt(masked, value) - delta
                v_s[:, hs] = v_p[i % 2, h] * inner.astype(bf16)
            grad_query = (nn(v_s[...], v_k[...]) * score_scale).astype(bf16)
            query_t = query.T
            low_t = low.T
            keys, values = [], []
            for h in range(4):
                hs = slice(h * HEAD, (h + 1) * HEAD)
                keys.append(nn(query_t[hs], v_s[:, h * rows : (h + 1) * rows]))
                values.append(nn(low_t[hs], v_p[i % 2, h]))
            grad_key = (jnp.concatenate(keys, axis=0) * score_scale).astype(bf16).T
            grad_value = jnp.concatenate(values, axis=0).astype(bf16).T
            v_dqkv[:, at] = grad_query
            v_dqkv[:, key_at] = grad_key
            v_dqkv[:, value_at] = grad_value
            smalls[4:5, at] = jnp.sum(grad_query.astype(f32), axis=0, keepdims=True)
            smalls[5:6, at] = jnp.sum(grad_value.astype(f32), axis=0, keepdims=True)

            @pl.when(i + 2 < width // GROUP)
            def _():
                p_copy(i + 2).start()

        if attends:
            loop(width // GROUP, attend)
            qkv_copy = pltpu.make_async_copy(v_dqkv, g_qkv.at[here], sem_o.at[1])
            qkv_copy.start()
            loads[6].wait()
            loads[0].wait()

            v_h[...] = nt(v_dqkv[...], v_in[...])

        def first_norm(i, carry):
            at = part(i, 64)
            rows_back, one, two = norm_back(v_x[at, :].astype(f32), v_h[at, :], norm(0))
            v_dx[at, :] = (rows_back + v_acc[at, :]).astype(bf16)
            return carry[0] + one, carry[1] + two

        if attends:
            sums = lax.fori_loop(0, rows // 64, first_norm, (nothing,) * 2, unroll=2)
            for k, value in enumerate(sums):
                smalls[k : k + 1, :] = jnp.sum(value, axis=0, keepdims=True)
            dx_copy = pltpu.make_async_copy(v_dx, dx_out, sem_o.at[2])
            dx_copy.start()
            input_copy = pltpu.make_async_copy(v_dx, inputs.at[0, picked, 0], sem_o.at[5])
            input_copy.start()
            for copy in (qkv_copy, dx_copy, input_copy):
                copy.wait()
        if stage == BOTH:
            feed_copy.wait()
        if feeds:
            for copy in outs:
                copy.wait()
            pltpu.make_async_copy(v_du, g_up.at[here], sem_o.at[3]).wait()

    @pl.when(jnp.logical_not(active))
    def _():
        smalls[...] = jnp.zeros_like(smalls)


def backward_call(slot, plan, stage, spans, norms, cot, recv, weights, stash, given, grads):
    rows, width = recv.shape
    hidden = weights[2].shape[1]
    any_ = pl.BlockSpec(memory_space=pl.ANY)
    vm = pl.BlockSpec(memory_space=pltpu.VMEM)
    shape = jax.ShapeDtypeStruct
    outs = {"smalls": shape((8 + hidden // WIDE, width), f32)}
    if stage != SECOND:
        outs["up"] = shape((2 * rows, hidden), bf16)
        outs["mid"] = shape((2 * rows, width), bf16)
    if stage != FIRST:
        outs["dx"] = shape((rows, width), bf16)
        outs["qkv"] = shape((2 * rows, 3 * width), bf16)
        outs["inputs"] = shape((1, 2, 1, rows, width), bf16)
    if stage == BOTH:
        outs["feed"] = shape((2 * rows, width), bf16)
    if stage == FIRST:
        outs["middle"] = shape((rows, width), f32)
    names = list(outs)
    kept = [name for name in names if name in grads and name not in ("smalls", "dx")]
    s_x, s_a, s_qkv, s_c, s_l, s_h, s_b, s_g, s_d, s_p, _ = stash
    results = pl.pallas_call(
        functools.partial(backward_kernel, slot, plan, stage, len(kept), len(given)),
        in_specs=[pl.BlockSpec(memory_space=pltpu.SMEM), vm] + [any_] * (13 + len(given) + len(kept)),
        out_specs=[vm] + [any_] * (len(names) - 1),
        out_shape=list(outs.values()),
        input_output_aliases={15 + len(given) + k: names.index(n) for k, n in enumerate(kept)},
        scratch_shapes=[pltpu.VMEM(w.shape, bf16) for w in weights] + [
            pltpu.VMEM((rows, width), bf16),
            pltpu.VMEM((rows, width), bf16),
            pltpu.VMEM((rows, 3 * width), bf16),
            pltpu.VMEM((rows, width), bf16),
            pltpu.VMEM((rows, width), f32),
            pltpu.VMEM((rows, width), f32),
            pltpu.VMEM((2, rows, WIDE), bf16),
            pltpu.VMEM((2, 4, rows, rows), bf16),
            pltpu.VMEM((rows, hidden), bf16),
            pltpu.VMEM((rows, width), bf16),
            pltpu.VMEM((rows, width), bf16),
            pltpu.VMEM((rows, 3 * width), bf16),
            pltpu.VMEM((rows, width), f32),
            pltpu.VMEM((rows, 4 * rows), bf16),
            pltpu.VMEM((4 * rows, GROUP), bf16),
            pltpu.VMEM((rows, width), bf16),
            pltpu.SemaphoreType.DMA((2 * hidden // WIDE,)),
            pltpu.SemaphoreType.DMA((8,)),
            pltpu.SemaphoreType.DMA((2,)),
            pltpu.SemaphoreType.DMA((2,)),
            pltpu.SemaphoreType.DMA((6,)),
        ],
        compiler_params=pltpu.CompilerParams(vmem_limit_bytes=VMEM),
        cost_estimate=pl.CostEstimate(flops=LARGE, bytes_accessed=1, transcendentals=0),
        name="layer_backward",
    )(
        spans, norms, cot, recv, *weights, s_x, s_qkv, s_c, s_l, s_h, s_d, s_p, *given,
        *[grads[name] for name in kept],
    )
    return {**grads, **dict(zip(names, results))}


def turn_kernel(blocks, *refs):
    count = len(blocks)
    for k, block in enumerate(blocks):
        source, target = refs[k], refs[count + k]

        @pl.when((pl.program_id(0) == k) if k + 1 < count else (pl.program_id(0) >= k))
        def _(source=source, target=target, block=block):
            flat = source[...].T
            pairs = flat.shape[0] // (2 * block)
            for core in range(2):

                @pl.when(lax.axis_index("dp") % 2 == core)
                def _(core=core):
                    for j in range(pairs):
                        at = slice(j * block, (j + 1) * block)
                        other = (2 * j + 1 - core) * block
                        own = (2 * j + core) * block
                        target[0, at, :] = flat[other : other + block]
                        target[1, at, :] = flat[own : own + block]


def turn_call(sources):
    rows = sources[0].shape[0]
    count = len(sources)
    size = lax.axis_size("dp")
    steps = count - 1 + sources[-1].shape[1] // WIDE

    def last(i):
        return jnp.maximum(i - (count - 1), 0)

    ins = [pl.BlockSpec((rows, WIDE), lambda i: (0, 0))] * (count - 1)
    ins.append(pl.BlockSpec((rows, WIDE), lambda i: (0, last(i))))
    outs = [pl.BlockSpec((2, WIDE // 2, rows), lambda i: (0, 0, 0))] * (count - 1)
    outs.append(pl.BlockSpec((2, WIDE // 2, rows), lambda i: (0, last(i), 0)))
    return pl.pallas_call(
        functools.partial(turn_kernel, [s.shape[1] // size for s in sources]),
        grid=(steps,),
        in_specs=ins,
        out_specs=outs,
        out_shape=[jax.ShapeDtypeStruct((2, s.shape[1] // 2, rows), bf16) for s in sources],
        compiler_params=pltpu.CompilerParams(vmem_limit_bytes=VMEM),
        cost_estimate=pl.CostEstimate(flops=1, bytes_accessed=1, transcendentals=0),
        name="turn",
    )(*sources)


def weight_kernel(widths, half, left, right, *rest):
    if len(rest) > len(widths):
        late, *outs, joined = rest
        rows = late.shape[0]

        @pl.when(pl.program_id(0) == 0)
        def _():
            joined[:rows, :] = right[:rows, :]
            joined[rows:, :] = jnp.where(
                lax.axis_index("section") == 0, late[...], right[rows:, :]
            )

        right = joined
    else:
        outs = rest
    total = nn(left[0], right[...]).astype(bf16)
    at = 0
    for width, out in zip(widths, outs):
        step, offset = divmod(at, right.shape[1])
        if len(widths) == 1:
            out[...] = total
        else:

            @pl.when(pl.program_id(1) == step)
            def _(out=out, cut=slice(offset, offset + width)):
                out[...] = total[:, cut]

        at += width


def weight_call(left, right, start, widths, half, late=None):
    _, height, rows = left.shape
    columns = sum(widths)
    tall = min(height, WIDE)
    wide = min(columns, WIDE)
    specs = [
        pl.BlockSpec((1, tall, rows), lambda i, j: (half, i, 0)),
        pl.BlockSpec((rows, wide), lambda i, j: (0, start // wide + j)),
    ]
    operands = (left, right)
    if late is not None:
        specs.append(pl.BlockSpec((rows // 2, wide), lambda i, j: (0, j)))
        operands += (late,)

    def out(width):
        if width > wide:
            return pl.BlockSpec((tall, wide), lambda i, j: (i, j))
        return pl.BlockSpec((tall, width), lambda i, j: (i, 0))

    return pl.pallas_call(
        functools.partial(weight_kernel, widths, half),
        grid=(height // tall, columns // wide),
        in_specs=specs,
        out_specs=[out(width) for width in widths],
        out_shape=[jax.ShapeDtypeStruct((height, width), bf16) for width in widths],
        scratch_shapes=[] if late is None else [pltpu.VMEM((rows, columns), bf16)],
        compiler_params=pltpu.CompilerParams(vmem_limit_bytes=VMEM),
        cost_estimate=pl.CostEstimate(flops=1, bytes_accessed=1, transcendentals=0),
        name="weight_product",
    )(*operands)


def sum_kernel(layout, lefts, fixed, free, place, *refs):
    count = sum(len(arrays) for arrays in layout)
    sources = iter(refs[:count])
    terms = [[next(sources) for _ in arrays] for arrays in layout]
    out, held, total, sem, out_sem = refs[-5:]
    me = lax.axis_index("dp")
    cells = list(itertools.product(range(2), repeat=len(free)))
    loads, slot = [], 0
    for cell in cells:
        loads.append([])
        for arrays, left, widths in zip(terms, lefts, layout):
            index = []
            for bit in left:
                if bit in free:
                    index.append(cell[free.index(bit)])
                else:
                    own = (me >> bit) & 1
                    index.append(own if fixed[bit] else 1 - own)
            at = 0
            for ref, (start, width) in zip(arrays, widths):
                copy = pltpu.make_async_copy(
                    ref.at[(*index, slice(None), pl.ds(start, width))],
                    held.at[slot, :, pl.ds(at, width)],
                    sem.at[len(loads[-1]), len(loads) - 1],
                )
                copy.start()
                loads[-1].append(copy)
                at += width
            slot += 1
    stores = []
    for k, cell in enumerate(cells):
        for copy in loads[k]:
            copy.wait()
        value = added([held[k * len(terms) + j] for j in range(len(terms))])
        total[k] = value.astype(total.dtype)
        stores.append(pltpu.make_async_copy(total.at[k], place(out, cell), out_sem.at[k]))
        stores[-1].start()
    for copy in stores:
        copy.wait()


def sum_call(terms, fixed, kind, into=None, start=0):
    rows = terms[0][0][0][0].shape[-2]
    layout = [[(at, width) for _, at, width in arrays] for arrays, _ in terms]
    lefts = [left for _, left in terms]
    columns = sum(width for _, width in layout[0])
    free = [bit for bit in lefts[0] if bit not in fixed]
    operands = [array for arrays, _ in terms for array, _, _ in arrays]
    cells = 2 ** len(free)
    aliases = {}
    wide = 0
    if into is None:
        shape = jax.ShapeDtypeStruct((2,) * len(free) + (rows, columns), kind)
    else:
        wide, into = into
        shape = jax.ShapeDtypeStruct((1, rows, wide), kind)
        if into is not None:
            aliases = {len(operands): 0}
            operands.append(into)

    given = len(operands)

    def place(out, cell):
        if wide:
            return out.at[0, :, pl.ds(start, columns)]
        return out.at[cell] if cell else out

    def kernel(*refs):
        refs = refs[: given - len(aliases)] + refs[given:]
        sum_kernel(layout, lefts, fixed, free, place, *refs)

    any_ = pl.BlockSpec(memory_space=pl.ANY)
    return pl.pallas_call(
        kernel,
        in_specs=[any_] * len(operands),
        out_specs=any_,
        out_shape=shape,
        input_output_aliases=aliases,
        scratch_shapes=[
            pltpu.VMEM((cells * len(terms), rows, columns), terms[0][0][0][0].dtype),
            pltpu.VMEM((cells, rows, columns), kind),
            pltpu.SemaphoreType.DMA((max(sum(len(arrays) for arrays, _ in terms), 1), cells)),
            pltpu.SemaphoreType.DMA((cells,)),
        ],
        compiler_params=pltpu.CompilerParams(
            vmem_limit_bytes=VMEM if len(free) > 1 or rows > columns // 8 else LESS
        ),
        cost_estimate=pl.CostEstimate(flops=SMALL, bytes_accessed=1, transcendentals=0),
        name="sum_terms",
    )(*operands)


highest = lax.Precision.HIGHEST


def added(terms):
    total = terms[0].astype(f32)
    for term in terms[1:]:
        total = total + term.astype(f32)
    return total


class Line:
    def __init__(self):
        self.last = None

    def after(self, values):
        if self.last is not None:
            values = lax.optimization_barrier(tuple(values) + (self.last,))[:-1]
        return list(values)

    def done(self, value):
        self.last = value


class Exchange:
    def __init__(self, line, terms, left, order):
        self.line = line
        self.terms = [(arrays, sorted(left, reverse=True)) for arrays in terms]
        self.fixed = {}
        self.order = list(order)
        self.kind = terms[0][0][0].dtype

    def total(self, fixed, kind, **where):
        values = iter(self.line.after([array for arrays, _ in self.terms for array, _, _ in arrays]))
        self.terms = [
            ([(next(values), at, width) for _, at, width in arrays], left)
            for arrays, left in self.terms
        ]
        total = sum_call(self.terms, fixed, kind, **where)
        self.line.done(total)
        return total

    def step(self):
        bit = self.order.pop(0)
        theirs = self.total({**self.fixed, bit: False}, self.kind)
        self.fixed[bit] = True
        left = [k for k in self.terms[0][1] if k not in self.fixed]
        self.terms.append((whole(crossed(theirs, bit)), left))

    def cut(self, widths):
        parts = []
        low = 0
        for width in widths:
            high = low + width
            terms = []
            for arrays, left in self.terms:
                chosen, at = [], 0
                for array, start, columns in arrays:
                    a, b = max(low, at), min(high, at + columns)
                    if a < b:
                        chosen.append((array, start + a - at, b - a))
                    at += columns
                terms.append((chosen, left))
            part_ = Exchange(self.line, [terms[0][0]], (), self.order)
            part_.terms = terms
            part_.fixed = dict(self.fixed)
            parts.append(part_)
            low = high
        return parts

    def finish(self, **where):
        while self.order:
            self.step()
        return self.total(self.fixed, f32, **where)


def crossed(value, bit):
    return lax.ppermute(value, "dp", [(i, i ^ (1 << bit)) for i in range(lax.axis_size("dp"))])


def whole(array):
    return [(array, 0, array.shape[-1])]


def whole(array):
    return [(array, 0, array.shape[-1])]


class WeightSum(Exchange):
    def __init__(self, line, left, right, start, widths, order, late=None):
        size = lax.axis_size("dp")
        bits = size.bit_length() - 1
        shape = [2] * (bits - 1) + [2 * left.shape[1] // size, -1]
        left, right = line.after((left, right))
        theirs = weight_call(left, right, start, widths, 0, late)
        line.done(theirs[-1])
        received = [whole(crossed(array, 0).reshape(shape)) for array in theirs]
        self.product = (left, right, start, [sum(widths)], 1, late)
        self.shape = shape
        super().__init__(line, (sum(received, []),), range(1, bits), order)

    def own(self):
        left, right = self.line.after(self.product[:2])
        (mine,) = weight_call(left, right, *self.product[2:])
        self.line.done(mine)
        self.terms.append((whole(mine.reshape(self.shape)), self.terms[0][1]))
        return self


def shards(
    features,
    cotangent,
    lengths,
    codebook_index,
    attention_in,
    attention_out,
    feed_up,
    feed_down,
    vectors,
    adaptive_weight,
    codebook_table,
):
    is_first = lax.axis_index("section") == 0
    adaptive = jnp.where(is_first, 0.0, 1.0)
    rows, width = features.shape[2:]
    hidden = feed_up.shape[2]
    size = lax.axis_size("dp")
    bits = size.bit_length() - 1
    weights = (attention_in[0], attention_out[0], feed_up[0], feed_down[0])

    def send(value, to):
        return lax.ppermute(value, "section", [(1 - to, to)])

    spans = lengths[:, 0]

    def forward(slot, plan, norms, recv, stash=(), stage=BOTH):
        return forward_call(
            slot, plan, stage, spans, norms, vectors, features, recv, weights, stash
        )

    def backward(slot, plan, stage, norms, recv, stash, grads, given=()):
        return backward_call(
            slot, plan, stage, spans, norms, cotangent, recv, weights, stash, given, grads
        )

    z_one, squares_one, stash = forward(0, (0, None), vectors, ())
    received_one = (send(z_one, 1),)
    table, z_one = lax.optimization_barrier((codebook_table, z_one))
    condition_table = jnp.dot(table, adaptive_weight, preferred_element_type=f32)
    one_hot = (
        codebook_index[:, 0][:, None]
        == jnp.arange(codebook_table.shape[0], dtype=jnp.int32)[None, :]
    ).astype(f32)
    norms = vectors[:, : 4 * width] + adaptive * jnp.dot(
        one_hot, condition_table, precision=highest
    )
    norms_one, norms_two = norms[:1], norms[1:]
    z_two, squares_two, stash = forward(1, (1, 0), norms_one, received_one, stash)
    received_two = send(z_two, 1)
    grads = backward(1, (None, 0), BOTH, norms_one, z_two, stash, {})
    smalls_one = grads["smalls"]
    back_one = send(grads["dx"], 0)
    z_three, squares_three, stash = forward(0, (None, 1), norms_two, (received_two,), stash)
    grads = backward(0, (0, 1), BOTH, norms_two, back_one, stash, grads)
    smalls_two = grads["smalls"]
    back_two = send(grads["dx"], 0)

    s_x, s_a, s_qkv, s_c, s_l, s_h, s_b, s_g, s_d, s_p, layer_outputs = stash
    side_first = list(range(1, bits))
    line_first = side_first[1:] + side_first[:1]
    line = Line()
    line.done(smalls_two)
    squares = jnp.sum(squares_one + squares_two + squares_three, axis=(1, 2))
    counted = jnp.sum(lengths).astype(f32)
    (totals,) = line.after((jnp.concatenate([squares, counted[None], jnp.zeros((123,), f32)]),))
    for bit in range(bits):
        totals = totals + crossed(totals, bit)
    t_a, t_b, t_c, t_g = turn_call(line.after((s_a, s_b, s_c, s_g)))
    line.done(t_a)
    (totals,) = line.after((totals,))
    line.done(totals)
    down = WeightSum(line, t_g, grads["feed"], 0, [width], side_first, back_two).own()
    down.step()
    (back_two,) = line.after((back_two,))
    grads = backward(1, (1, None), FIRST, vectors, back_two, stash, grads)
    smalls_three = grads["smalls"]
    line.done(smalls_three)
    up = WeightSum(line, t_b, grads["up"], 0, [WIDE] * (hidden // WIDE), side_first).own()
    up.step()
    down.step()
    out = WeightSum(line, t_c, grads["mid"], 0, [width], side_first).own()
    (middle,) = line.after((grads["middle"],))
    grads = backward(
        1, (1, None), SECOND, vectors, back_two, stash, grads, (grads["mid"], middle)
    )
    smalls_four = grads["smalls"]
    line.done(smalls_four)
    g_qkv, input_grads = grads["qkv"], grads["inputs"]
    down.step()
    into_one = WeightSum(line, t_a, g_qkv, 0, [width] * 3, side_first).own()

    smalls = smalls_one + smalls_two + smalls_three + smalls_four
    table_grad = one_hot[0][:, None] * smalls_one[:4].reshape(1, -1) + one_hot[1][:, None] * (
        smalls_two[:4].reshape(1, -1) * adaptive
    )
    codes = table_grad.shape[0]
    share = table_grad.shape[1] // (2 * size)
    table_blocks = table_grad.reshape(codes, 2, size, share).transpose(2, 1, 0, 3)
    packed = jnp.concatenate([smalls.reshape(size, -1), table_blocks.reshape(size, -1)], axis=1)
    count = packed.shape[1]
    block = width // size
    packed = jnp.pad(packed.reshape(size, block, -1), ((0, 0), (0, 0), (0, 128 - count // block)))
    packed = packed.astype(bf16).reshape([2] * bits + [block, 128])
    core = lax.axis_index("dp") & 1
    (other, own) = [
        lax.dynamic_index_in_dim(packed, which, bits - 1, keepdims=False)
        for which in (1 - core, core)
    ]
    other = crossed(other, 0)
    into_one, into_two = into_one.cut([2 * width, width])
    up_one, up_two = up.cut([hidden // 2] * 2)
    into_two.terms = [
        (arrays + whole(extra), left)
        for (arrays, left), extra in zip(into_two.terms, (other, own))
    ]
    into_one.step()
    up_one.step()
    up_two.step()
    into_two.step()
    out.step()
    down = down.finish(into=(width, None))
    up_one.step()
    into_one.step()
    up_two.step()
    into_two.step()
    up = up_one.finish(into=(hidden, None))
    into_one.step()
    out.step()
    up = up_two.finish(into=(hidden, up), start=hidden // 2)
    into_two.step()
    into = into_one.finish(into=(3 * width, None))
    out.step()
    last = into_two.finish()
    out = out.finish(into=(width, None))
    into = lax.dynamic_update_slice(into, last[None, :, :width], (0, 0, 2 * width))
    small_sum = last[:, width : width + count // block].reshape(-1)
    vector_share = small_sum[: smalls.size // size]
    table_share = small_sum[smalls.size // size :].reshape(2, codes, share)
    table_own = jnp.where(is_first, send(table_share[0], 0), table_share[1])
    grad_adaptive = lax.dot_general(
        codebook_table.astype(f32),
        table_own,
        (((0,), (0,)), ((), ())),
        precision=highest,
        preferred_element_type=f32,
    )
    residual_rms = jnp.sqrt(totals[:4] / (totals[4] * width))[None]

    return (
        layer_outputs,
        input_grads,
        into,
        out,
        up,
        down,
        vector_share[None],
        grad_adaptive,
        residual_rms,
    )


def solution(mesh):
    placed = (
        P(None, "dp", None, None),
        P(None, "dp", None, None),
        P(None, "dp"),
        P(None, "dp"),
        P("section", None, None),
        P("section", None, None),
        P("section", None, None),
        P("section", None, None),
        P("section", None),
        P(),
        P(),
    )
    return jax.shard_map(
        shards,
        mesh=mesh,
        in_specs=placed,
        out_specs=(
            P("section", None, "dp", None, None),
            P("section", None, "dp", None, None),
            P("section", "dp", None),
            P("section", "dp", None),
            P("section", "dp", None),
            P("section", "dp", None),
            P("section", "dp"),
            P(None, ("section", "dp")),
            P("section", None),
        ),
        check_vma=False,
    )
```

```python
import functools
import itertools

import jax
import jax.numpy as jnp
from jax import lax
from jax.experimental import pallas as pl
from jax.experimental.pallas import tpu as pltpu
from jax.sharding import PartitionSpec as P

HEAD = 64
norm_eps = 1e-05
root_half = 0.7071067811865476
slope_scale = 0.3989422804014327
score_scale = 0.125
big_negative = -1e30
f32 = jnp.float32
bf16 = jnp.bfloat16
GROUP = 4 * HEAD
TILE = 512
WIDE = 1024
BROAD = 2048
VMEM = 62 * 2**20
SMALL = 10**6
LARGE = 10**11
BOTH, FIRST, SECOND = range(3)
LESS = 16 * 2**20


def nn(a, b):
    return lax.dot_general(a, b, (((1,), (0,)), ((), ())), preferred_element_type=f32)


def nt(a, b):
    return lax.dot_general(a, b, (((1,), (1,)), ((), ())), preferred_element_type=f32)


def row_stats(rows):
    average = jnp.mean(rows, axis=-1, keepdims=True)
    centered = rows - average
    inverse = lax.rsqrt(jnp.mean(centered * centered, axis=-1, keepdims=True) + norm_eps)
    return centered * inverse, inverse


def gate(values):
    bell = jnp.exp(-0.5 * values * values)
    upper = 0.5 * (1.0 + lax.erf(values * root_half))
    return values * upper, upper + values * bell * slope_scale


def loop(count, body, unroll=1):
    def run(i, carry):
        body(i)
        return carry

    lax.fori_loop(0, count, run, 0, unroll=unroll)


def part(i, size):
    return pl.ds(pl.multiple_of(i * size, size), size)


def copies(pairs, sem):
    return [pltpu.make_async_copy(a, b, sem.at[i]) for i, (a, b) in enumerate(pairs)]


def chosen_tick(first, plan):
    picked = jnp.where(first, plan[0] or 0, plan[1] or 0)
    active = jnp.where(first, int(plan[0] is not None), int(plan[1] is not None)) == 1
    return active, picked


def early_rows(rows):
    return 3 * rows // 4


def forward_kernel(slot, plan, stage, aliased, pieces, *refs):
    starts, ends = stage != SECOND, stage != FIRST
    spans, norms, vectors, feat, w_in, w_out, w_up, w_down = refs[:8]
    recv = refs[8 : 8 + pieces]
    refs = refs[8 + pieces :]
    kept = refs[:aliased]
    refs = refs[aliased:]
    z_out, squares_out = refs[:2]
    s_x, s_a, s_qkv, s_c, s_l, s_h, s_b, s_g, s_d, s_p, layers = refs[2:13]
    (v_in, v_out, v_up, v_down, v_x, v_a, v_qkv, v_c, v_l, v_h, v_b, v_g, v_d, v_p, v_bias, v_acc, v_z,
     sem_w, sem_x, sem_o, sem_p, sem_g, sem_d) = refs[13:]
    rows, width = v_x.shape
    hidden = v_up.shape[1]
    here = pl.ds(slot * rows, rows)
    first = lax.axis_index("section") == 0
    active, picked = chosen_tick(first, plan)

    def norm(k):
        return norms[:, k * width : (k + 1) * width]

    def bias(k):
        return vectors[:, k * width : (k + 1) * width]

    @pl.when(active)
    def _():
        length = spans[picked]
        causal = first

        loaded = pltpu.make_async_copy(feat.at[picked, 0], v_x, sem_x.at[0])
        if starts:
            pl.when(first)(loaded.start)

            @pl.when(jnp.logical_not(first))
            def _():
                at = 0
                for piece in recv:
                    pltpu.make_async_copy(
                        piece, v_x.at[pl.ds(at, piece.shape[0])], sem_x.at[0]
                    ).start()
                    at += piece.shape[0]

        def column(source, target, index, size):
            def at(i):
                return pltpu.make_async_copy(
                    source.at[:, part(i, size)], target.at[:, part(i, size)], sem_w.at[index + i]
                )

            return at

        def down_copy(i):
            return pltpu.make_async_copy(
                w_down.at[part(i, BROAD)], v_down.at[part(i, BROAD)], sem_w.at[3 + 1 + hidden // BROAD + i]
            )

        in_copy = column(w_in, v_in, 0, WIDE)
        out_copy = column(w_out, v_out, 3, WIDE)
        up_copy = column(w_up, v_up, 4, BROAD)
        if starts:
            for i in range(3):
                in_copy(i).start()

        outs = []

        def send(source, target, index):
            copy = pltpu.make_async_copy(source, target, sem_o.at[index])
            copy.start()
            outs.append(copy)

        valid = lambda i, n: (lax.broadcasted_iota(jnp.int32, (n, 1), 0) + i * n < length).astype(f32)

        def square(values, mask):
            return jnp.sum((values * values * mask).reshape(-1, 8, width), axis=0)

        nothing = jnp.zeros((8, width), f32)
        sums_one = (nothing, nothing)
        groups = width // GROUP

        def p_copy(i):
            return pltpu.make_async_copy(
                v_p.at[i % 2], s_p.at[slot, pl.ds(i * 4, 4)], sem_p.at[i % 2]
            )

        def start_feed():
            for i in range(hidden // BROAD):
                up_copy(i).start()
                down_copy(i).start()

        half = rows // 2
        low = early_rows(rows) if stage == SECOND else 0
        high = early_rows(rows) if stage == FIRST else rows
        these = slice(low, high)
        count = high - low
        there = pl.ds(slot * rows + low, count)
        if stage == SECOND:
            start_feed()
            entries = [
                pltpu.make_async_copy(kept[5].at[there], v_h.at[pl.ds(low, count)], sem_o.at[0]),
                pltpu.make_async_copy(kept[6].at[there], v_b.at[pl.ds(low, count)], sem_o.at[1]),
            ]
            for copy in entries:
                copy.start()
            for copy in entries:
                copy.wait()
            v_acc[these, :] = jnp.broadcast_to(bias(7), (count, width))
        if starts:
            def bias_rows(i):
                at = part(i, 128)
                query = lax.broadcasted_iota(jnp.int32, (128, rows), 0) + i * 128
                key = lax.broadcasted_iota(jnp.int32, (128, rows), 1)
                open_ = (key < length) & ((key <= query) | jnp.logical_not(causal))
                v_bias[at, :] = jnp.where(open_, 0.0, big_negative)

            loop(rows // 128, bias_rows)
            loaded.wait()

            def first_norm(i):
                at = part(i, 64)
                normed, _ = row_stats(v_x[at, :].astype(f32))
                v_a[at, :] = (normed * norm(0) + norm(1)).astype(bf16)

            loop(rows // 64, first_norm, 2)
            send(v_x, s_x.at[here], 0)
            send(v_a, s_a.at[here], 1)
            def project(i):
                in_copy(i).wait()
                at = part(i, WIDE)
                shift = vectors[:, pl.ds(pl.multiple_of((4 + i // 2) * width, width), width)]
                tile = nn(v_a[...], v_in[:, at]) + jnp.where(i == 1, 0.0, shift)
                v_qkv[:, at] = tile.astype(bf16)

            loop(3 * width // WIDE, project)
            out_copy(0).start()
            start_feed()
            send(v_qkv, s_qkv.at[here], 2)
            lane = lax.broadcasted_iota(jnp.int32, (1, GROUP), 1) // HEAD

            def attend(i):
                at = part(i, GROUP)
                query = v_qkv[:, at]
                key = v_qkv[:, pl.ds(pl.multiple_of(width + i * GROUP, GROUP), GROUP)]
                value = v_qkv[:, pl.ds(pl.multiple_of(2 * width + i * GROUP, GROUP), GROUP)]

                @pl.when(i >= 2)
                def _():
                    p_copy(i - 2).wait()

                half = rows // 2

                def rows_part(r, keys):
                    picked_rows = slice(r * half, (r + 1) * half)
                    scaled = query[picked_rows] * score_scale
                    total = jnp.zeros((half, GROUP), f32)
                    sums = jnp.ones((half, GROUP), f32)
                    for h in range(4):
                        masked = jnp.where(lane == h, scaled, 0).astype(bf16)
                        scores = nt(masked, key[:keys]) + v_bias[picked_rows, :keys]
                        top = jnp.max(scores, axis=-1, keepdims=True)
                        raised = jnp.exp(scores - top).astype(bf16)
                        v_p[i % 2, h, picked_rows, :keys] = raised
                        if keys < rows:
                            v_p[i % 2, h, picked_rows, keys:] = jnp.zeros((half, rows - keys), bf16)
                        product = nn(raised, jnp.where(lane == h, value[:keys], 1).astype(bf16))
                        total = jnp.where(lane == h, product, total)
                        sums = jnp.where(lane == (h ^ 1), product, sums)
                    inverse = 1.0 / jnp.concatenate(
                        [pltpu.roll(sums[:, k : k + 128], HEAD, 1) for k in (0, 128)], axis=1
                    )
                    v_l[picked_rows, at] = inverse
                    v_c[picked_rows, at] = (total * inverse).astype(bf16)

                @pl.when(causal)
                def _():
                    rows_part(0, half)
                    rows_part(1, rows)

                @pl.when(jnp.logical_not(causal))
                def _():
                    rows_part(0, rows)
                    rows_part(1, rows)

                p_copy(i).start()

            loop(groups, attend)
            send(v_c, s_c.at[here], 8)
            send(v_l, s_l.at[here], 9)
            out_copy(0).wait()
            def mix(i):
                at = part(i, WIDE)
                v_acc[:, at] = nn(v_c[...], v_out[:, at]) + bias(6)

            loop(width // WIDE, mix)

            def second_norm(i, carry):
                at = part(i, 64)
                branch = v_acc[at, :]
                middle = v_x[at, :].astype(f32) + branch
                v_h[at, :] = middle
                normed, _ = row_stats(middle)
                v_b[at, :] = (normed * norm(2) + norm(3)).astype(bf16)
                v_acc[at, :] = jnp.broadcast_to(bias(7), (64, width))
                mask = valid(i, 64)
                return (carry[0] + square(middle, mask), carry[1] + square(branch, mask))

            sums_one = lax.fori_loop(0, rows // 64, second_norm, sums_one, unroll=2)
            send(v_h, s_h.at[here], 3)
            send(v_b, s_b.at[here], 4)

        def feed(i):
            up_copy(i).wait()
            down_copy(i).wait()
            at = part(i, BROAD)
            shift = vectors[:, pl.ds(pl.multiple_of(8 * width + i * BROAD, BROAD), BROAD)]
            act, slope = gate(nn(v_b[these, :], v_up[:, at]) + shift)
            act = act.astype(bf16)
            v_g[these, at] = act
            v_d[these, at] = slope.astype(bf16)
            v_acc[these, :] += nn(act, v_down[at, :])
            g_copy(i).start()
            d_copy(i).start()

        def g_copy(i):
            at = part(i, BROAD)
            return pltpu.make_async_copy(v_g.at[pl.ds(low, count), at], s_g.at[there, at], sem_g.at[i])

        def d_copy(i):
            at = part(i, BROAD)
            return pltpu.make_async_copy(v_d.at[pl.ds(low, count), at], s_d.at[there, at], sem_d.at[i])

        loop(hidden // BROAD, feed)

        def finish(i, carry):
            at = part(i, 64)
            branch = v_acc[at, :]
            output = v_h[at, :] + branch
            v_z[at, :] = output.astype(bf16)
            mask = valid(i, 64)
            return (carry[0] + square(output, mask), carry[1] + square(branch, mask))

        sums_two = lax.fori_loop(low // 64, high // 64, finish, (nothing, nothing), unroll=2)
        send(v_z.at[pl.ds(low, count)], z_out, 7)
        send(v_z.at[pl.ds(low, count)], layers.at[0, picked, 0, pl.ds(low, count)], 5)
        for k, value in enumerate((sums_one[0], sums_two[0], sums_one[1], sums_two[1])):
            squares_out[k] = value
        for copy in outs:
            copy.wait()
        for i in range(hidden // BROAD):
            g_copy(i).wait()
            d_copy(i).wait()
        if starts:
            p_copy(groups - 2).wait()
            p_copy(groups - 1).wait()

    @pl.when(jnp.logical_not(active))
    def _():
        squares_out[...] = jnp.zeros_like(squares_out)


def stash_shapes(rows, width, hidden):
    heads = width // HEAD
    return [
        jax.ShapeDtypeStruct((2 * rows, width), bf16),
        jax.ShapeDtypeStruct((2 * rows, width), bf16),
        jax.ShapeDtypeStruct((2 * rows, 3 * width), bf16),
        jax.ShapeDtypeStruct((2 * rows, width), bf16),
        jax.ShapeDtypeStruct((2 * rows, width), f32),
        jax.ShapeDtypeStruct((2 * rows, width), f32),
        jax.ShapeDtypeStruct((2 * rows, width), bf16),
        jax.ShapeDtypeStruct((2 * rows, hidden), bf16),
        jax.ShapeDtypeStruct((2 * rows, hidden), bf16),
        jax.ShapeDtypeStruct((2, heads, rows, rows), bf16),
        jax.ShapeDtypeStruct((1, 2, 1, rows, width), bf16),
    ]


def forward_call(slot, plan, stage, spans, norms, vectors, feat, recv, weights, stash=()):
    rows, width = feat.shape[2:]
    count = {BOTH: rows, FIRST: early_rows(rows), SECOND: rows - early_rows(rows)}[stage]
    hidden = weights[2].shape[1]
    any_ = pl.BlockSpec(memory_space=pl.ANY)
    vm = pl.BlockSpec(memory_space=pltpu.VMEM)
    shapes = stash_shapes(rows, width, hidden)
    results = pl.pallas_call(
        functools.partial(forward_kernel, slot, plan, stage, len(stash), len(recv)),
        in_specs=[pl.BlockSpec(memory_space=pltpu.SMEM), vm, vm] + [any_] * (5 + len(recv) + len(stash)),
        out_specs=[any_, vm] + [any_] * len(shapes),
        out_shape=[jax.ShapeDtypeStruct((count, width), bf16), jax.ShapeDtypeStruct((4, 8, width), f32)] + shapes,
        input_output_aliases={8 + len(recv) + k: 2 + k for k in range(len(stash))},
        scratch_shapes=[
            pltpu.VMEM(w.shape, bf16) for w in weights
        ] + [
            pltpu.VMEM((rows, width), bf16),
            pltpu.VMEM((rows, width), bf16),
            pltpu.VMEM((rows, 3 * width), bf16),
            pltpu.VMEM((rows, width), bf16),
            pltpu.VMEM((rows, width), f32),
            pltpu.VMEM((rows, width), f32),
            pltpu.VMEM((rows, width), bf16),
            pltpu.VMEM((rows, hidden), bf16),
            pltpu.VMEM((rows, hidden), bf16),
            pltpu.VMEM((2, 4, rows, rows), bf16),
            pltpu.VMEM((rows, rows), f32),
            pltpu.VMEM((rows, width), f32),
            pltpu.VMEM((rows, width), bf16),
            pltpu.SemaphoreType.DMA((4 + 2 * hidden // WIDE,)),
            pltpu.SemaphoreType.DMA((1,)),
            pltpu.SemaphoreType.DMA((10,)),
            pltpu.SemaphoreType.DMA((2,)),
            pltpu.SemaphoreType.DMA((hidden // WIDE,)),
            pltpu.SemaphoreType.DMA((hidden // WIDE,)),
        ],
        compiler_params=pltpu.CompilerParams(vmem_limit_bytes=VMEM),
        cost_estimate=pl.CostEstimate(flops=LARGE, bytes_accessed=1, transcendentals=0),
        name="layer_forward",
    )(spans, norms, vectors, feat, *weights, *recv, *stash)
    return results[0], results[1], results[2:]


def backward_kernel(slot, plan, stage, aliased, given, *refs):
    feeds, attends = stage != SECOND, stage != FIRST
    spans, norms, cot, recv, w_in, w_out, w_up, w_down = refs[:8]
    s_x, s_qkv, s_c, s_l, s_h, s_d, s_p = refs[8:15]
    if stage == SECOND:
        mid_in, middle_in = refs[15:17]
    refs = refs[15 + given + aliased :]
    smalls = refs[0]
    refs = refs[1:]
    if feeds:
        g_up, g_mid = refs[:2]
        refs = refs[2:]
    if attends:
        dx_out, g_qkv, inputs = refs[:3]
        refs = refs[3:]
    if stage == BOTH:
        g_feed = refs[0]
        refs = refs[1:]
    if stage == FIRST:
        middle_out = refs[0]
        refs = refs[1:]
    (v_in, v_out, v_up, v_down, v_x, v_dy, v_qkv, v_c, v_l, v_h, v_d, v_p, v_du, v_do, v_dc, v_dqkv, v_acc,
     v_s, v_k, v_dx, sem_w, sem_x, sem_d, sem_p, sem_o) = refs
    rows, width = v_x.shape
    hidden = v_up.shape[1]
    here = pl.ds(slot * rows, rows)
    tiles = hidden // WIDE

    first = lax.axis_index("section") == 0
    active, picked = chosen_tick(first, plan)

    def norm(k):
        return norms[:, k * width : (k + 1) * width]

    @pl.when(active)
    def _():
        length = spans[picked]
        if stage != BOTH:
            smalls[...] = jnp.zeros_like(smalls)

        if feeds:

            @pl.when(jnp.logical_not(first))
            def _():
                pltpu.make_async_copy(cot.at[picked, 0], v_dy, sem_x.at[0]).start()

            @pl.when(first)
            def _():
                pltpu.make_async_copy(recv, v_dy, sem_x.at[0]).start()

        def down_copy(i):
            return pltpu.make_async_copy(
                w_down.at[part(i, WIDE)], v_down.at[part(i, WIDE)], sem_w.at[i]
            )

        def up_copy(i):
            at = part(i, WIDE)
            return pltpu.make_async_copy(w_up.at[:, at], v_up.at[:, at], sem_w.at[tiles + i])

        def d_copy(i):
            return pltpu.make_async_copy(
                s_d.at[here, part(i, WIDE)], v_d.at[i % 2], sem_d.at[i % 2]
            )

        def p_copy(i):
            return pltpu.make_async_copy(
                s_p.at[slot, pl.ds(i * 4, 4)], v_p.at[i % 2], sem_p.at[i % 2]
            )

        loads = copies(
            [
                (s_x.at[here], v_x),
                (s_qkv.at[here], v_qkv),
                (s_c.at[here], v_c),
                (s_l.at[here], v_l),
                (s_h.at[here], v_h),
                (w_out, v_out),
                (w_in, v_in),
            ],
            sem_x.at[pl.ds(1, 7)],
        )
        if feeds:
            d_copy(0).start()
            for i in range(tiles):
                down_copy(i).start()
                up_copy(i).start()
                if i == 0:
                    d_copy(1).start()
            loads[4].start()
        if stage == SECOND:
            entries = [
                pltpu.make_async_copy(mid_in.at[here], v_do, sem_o.at[0]),
                pltpu.make_async_copy(middle_in, v_acc, sem_o.at[3]),
            ]
            for copy in entries:
                copy.start()
        def enter_attention():
            for k in (5, 1, 2, 3):
                loads[k].start()
            p_copy(0).start()
            p_copy(1).start()

        def enter_last():
            loads[6].start()
            loads[0].start()

        if stage == SECOND:
            enter_attention()
            enter_last()
        nothing = jnp.zeros((8, width), f32)

        def fold(values):
            return jnp.sum(values.reshape(-1, 8, width), axis=0)

        def enter(i, total):
            at = part(i, 64)
            place = lax.broadcasted_iota(jnp.int32, (64, 1), 0) + i * 64
            masked = jnp.where(place < length, v_dy[at, :].astype(f32), 0.0)
            v_dy[at, :] = masked.astype(bf16)
            v_acc[at, :] = jnp.zeros((64, width), f32)
            return total + fold(masked)

        if feeds:
            pltpu.make_async_copy(recv, v_dy, sem_x.at[0]).wait()
            total = lax.fori_loop(0, rows // 64, enter, nothing, unroll=2)
            smalls[7:8, :] = jnp.sum(total, axis=0, keepdims=True)
        if stage == BOTH:
            feed_copy = pltpu.make_async_copy(v_dy, g_feed.at[here], sem_o.at[4])
            feed_copy.start()

        def feed(i):
            down_copy(i).wait()
            up_copy(i).wait()
            d_copy(i).wait()
            if stage == BOTH:
                pl.when(i == tiles - 3)(enter_attention)
                pl.when(i == tiles - 1)(enter_last)
            at = part(i, WIDE)
            pre = (nt(v_dy[...], v_down[at, :]) * v_d[i % 2].astype(f32)).astype(bf16)
            v_du[:, at] = pre
            v_acc[...] += nt(pre, v_up[:, at])
            smalls[pl.ds(8 + i, 1), :] = jnp.sum(v_du[:, at].astype(f32), axis=0, keepdims=True)
            pltpu.make_async_copy(v_du.at[:, at], g_up.at[here, at], sem_o.at[3]).start()

            @pl.when(i + 2 < tiles)
            def _():
                d_copy(i + 2).start()

        if feeds:
            loop(tiles, feed)
            loads[4].wait()

        def norm_back(source, grad, gain):
            normed, inverse = row_stats(source)
            scaled = grad * gain
            mean_one = jnp.mean(scaled, axis=-1, keepdims=True)
            mean_two = jnp.mean(scaled * normed, axis=-1, keepdims=True)
            return inverse * (scaled - mean_one - normed * mean_two), fold(grad * normed), fold(grad)

        def second_norm(i, carry):
            at = part(i, 64)
            rows_back, one, two = norm_back(v_h[at, :], v_acc[at, :], norm(2))
            middle = rows_back + v_dy[at, :].astype(f32)
            v_acc[at, :] = middle
            low = middle.astype(bf16)
            v_do[at, :] = low
            return carry[0] + one, carry[1] + two, carry[2] + fold(low.astype(f32))

        if feeds:
            sums = lax.fori_loop(0, rows // 64, second_norm, (nothing,) * 3, unroll=2)
            for k, value in zip((2, 3, 6), sums):
                smalls[k : k + 1, :] = jnp.sum(value, axis=0, keepdims=True)
            outs = [pltpu.make_async_copy(v_do, g_mid.at[here], sem_o.at[0])]
            if stage == FIRST:
                outs.append(pltpu.make_async_copy(v_acc, middle_out, sem_o.at[1]))
            for copy in outs:
                copy.start()
        if stage == SECOND:
            for copy in entries:
                copy.wait()
        if attends:
            loads[5].wait()
            v_dc[...] = nt(v_do[...], v_out[...]).astype(bf16)
            for k in (1, 2, 3):
                loads[k].wait()
        lane = lax.broadcasted_iota(jnp.int32, (1, GROUP), 1) // HEAD

        def attend(i):
            p_copy(i).wait()
            at = part(i, GROUP)
            key_at = pl.ds(pl.multiple_of(width + i * GROUP, GROUP), GROUP)
            value_at = pl.ds(pl.multiple_of(2 * width + i * GROUP, GROUP), GROUP)
            key = v_qkv[:, key_at]
            value = v_qkv[:, value_at]
            query = v_qkv[:, at]
            wide = v_dc[:, at].astype(f32) * v_l[:, at]
            low = wide.astype(bf16)
            dots = wide * v_c[:, at].astype(f32)
            for h in range(4):
                hs = slice(h * rows, (h + 1) * rows)
                v_k[hs, :] = jnp.where(lane == h, key, 0).astype(bf16)
                masked = jnp.where(lane == h, low, 0).astype(bf16)
                delta = jnp.sum(jnp.where(lane == h, dots, 0.0), axis=-1, keepdims=True)
                inner = nt(masked, value) - delta
                v_s[:, hs] = v_p[i % 2, h] * inner.astype(bf16)
            grad_query = (nn(v_s[...], v_k[...]) * score_scale).astype(bf16)
            query_t = query.T
            low_t = low.T
            keys, values = [], []
            for h in range(4):
                hs = slice(h * HEAD, (h + 1) * HEAD)
                keys.append(nn(query_t[hs], v_s[:, h * rows : (h + 1) * rows]))
                values.append(nn(low_t[hs], v_p[i % 2, h]))
            grad_key = (jnp.concatenate(keys, axis=0) * score_scale).astype(bf16).T
            grad_value = jnp.concatenate(values, axis=0).astype(bf16).T
            v_dqkv[:, at] = grad_query
            v_dqkv[:, key_at] = grad_key
            v_dqkv[:, value_at] = grad_value
            smalls[4:5, at] = jnp.sum(grad_query.astype(f32), axis=0, keepdims=True)
            smalls[5:6, at] = jnp.sum(grad_value.astype(f32), axis=0, keepdims=True)

            @pl.when(i + 2 < width // GROUP)
            def _():
                p_copy(i + 2).start()

        if attends:
            loop(width // GROUP, attend)
            qkv_copy = pltpu.make_async_copy(v_dqkv, g_qkv.at[here], sem_o.at[1])
            qkv_copy.start()
            loads[6].wait()
            loads[0].wait()

            v_h[...] = nt(v_dqkv[...], v_in[...])

        def first_norm(i, carry):
            at = part(i, 64)
            rows_back, one, two = norm_back(v_x[at, :].astype(f32), v_h[at, :], norm(0))
            v_dx[at, :] = (rows_back + v_acc[at, :]).astype(bf16)
            return carry[0] + one, carry[1] + two

        if attends:
            sums = lax.fori_loop(0, rows // 64, first_norm, (nothing,) * 2, unroll=2)
            for k, value in enumerate(sums):
                smalls[k : k + 1, :] = jnp.sum(value, axis=0, keepdims=True)
            dx_copy = pltpu.make_async_copy(v_dx, dx_out, sem_o.at[2])
            dx_copy.start()
            input_copy = pltpu.make_async_copy(v_dx, inputs.at[0, picked, 0], sem_o.at[5])
            input_copy.start()
            for copy in (qkv_copy, dx_copy, input_copy):
                copy.wait()
        if stage == BOTH:
            feed_copy.wait()
        if feeds:
            for copy in outs:
                copy.wait()
            pltpu.make_async_copy(v_du, g_up.at[here], sem_o.at[3]).wait()

    @pl.when(jnp.logical_not(active))
    def _():
        smalls[...] = jnp.zeros_like(smalls)


def backward_call(slot, plan, stage, spans, norms, cot, recv, weights, stash, given, grads):
    rows, width = recv.shape
    hidden = weights[2].shape[1]
    any_ = pl.BlockSpec(memory_space=pl.ANY)
    vm = pl.BlockSpec(memory_space=pltpu.VMEM)
    shape = jax.ShapeDtypeStruct
    outs = {"smalls": shape((8 + hidden // WIDE, width), f32)}
    if stage != SECOND:
        outs["up"] = shape((2 * rows, hidden), bf16)
        outs["mid"] = shape((2 * rows, width), bf16)
    if stage != FIRST:
        outs["dx"] = shape((rows, width), bf16)
        outs["qkv"] = shape((2 * rows, 3 * width), bf16)
        outs["inputs"] = shape((1, 2, 1, rows, width), bf16)
    if stage == BOTH:
        outs["feed"] = shape((2 * rows, width), bf16)
    if stage == FIRST:
        outs["middle"] = shape((rows, width), f32)
    names = list(outs)
    kept = [name for name in names if name in grads and name not in ("smalls", "dx")]
    s_x, s_a, s_qkv, s_c, s_l, s_h, s_b, s_g, s_d, s_p, _ = stash
    results = pl.pallas_call(
        functools.partial(backward_kernel, slot, plan, stage, len(kept), len(given)),
        in_specs=[pl.BlockSpec(memory_space=pltpu.SMEM), vm] + [any_] * (13 + len(given) + len(kept)),
        out_specs=[vm] + [any_] * (len(names) - 1),
        out_shape=list(outs.values()),
        input_output_aliases={15 + len(given) + k: names.index(n) for k, n in enumerate(kept)},
        scratch_shapes=[pltpu.VMEM(w.shape, bf16) for w in weights] + [
            pltpu.VMEM((rows, width), bf16),
            pltpu.VMEM((rows, width), bf16),
            pltpu.VMEM((rows, 3 * width), bf16),
            pltpu.VMEM((rows, width), bf16),
            pltpu.VMEM((rows, width), f32),
            pltpu.VMEM((rows, width), f32),
            pltpu.VMEM((2, rows, WIDE), bf16),
            pltpu.VMEM((2, 4, rows, rows), bf16),
            pltpu.VMEM((rows, hidden), bf16),
            pltpu.VMEM((rows, width), bf16),
            pltpu.VMEM((rows, width), bf16),
            pltpu.VMEM((rows, 3 * width), bf16),
            pltpu.VMEM((rows, width), f32),
            pltpu.VMEM((rows, 4 * rows), bf16),
            pltpu.VMEM((4 * rows, GROUP), bf16),
            pltpu.VMEM((rows, width), bf16),
            pltpu.SemaphoreType.DMA((2 * hidden // WIDE,)),
            pltpu.SemaphoreType.DMA((8,)),
            pltpu.SemaphoreType.DMA((2,)),
            pltpu.SemaphoreType.DMA((2,)),
            pltpu.SemaphoreType.DMA((6,)),
        ],
        compiler_params=pltpu.CompilerParams(vmem_limit_bytes=VMEM),
        cost_estimate=pl.CostEstimate(flops=LARGE, bytes_accessed=1, transcendentals=0),
        name="layer_backward",
    )(
        spans, norms, cot, recv, *weights, s_x, s_qkv, s_c, s_l, s_h, s_d, s_p, *given,
        *[grads[name] for name in kept],
    )
    return {**grads, **dict(zip(names, results))}


def turn_kernel(blocks, *refs):
    count = len(blocks)
    for k, block in enumerate(blocks):
        source, target = refs[k], refs[count + k]

        @pl.when((pl.program_id(0) == k) if k + 1 < count else (pl.program_id(0) >= k))
        def _(source=source, target=target, block=block):
            flat = source[...].T
            pairs = flat.shape[0] // (2 * block)
            for core in range(2):

                @pl.when(lax.axis_index("dp") % 2 == core)
                def _(core=core):
                    for j in range(pairs):
                        at = slice(j * block, (j + 1) * block)
                        other = (2 * j + 1 - core) * block
                        own = (2 * j + core) * block
                        target[0, at, :] = flat[other : other + block]
                        target[1, at, :] = flat[own : own + block]


def turn_call(sources):
    rows = sources[0].shape[0]
    count = len(sources)
    size = lax.axis_size("dp")
    steps = count - 1 + sources[-1].shape[1] // WIDE

    def last(i):
        return jnp.maximum(i - (count - 1), 0)

    ins = [pl.BlockSpec((rows, WIDE), lambda i: (0, 0))] * (count - 1)
    ins.append(pl.BlockSpec((rows, WIDE), lambda i: (0, last(i))))
    outs = [pl.BlockSpec((2, WIDE // 2, rows), lambda i: (0, 0, 0))] * (count - 1)
    outs.append(pl.BlockSpec((2, WIDE // 2, rows), lambda i: (0, last(i), 0)))
    return pl.pallas_call(
        functools.partial(turn_kernel, [s.shape[1] // size for s in sources]),
        grid=(steps,),
        in_specs=ins,
        out_specs=outs,
        out_shape=[jax.ShapeDtypeStruct((2, s.shape[1] // 2, rows), bf16) for s in sources],
        compiler_params=pltpu.CompilerParams(vmem_limit_bytes=VMEM),
        cost_estimate=pl.CostEstimate(flops=1, bytes_accessed=1, transcendentals=0),
        name="turn",
    )(*sources)


def weight_kernel(widths, half, left, right, *rest):
    if len(rest) > len(widths):
        late, *outs, joined = rest
        rows = late.shape[0]

        @pl.when(pl.program_id(0) == 0)
        def _():
            joined[:rows, :] = right[:rows, :]
            joined[rows:, :] = jnp.where(
                lax.axis_index("section") == 0, late[...], right[rows:, :]
            )

        right = joined
    else:
        outs = rest
    total = nn(left[0], right[...]).astype(bf16)
    at = 0
    for width, out in zip(widths, outs):
        step, offset = divmod(at, right.shape[1])
        if len(widths) == 1:
            out[...] = total
        else:

            @pl.when(pl.program_id(1) == step)
            def _(out=out, cut=slice(offset, offset + width)):
                out[...] = total[:, cut]

        at += width


def weight_call(left, right, start, widths, half, late=None):
    _, height, rows = left.shape
    columns = sum(widths)
    tall = min(height, WIDE)
    wide = min(columns, WIDE)
    specs = [
        pl.BlockSpec((1, tall, rows), lambda i, j: (half, i, 0)),
        pl.BlockSpec((rows, wide), lambda i, j: (0, start // wide + j)),
    ]
    operands = (left, right)
    if late is not None:
        specs.append(pl.BlockSpec((rows // 2, wide), lambda i, j: (0, j)))
        operands += (late,)

    def out(width):
        if width > wide:
            return pl.BlockSpec((tall, wide), lambda i, j: (i, j))
        return pl.BlockSpec((tall, width), lambda i, j: (i, 0))

    return pl.pallas_call(
        functools.partial(weight_kernel, widths, half),
        grid=(height // tall, columns // wide),
        in_specs=specs,
        out_specs=[out(width) for width in widths],
        out_shape=[jax.ShapeDtypeStruct((height, width), bf16) for width in widths],
        scratch_shapes=[] if late is None else [pltpu.VMEM((rows, columns), bf16)],
        compiler_params=pltpu.CompilerParams(vmem_limit_bytes=VMEM),
        cost_estimate=pl.CostEstimate(flops=1, bytes_accessed=1, transcendentals=0),
        name="weight_product",
    )(*operands)


def sum_kernel(layout, lefts, fixed, free, place, *refs):
    count = sum(len(arrays) for arrays in layout)
    sources = iter(refs[:count])
    terms = [[next(sources) for _ in arrays] for arrays in layout]
    out, held, total, sem, out_sem = refs[-5:]
    me = lax.axis_index("dp")
    cells = list(itertools.product(range(2), repeat=len(free)))
    loads, slot = [], 0
    for cell in cells:
        loads.append([])
        for arrays, left, widths in zip(terms, lefts, layout):
            index = []
            for bit in left:
                if bit in free:
                    index.append(cell[free.index(bit)])
                else:
                    own = (me >> bit) & 1
                    index.append(own if fixed[bit] else 1 - own)
            at = 0
            for ref, (start, width) in zip(arrays, widths):
                copy = pltpu.make_async_copy(
                    ref.at[(*index, slice(None), pl.ds(start, width))],
                    held.at[slot, :, pl.ds(at, width)],
                    sem.at[len(loads[-1]), len(loads) - 1],
                )
                copy.start()
                loads[-1].append(copy)
                at += width
            slot += 1
    stores = []
    for k, cell in enumerate(cells):
        for copy in loads[k]:
            copy.wait()
        value = added([held[k * len(terms) + j] for j in range(len(terms))])
        total[k] = value.astype(total.dtype)
        stores.append(pltpu.make_async_copy(total.at[k], place(out, cell), out_sem.at[k]))
        stores[-1].start()
    for copy in stores:
        copy.wait()


def sum_call(terms, fixed, kind, into=None, start=0):
    rows = terms[0][0][0][0].shape[-2]
    layout = [[(at, width) for _, at, width in arrays] for arrays, _ in terms]
    lefts = [left for _, left in terms]
    columns = sum(width for _, width in layout[0])
    free = [bit for bit in lefts[0] if bit not in fixed]
    operands = [array for arrays, _ in terms for array, _, _ in arrays]
    cells = 2 ** len(free)
    aliases = {}
    wide = 0
    if into is None:
        shape = jax.ShapeDtypeStruct((2,) * len(free) + (rows, columns), kind)
    else:
        wide, into = into
        shape = jax.ShapeDtypeStruct((1, rows, wide), kind)
        if into is not None:
            aliases = {len(operands): 0}
            operands.append(into)

    given = len(operands)

    def place(out, cell):
        if wide:
            return out.at[0, :, pl.ds(start, columns)]
        return out.at[cell] if cell else out

    def kernel(*refs):
        refs = refs[: given - len(aliases)] + refs[given:]
        sum_kernel(layout, lefts, fixed, free, place, *refs)

    any_ = pl.BlockSpec(memory_space=pl.ANY)
    return pl.pallas_call(
        kernel,
        in_specs=[any_] * len(operands),
        out_specs=any_,
        out_shape=shape,
        input_output_aliases=aliases,
        scratch_shapes=[
            pltpu.VMEM((cells * len(terms), rows, columns), terms[0][0][0][0].dtype),
            pltpu.VMEM((cells, rows, columns), kind),
            pltpu.SemaphoreType.DMA((max(sum(len(arrays) for arrays, _ in terms), 1), cells)),
            pltpu.SemaphoreType.DMA((cells,)),
        ],
        compiler_params=pltpu.CompilerParams(
            vmem_limit_bytes=VMEM if len(free) > 1 or rows > columns // 8 else LESS
        ),
        cost_estimate=pl.CostEstimate(flops=SMALL, bytes_accessed=1, transcendentals=0),
        name="sum_terms",
    )(*operands)


highest = lax.Precision.HIGHEST


def added(terms):
    total = terms[0].astype(f32)
    for term in terms[1:]:
        total = total + term.astype(f32)
    return total


class Line:
    def __init__(self):
        self.last = None

    def after(self, values):
        if self.last is not None:
            values = lax.optimization_barrier(tuple(values) + (self.last,))[:-1]
        return list(values)

    def done(self, value):
        self.last = value


class Exchange:
    def __init__(self, line, terms, left, order):
        self.line = line
        self.terms = [(arrays, sorted(left, reverse=True)) for arrays in terms]
        self.fixed = {}
        self.order = list(order)
        self.kind = terms[0][0][0].dtype

    def total(self, fixed, kind, **where):
        values = iter(self.line.after([array for arrays, _ in self.terms for array, _, _ in arrays]))
        self.terms = [
            ([(next(values), at, width) for _, at, width in arrays], left)
            for arrays, left in self.terms
        ]
        total = sum_call(self.terms, fixed, kind, **where)
        self.line.done(total)
        return total

    def step(self):
        bit = self.order.pop(0)
        theirs = self.total({**self.fixed, bit: False}, self.kind)
        self.fixed[bit] = True
        left = [k for k in self.terms[0][1] if k not in self.fixed]
        self.terms.append((whole(crossed(theirs, bit)), left))

    def cut(self, widths):
        parts = []
        low = 0
        for width in widths:
            high = low + width
            terms = []
            for arrays, left in self.terms:
                chosen, at = [], 0
                for array, start, columns in arrays:
                    a, b = max(low, at), min(high, at + columns)
                    if a < b:
                        chosen.append((array, start + a - at, b - a))
                    at += columns
                terms.append((chosen, left))
            part_ = Exchange(self.line, [terms[0][0]], (), self.order)
            part_.terms = terms
            part_.fixed = dict(self.fixed)
            parts.append(part_)
            low = high
        return parts

    def finish(self, **where):
        while self.order:
            self.step()
        return self.total(self.fixed, f32, **where)


def crossed(value, bit):
    return lax.ppermute(value, "dp", [(i, i ^ (1 << bit)) for i in range(lax.axis_size("dp"))])


def whole(array):
    return [(array, 0, array.shape[-1])]


def whole(array):
    return [(array, 0, array.shape[-1])]


class WeightSum(Exchange):
    def __init__(self, line, left, right, start, widths, order, late=None):
        size = lax.axis_size("dp")
        bits = size.bit_length() - 1
        shape = [2] * (bits - 1) + [2 * left.shape[1] // size, -1]
        left, right = line.after((left, right))
        theirs = weight_call(left, right, start, widths, 0, late)
        line.done(theirs[-1])
        received = [whole(crossed(array, 0).reshape(shape)) for array in theirs]
        self.product = (left, right, start, [sum(widths)], 1, late)
        self.shape = shape
        super().__init__(line, (sum(received, []),), range(1, bits), order)

    def own(self):
        left, right = self.line.after(self.product[:2])
        (mine,) = weight_call(left, right, *self.product[2:])
        self.line.done(mine)
        self.terms.append((whole(mine.reshape(self.shape)), self.terms[0][1]))
        return self


def shards(
    features,
    cotangent,
    lengths,
    codebook_index,
    attention_in,
    attention_out,
    feed_up,
    feed_down,
    vectors,
    adaptive_weight,
    codebook_table,
):
    is_first = lax.axis_index("section") == 0
    adaptive = jnp.where(is_first, 0.0, 1.0)
    rows, width = features.shape[2:]
    hidden = feed_up.shape[2]
    size = lax.axis_size("dp")
    bits = size.bit_length() - 1
    weights = (attention_in[0], attention_out[0], feed_up[0], feed_down[0])

    def send(value, to):
        return lax.ppermute(value, "section", [(1 - to, to)])

    spans = lengths[:, 0]

    def forward(slot, plan, norms, recv, stash=(), stage=BOTH):
        return forward_call(
            slot, plan, stage, spans, norms, vectors, features, recv, weights, stash
        )

    def backward(slot, plan, stage, norms, recv, stash, grads, given=()):
        return backward_call(
            slot, plan, stage, spans, norms, cotangent, recv, weights, stash, given, grads
        )

    z_one, squares_one, stash = forward(0, (0, None), vectors, ())
    received_one = (send(z_one, 1),)
    table, z_one = lax.optimization_barrier((codebook_table, z_one))
    condition_table = jnp.dot(table, adaptive_weight, preferred_element_type=f32)
    one_hot = (
        codebook_index[:, 0][:, None]
        == jnp.arange(codebook_table.shape[0], dtype=jnp.int32)[None, :]
    ).astype(f32)
    norms = vectors[:, : 4 * width] + adaptive * jnp.dot(
        one_hot, condition_table, precision=highest
    )
    norms_one, norms_two = norms[:1], norms[1:]
    z_two, squares_two, stash = forward(1, (1, 0), norms_one, received_one, stash)
    received_two = send(z_two, 1)
    grads = backward(1, (None, 0), BOTH, norms_one, z_two, stash, {})
    smalls_one = grads["smalls"]
    back_one = send(grads["dx"], 0)
    z_three, squares_three, stash = forward(0, (None, 1), norms_two, (received_two,), stash)
    grads = backward(0, (0, 1), BOTH, norms_two, back_one, stash, grads)
    smalls_two = grads["smalls"]
    back_two = send(grads["dx"], 0)

    s_x, s_a, s_qkv, s_c, s_l, s_h, s_b, s_g, s_d, s_p, layer_outputs = stash
    side_first = list(range(1, bits))
    line_first = side_first[1:] + side_first[:1]
    line = Line()
    line.done(smalls_two)
    squares = jnp.sum(squares_one + squares_two + squares_three, axis=(1, 2))
    counted = jnp.sum(lengths).astype(f32)
    (totals,) = line.after((jnp.concatenate([squares, counted[None], jnp.zeros((123,), f32)]),))
    for bit in range(bits):
        totals = totals + crossed(totals, bit)
    t_a, t_b, t_c, t_g = turn_call(line.after((s_a, s_b, s_c, s_g)))
    line.done(t_a)
    (totals,) = line.after((totals,))
    line.done(totals)
    down = WeightSum(line, t_g, grads["feed"], 0, [width], side_first, back_two).own()
    down.step()
    (back_two,) = line.after((back_two,))
    grads = backward(1, (1, None), FIRST, vectors, back_two, stash, grads)
    smalls_three = grads["smalls"]
    line.done(smalls_three)
    up = WeightSum(line, t_b, grads["up"], 0, [WIDE] * (hidden // WIDE), side_first).own()
    up.step()
    down.step()
    out = WeightSum(line, t_c, grads["mid"], 0, [width], side_first).own()
    (middle,) = line.after((grads["middle"],))
    grads = backward(
        1, (1, None), SECOND, vectors, back_two, stash, grads, (grads["mid"], middle)
    )
    smalls_four = grads["smalls"]
    line.done(smalls_four)
    g_qkv, input_grads = grads["qkv"], grads["inputs"]
    down.step()
    into_one = WeightSum(line, t_a, g_qkv, 0, [width] * 3, side_first).own()

    smalls = smalls_one + smalls_two + smalls_three + smalls_four
    table_grad = one_hot[0][:, None] * smalls_one[:4].reshape(1, -1) + one_hot[1][:, None] * (
        smalls_two[:4].reshape(1, -1) * adaptive
    )
    codes = table_grad.shape[0]
    share = table_grad.shape[1] // (2 * size)
    table_blocks = table_grad.reshape(codes, 2, size, share).transpose(2, 1, 0, 3)
    packed = jnp.concatenate([smalls.reshape(size, -1), table_blocks.reshape(size, -1)], axis=1)
    count = packed.shape[1]
    block = width // size
    packed = jnp.pad(packed.reshape(size, block, -1), ((0, 0), (0, 0), (0, 128 - count // block)))
    packed = packed.astype(bf16).reshape([2] * bits + [block, 128])
    core = lax.axis_index("dp") & 1
    (other, own) = [
        lax.dynamic_index_in_dim(packed, which, bits - 1, keepdims=False)
        for which in (1 - core, core)
    ]
    other = crossed(other, 0)
    into_one, into_two = into_one.cut([2 * width, width])
    up_one, up_two = up.cut([hidden // 2] * 2)
    into_two.terms = [
        (arrays + whole(extra), left)
        for (arrays, left), extra in zip(into_two.terms, (other, own))
    ]
    into_one.step()
    up_one.step()
    up_two.step()
    into_two.step()
    out.step()
    down = down.finish(into=(width, None))
    up_one.step()
    into_one.step()
    up_two.step()
    into_two.step()
    up = up_one.finish(into=(hidden, None))
    into_one.step()
    out.step()
    up = up_two.finish(into=(hidden, up), start=hidden // 2)
    into_two.step()
    into = into_one.finish(into=(3 * width, None))
    out.step()
    last = into_two.finish()
    out = out.finish(into=(width, None))
    into = lax.dynamic_update_slice(into, last[None, :, :width], (0, 0, 2 * width))
    small_sum = last[:, width : width + count // block].reshape(-1)
    vector_share = small_sum[: smalls.size // size]
    table_share = small_sum[smalls.size // size :].reshape(2, codes, share)
    table_own = jnp.where(is_first, send(table_share[0], 0), table_share[1])
    grad_adaptive = lax.dot_general(
        codebook_table.astype(f32),
        table_own,
        (((0,), (0,)), ((), ())),
        precision=highest,
        preferred_element_type=f32,
    )
    residual_rms = jnp.sqrt(totals[:4] / (totals[4] * width))[None]

    return (
        layer_outputs,
        input_grads,
        into,
        out,
        up,
        down,
        vector_share[None],
        grad_adaptive,
        residual_rms,
    )


def solution(mesh):
    placed = (
        P(None, "dp", None, None),
        P(None, "dp", None, None),
        P(None, "dp"),
        P(None, "dp"),
        P("section", None, None),
        P("section", None, None),
        P("section", None, None),
        P("section", None, None),
        P("section", None),
        P(),
        P(),
    )
    return jax.shard_map(
        shards,
        mesh=mesh,
        in_specs=placed,
        out_specs=(
            P("section", None, "dp", None, None),
            P("section", None, "dp", None, None),
            P("section", "dp", None),
            P("section", "dp", None),
            P("section", "dp", None),
            P("section", "dp", None),
            P("section", "dp"),
            P(None, ("section", "dp")),
            P("section", None),
        ),
        check_vma=False,
    )
```
